32 devices in a mesh: row: 4 (over y, core), col: 8 (over z, x).
Axes of the slice: x: 2, y: 2, z: 4, core: 2. Of those that a mesh axis runs over, the one named last changes fastest.
Arguments:
- hidden_in: bfloat16 [10880, 1024], P(('row', 'col')), may hold values from -6 to 6
- cond: bfloat16 [16, 1024], P('row'), may hold values from -6 to 6
- scale_sizes: int32 [16, 10], P('row'), may hold values from 1 to 256, 680 in all within a row
- w_ada: bfloat16 [2, 1024, 6, 1024], P(None, 'row', None, 'col'), may hold values from -0.09375 to 0.09375
- b_ada: bfloat16 [2, 6, 1024], P(None, None, 'col'), may hold values from -1 to 1
- w_qkv: bfloat16 [2, 1024, 3, 1024], P(None, 'row', None, 'col'), may hold values from -0.1875 to 0.1875
- b_qkv: bfloat16 [2, 2, 1024], P(None, None, 'col'), may hold values from -3 to 3
- head_scale: bfloat16 [2, 16], P(None, 'col'), may hold values from 6 to 16
- w_proj: bfloat16 [2, 1024, 1024], P(None, 'col', 'row'), may hold values from -0.75 to 0.75
- b_proj: bfloat16 [2, 1024], P(None, 'col'), may hold values from -3 to 3
- w_fc1: bfloat16 [2, 1024, 4096], P(None, 'row', 'col'), may hold values from -0.1875 to 0.1875
- b_fc1: bfloat16 [2, 4096], P(None, 'col'), may hold values from -3 to 3
- w_fc2: bfloat16 [2, 4096, 1024], P(None, 'col', 'row'), may hold values from -0.09375 to 0.09375
- b_fc2: bfloat16 [2, 1024], P(None, 'col'), may hold values from -3 to 3
- grad_out: bfloat16 [10880, 1024], P(('row', 'col')), may hold values from -6 to 6
Outputs:
- mixed: bfloat16 [10880, 1024], P(('row', 'col'))
- grad_in: float32 [10880, 1024], P(('row', 'col'))
- grad_w_ada: float32 [2, 1024, 6, 1024], P(None, 'row', None, 'col')
- grad_b_ada: float32 [2, 6, 1024], P(None, None, 'col')
- grad_w_qkv: float32 [2, 1024, 3, 1024], P(None, 'row', None, 'col')
- grad_b_qkv: float32 [2, 2, 1024], P(None, None, 'col')
- grad_head_scale: float32 [2, 16], P(None, 'col')
- grad_w_proj: float32 [2, 1024, 1024], P(None, 'col', 'row')
- grad_b_proj: float32 [2, 1024], P(None, 'col')
- grad_w_fc1: float32 [2, 1024, 4096], P(None, 'row', 'col')
- grad_b_fc1: float32 [2, 4096], P(None, 'col')
- grad_w_fc2: float32 [2, 4096, 1024], P(None, 'col', 'row')
- grad_b_fc2: float32 [2, 1024], P(None, 'col')
The draws below stay inside these ranges and needn't reach their ends.
Inputs may be any that keep to these rules, and one draw needn't show every extreme that they name: `scale_sizes`: each row holds the token counts of the 10 scales of one sequence in order, summing to 680.
All inputs are finite; a program needn't handle non-finite values.
Results may differ from the reference program's by a relative error of at most 0.025.
Values may be sent and summed in bfloat16 or wider, within the bound.
No kernel may reach another device: no remote copies, remote signals or barrier semaphores. Data moves between devices by JAX's collectives and lax.ppermute only.
A program may use at most 256 MiB of HBM per device.

```python
import math
import jax
import jax.numpy as jnp
import numpy as np
from jax import lax

D = 1024
HEADS = 16
FF = 4096
LAYERS = 2
SEQ_LEN = 680
SCALES = 10
MOST = 256
SEQS = 16
TOKENS = 10880


def levels(rng, dims, cuts, low, high):
    def one(dim, blocks):
        draws = jax.random.uniform(jax.random.fold_in(jax.random.fold_in(rng, 6), dim), (blocks,), jnp.float32, low / len(cuts), high / len(cuts))
        return jnp.repeat(jnp.exp(draws), dims[dim] // blocks).reshape((-1,) + (1,) * (len(dims) - dim - 1))

    loudness = one(*cuts[0])
    for cut in cuts[1:]:
        loudness = loudness * one(*cut)
    return loudness


def length_profile(number_of, total, limit, lean):
    weights = [(1 << 20) // math.isqrt(standing ** lean) + 1 for standing in range(2, number_of + 1)]
    spare, given = total - limit - (number_of - 1), [1] * (number_of - 1)
    while spare > 0:
        candidates = [i for i in range(number_of - 1) if given[i] < limit]
        pool, remaining = sum([weights[i] for i in candidates]), spare
        for i in candidates:
            extra = min(limit - given[i], max(1, remaining * weights[i] // pool), spare)
            given[i] = given[i] + extra
            spare = spare - extra
    return np.array([limit] + given)


def uneven(stream_key, amount, total, bound, slope):
    if amount == 2:
        one = jax.random.randint(stream_key, (), max(1, total - bound), min(bound, total - 1) + 1)
        return jnp.stack([one, total - one])
    lengths = jnp.asarray(length_profile(amount, total, bound, slope), jnp.int32)
    twos = (amount - 1) // 2
    donor, taker = lengths[1:1 + 2 * twos:2], lengths[2:2 + 2 * twos:2]
    margin = jnp.minimum(donor - 1, bound - taker)
    shifted = jax.random.randint(jax.random.fold_in(stream_key, 1), (twos,), 0, 1 << 20) % (margin + 1)
    lengths = lengths.at[1:1 + 2 * twos:2].set(donor - shifted).at[2:2 + 2 * twos:2].set(taker + shifted)
    return lengths[jax.random.permutation(jax.random.fold_in(stream_key, 2), amount)]


def gaussian(rng, dims, deviation, most, cuts=(), kind=jnp.bfloat16):
    level = levels(rng, dims, cuts, -0.22, 0.18) if cuts else 1.0
    values = jax.random.normal(rng, dims, jnp.float32) * deviation * level
    return jnp.minimum(jnp.maximum(values, -most), most).astype(kind)


def setup_inputs(seed: int = 0) -> dict:
    keys = jax.random.split(jax.random.key(seed), 16)
    hidden_in = gaussian(keys[0], (TOKENS, D), 1.0, 6.0, ((0, 32),))
    cond = gaussian(keys[1], (SEQS, D), 1.0, 6.0, ((0, 4),))
    scale_sizes = jax.vmap(lambda own: uneven(own, SCALES, SEQ_LEN, MOST, 1))(jax.random.split(keys[2], SEQS)).reshape((SEQS, SCALES)).astype(jnp.int32)
    w_ada = gaussian(keys[3], (LAYERS, D, 6, D), (4 * D) ** -0.5, 0.09375, ((1, 4), (3, 8)))
    b_ada = gaussian(keys[4], (LAYERS, 6, D), 0.2, 1.0, ((2, 8),))
    w_qkv = gaussian(keys[5], (LAYERS, D, 3, D), D ** -0.5, 0.1875, ((1, 4), (3, 8)))
    b_qkv = gaussian(keys[6], (LAYERS, 2, D), 0.5, 3.0, ((2, 8),))
    head_scale = jnp.clip(jnp.exp(math.log(16.0) - 0.98082925 * jax.random.uniform(keys[7], (LAYERS, HEADS), jnp.float32) ** levels(keys[7], (LAYERS, HEADS), ((1, 8),), -0.2, 0.2)), 6.0, 16.0).astype(jnp.bfloat16)
    w_proj = gaussian(keys[8], (LAYERS, D, D), (D // 16) ** -0.5, 0.75, ((1, 8), (2, 4)))
    b_proj = gaussian(keys[9], (LAYERS, D), 0.5, 3.0, ((1, 8),))
    w_fc1 = gaussian(keys[10], (LAYERS, D, FF), D ** -0.5, 0.1875, ((1, 4), (2, 8)))
    b_fc1 = gaussian(keys[11], (LAYERS, FF), 0.5, 3.0, ((1, 8),))
    w_fc2 = gaussian(keys[12], (LAYERS, FF, D), FF ** -0.5, 0.09375, ((1, 8), (2, 4)))
    b_fc2 = gaussian(keys[13], (LAYERS, D), 0.5, 3.0, ((1, 8),))
    grad_out = gaussian(keys[14], (TOKENS, D), 1.0, 6.0, ((0, 32),))
    return dict(hidden_in=hidden_in, cond=cond, scale_sizes=scale_sizes, w_ada=w_ada, b_ada=b_ada, w_qkv=w_qkv, b_qkv=b_qkv, head_scale=head_scale, w_proj=w_proj, b_proj=b_proj, w_fc1=w_fc1, b_fc1=b_fc1, w_fc2=w_fc2, b_fc2=b_fc2, grad_out=grad_out)


HIGH = lax.Precision.HIGHEST
EPS_NORM = 1e-06
EPS_UNIT = 1e-06
NEG_FILL = -1e+30

@jax.custom_vjp
def low(v):
    return lax.optimization_barrier(v.astype(jnp.bfloat16)).astype(jnp.float32)

@jax.custom_vjp
def low_back(v):
    return v

def low_keep(v):
    return (low(v), None)

def low_pass(kept, grad):
    return (grad,)

def back_keep(v):
    return (v, None)

def back_low(kept, grad):
    return (low(grad),)
low.defvjp(low_keep, low_pass)
low_back.defvjp(back_keep, back_low)

def block_ends(scale_sizes, seq_len):
    ends = jnp.cumsum(scale_sizes, axis=1)
    starts = ends - scale_sizes
    position = jnp.arange(seq_len, dtype=jnp.int32)
    picked = jnp.where(starts[:, None, :] <= position[None, :, None], scale_sizes[:, None, :], 0)
    return lax.optimization_barrier(jnp.sum(picked, axis=2)).astype(jnp.int32)

def layer_norm(values):
    center = lax.optimization_barrier(jnp.mean(values, axis=-1, keepdims=True))
    spread = lax.optimization_barrier(jnp.mean(values * values, axis=-1, keepdims=True)) - center * center
    return (values - center) * lax.rsqrt(spread + EPS_NORM)

def attend(pieces):
    queries, key_rows, value_rows, ends = pieces
    position = jnp.arange(key_rows.shape[0], dtype=jnp.int32)
    scores = low_back(jnp.einsum('the,she->hts', queries, key_rows, precision=HIGH))
    visible = position[None, :] < ends[:, None]
    scores = jnp.where(visible[None], scores, NEG_FILL)
    top = lax.optimization_barrier(jnp.max(scores, axis=-1, keepdims=True))
    expo = jnp.exp(scores - top)
    probs = low(expo / lax.optimization_barrier(jnp.sum(expo, axis=-1, keepdims=True)))
    return jnp.einsum('hts,she->the', probs, value_rows, precision=HIGH)

def block(state, silu_cond, ends, params):
    w_ada, b_ada, w_qkv, b_qkv, head_scale, w_proj, b_proj, w_fc1, b_fc1, w_fc2, b_fc2 = params
    groups, seq_len, width = state.shape
    heads = head_scale.shape[0]
    ada = low_back(jnp.einsum('gd,dkf->gkf', low(silu_cond), w_ada, precision=HIGH) + b_ada)
    gamma1, gamma2, scale1, scale2, shift1, shift2 = [ada[:, index][:, None, :] for index in range(6)]
    hidden1 = low(layer_norm(state) * (1.0 + scale1) + shift1)
    bias_three = jnp.stack((b_qkv[0], jnp.zeros_like(b_qkv[0]), b_qkv[1]))
    mixed_qkv = low_back(jnp.einsum('gtd,dkf->gtkf', hidden1, w_qkv, precision=HIGH) + bias_three)
    mixed_qkv = mixed_qkv.reshape(groups, seq_len, 3, heads, width // heads)
    queries, key_rows, value_rows = (mixed_qkv[:, :, 0], mixed_qkv[:, :, 1], mixed_qkv[:, :, 2])
    q_norm = low(queries * lax.rsqrt(lax.optimization_barrier(jnp.sum(queries * queries, axis=-1, keepdims=True)) + EPS_UNIT) * head_scale[:, None])
    k_norm = low(key_rows * lax.rsqrt(lax.optimization_barrier(jnp.sum(key_rows * key_rows, axis=-1, keepdims=True)) + EPS_UNIT))
    attended = lax.map(jax.checkpoint(attend), (q_norm, k_norm, low(value_rows), ends))
    attn_low = low(low_back(attended)).reshape(groups, seq_len, width)
    branch = low_back(jnp.einsum('gtd,df->gtf', attn_low, w_proj, precision=HIGH) + b_proj)
    middle = state + gamma1 * branch
    hidden2 = low(layer_norm(middle) * (1.0 + scale2) + shift2)
    pre_act = low_back(jnp.einsum('gtd,df->gtf', hidden2, w_fc1, precision=HIGH) + b_fc1)
    act_low = low(jax.nn.gelu(pre_act, approximate=True))
    feed = low_back(jnp.einsum('gtd,df->gtf', act_low, w_fc2, precision=HIGH) + b_fc2)
    return middle + gamma2 * feed

def reference(hidden_in, cond, scale_sizes, w_ada, b_ada, w_qkv, b_qkv, head_scale, w_proj, b_proj, w_fc1, b_fc1, w_fc2, b_fc2, grad_out):
    weights = tuple((a.astype(jnp.float32) for a in (w_ada, b_ada, w_qkv, b_qkv, head_scale, w_proj, b_proj, w_fc1, b_fc1, w_fc2, b_fc2)))
    seqs = cond.shape[0]
    group = 4 if seqs % 4 == 0 else 1
    steps_count = seqs // group
    ends = block_ends(scale_sizes, SEQ_LEN).reshape(steps_count, group, SEQ_LEN)
    states = hidden_in.astype(jnp.float32).reshape(steps_count, group, SEQ_LEN, D)
    silu_all = jax.nn.silu(cond.astype(jnp.float32)).reshape(steps_count, group, D)
    cotangent = grad_out.astype(jnp.float32).reshape(steps_count, group, SEQ_LEN, D)

    def step_fn(totals, item):
        state_group, cond_group, ends_group, grad_group = item

        def run(values, params):
            for layer_index in range(LAYERS):
                values = block(values, cond_group, ends_group, tuple((p[layer_index] for p in params)))
            return values
        result, pull = jax.vjp(run, state_group, weights)
        grad_state, grad_weights = pull(grad_group)
        return (jax.tree.map(jnp.add, totals, grad_weights), (result, grad_state))
    init = jax.tree.map(jnp.zeros_like, weights)
    totals, (results, grad_states) = lax.scan(step_fn, init, (states, silu_all, ends, cotangent))
    return (results.reshape(TOKENS, D).astype(jnp.bfloat16), grad_states.reshape(TOKENS, D), totals[0], totals[1], totals[2], totals[3], totals[4], totals[5], totals[6], totals[7], totals[8], totals[9], totals[10])
```

```python
import jax
import jax.numpy as jnp
from jax import lax
from jax.sharding import PartitionSpec as P

HIGH = lax.Precision.HIGHEST
EPS_NORM = 1e-06
EPS_UNIT = 1e-06
NEG_FILL = -1e30


def block_ends(scale_sizes, seq_len):
    ends = jnp.cumsum(scale_sizes, axis=1)
    starts = ends - scale_sizes
    position = jnp.arange(seq_len, dtype=jnp.int32)
    picked = jnp.where(starts[:, None, :] <= position[None, :, None], scale_sizes[:, None, :], 0)
    return jnp.sum(picked, axis=2)


def normalize(values):
    center = jnp.mean(values, axis=-1, keepdims=True)
    spread = jnp.mean(values * values, axis=-1, keepdims=True) - center * center
    rstd = lax.rsqrt(spread + EPS_NORM)
    return ((values - center) * rstd, rstd)


def norm_back(grad_normed, normed, rstd):
    means = jnp.mean(grad_normed, axis=-1, keepdims=True)
    crosses = jnp.mean(grad_normed * normed, axis=-1, keepdims=True)
    return rstd * (grad_normed - means - normed * crosses)


def unit_pair(queries, key_rows, scale_here):
    q_norm = (
        queries
        * lax.rsqrt(jnp.sum(queries * queries, axis=-1, keepdims=True) + EPS_UNIT)
        * scale_here[:, None]
    )
    k_norm = key_rows * lax.rsqrt(jnp.sum(key_rows * key_rows, axis=-1, keepdims=True) + EPS_UNIT)
    return (q_norm, k_norm)


def project_in(hidden_low, weight):
    return (
        jnp.dot(
            lax.all_gather(hidden_low, "col", axis=0, tiled=True),
            weight,
            preferred_element_type=jnp.float32,
        ),
        hidden_low,
    )


def back_in(grad_three, kept, weight, whole_weight):
    tok_row = grad_three.shape[0]
    grad_low = grad_three.reshape(tok_row, grad_three.shape[1] * grad_three.shape[2])
    own_grads = lax.all_to_all(grad_three, "col", split_axis=0, concat_axis=2, tiled=True)
    grad_hidden = lax.dot_general(
        own_grads, whole_weight, (((1, 2), (1, 2)), ((), ())), preferred_element_type=jnp.float32
    )

    def add_piece(total, piece, start):
        return lax.dot_general(
            piece, grad_low, (((0,), (0,)), ((), ())), preferred_element_type=jnp.float32
        )

    init = jnp.zeros(weight.shape, jnp.float32)
    grad_weight = add_piece(init, lax.all_gather(kept, "col", axis=0, tiled=True), jnp.int32(0))
    return (grad_hidden, grad_weight)


def project_out(act_low, whole_weight):
    own_rows = lax.all_to_all(act_low, "col", split_axis=0, concat_axis=1, tiled=True)
    return jnp.dot(own_rows, whole_weight, preferred_element_type=jnp.float32)


def back_out(grad_low, act_low, weight):

    def add_piece(carry, piece, start):
        part = lax.dot_general(
            piece, weight, (((1,), (1,)), ((), ())), preferred_element_type=jnp.float32
        )
        grad_weight = lax.dot_general(
            act_low, piece, (((0,), (0,)), ((), ())), preferred_element_type=jnp.float32
        )
        return (part, grad_weight)

    init = (
        jnp.zeros((act_low.shape[0], weight.shape[0]), jnp.float32),
        jnp.zeros(weight.shape, jnp.float32),
    )
    return add_piece(init, lax.all_gather(grad_low, "col", axis=0, tiled=True), jnp.int32(0))


def masked_scores(q_rows, k_rows, ends):
    position = jnp.arange(k_rows.shape[0], dtype=jnp.int32)
    scores = jnp.einsum("the,she->hts", q_rows, k_rows, preferred_element_type=jnp.float32)
    visible = position[None, :] < ends[:, None]
    return jnp.where(visible[None], scores, NEG_FILL)


def attend(pieces):
    q_rows, k_rows, v_rows, ends = pieces
    scores = masked_scores(q_rows, k_rows, ends)
    top = jnp.max(scores, axis=-1, keepdims=True)
    expo = jnp.exp(scores - top)
    total = jnp.sum(expo, axis=-1, keepdims=True)
    probs = (expo / total).astype(jnp.bfloat16)
    attended = jnp.einsum("hts,she->the", probs, v_rows, preferred_element_type=jnp.float32)
    return (attended, (top + jnp.log(total))[..., 0])


def attend_back(pieces):
    q_rows, k_rows, v_rows, ends, log_total, grad_rows = pieces
    scores = masked_scores(q_rows, k_rows, ends)
    probs = jnp.exp(scores - log_total[..., None])
    grad_probs = jnp.einsum("the,she->hts", grad_rows, v_rows, preferred_element_type=jnp.float32)
    delta = jnp.sum(probs * grad_probs, axis=-1, keepdims=True)
    grad_scores = (probs * (grad_probs - delta)).astype(jnp.bfloat16)
    grad_q = jnp.einsum("hts,she->the", grad_scores, k_rows, preferred_element_type=jnp.float32)
    grad_k = jnp.einsum("hts,the->she", grad_scores, q_rows, preferred_element_type=jnp.float32)
    grad_v = jnp.einsum(
        "hts,the->she", probs.astype(jnp.bfloat16), grad_rows, preferred_element_type=jnp.float32
    )
    return (grad_q, grad_k, grad_v)


def gelu_tanh(values):
    return jax.nn.gelu(values, approximate=True)


def on_device(
    hidden_in,
    cond,
    scale_sizes,
    w_ada,
    b_ada,
    w_qkv,
    b_qkv,
    head_scale,
    w_proj,
    b_proj,
    w_fc1,
    b_fc1,
    w_fc2,
    b_fc2,
    grad_out,
):
    seq_row, width = cond.shape
    rows_dev = hidden_in.shape[0]
    tok_row = rows_dev * lax.axis_size("col")
    seq_len = tok_row // seq_row
    layer_count = w_ada.shape[0]
    d_col = b_qkv.shape[2]
    heads_dev = head_scale.shape[1]
    head_width = d_col // heads_dev
    full_ada, full_qkv, full_fc1, full_proj, full_fc2 = (
        lax.all_gather(w_ada, "row", axis=1, tiled=True),
        lax.all_gather(w_qkv, "row", axis=1, tiled=True),
        lax.all_gather(w_fc1, "row", axis=1, tiled=True),
        lax.all_gather(w_proj, "row", axis=2, tiled=True),
        lax.all_gather(w_fc2, "row", axis=2, tiled=True),
    )
    whole_proj, whole_fc2, whole_qkv, whole_fc1 = (
        lax.all_gather(full_proj, "col", axis=1, tiled=True),
        lax.all_gather(full_fc2, "col", axis=1, tiled=True),
        lax.all_gather(full_qkv, "col", axis=3, tiled=True),
        lax.all_gather(full_fc1, "col", axis=2, tiled=True),
    )
    ends = block_ends(scale_sizes, seq_len)
    silu_low = jax.nn.silu(cond.astype(jnp.float32)).astype(jnp.bfloat16)
    places = lax.axis_index("col") * rows_dev + jnp.arange(rows_dev, dtype=jnp.int32)
    member = (places[:, None] // seq_len == jnp.arange(seq_row, dtype=jnp.int32)[None, :]).astype(
        jnp.float32
    )

    def per_token(values):
        return jnp.dot(member, values, precision=HIGH)

    def per_sequence(values):
        return lax.dot_general(member, values, (((0,), (0,)), ((), ())), precision=HIGH)

    ada_parts = []
    for layer_index in range(layer_count):
        part = jnp.dot(
            silu_low,
            full_ada[layer_index].reshape(width, 6 * d_col),
            preferred_element_type=jnp.float32,
        )
        ada_parts.append(
            part.reshape(seq_row, 6, d_col) + b_ada[layer_index].astype(jnp.float32)[None]
        )
    ada_full, bias_proj_full, bias_fc2_full = (
        lax.all_gather(jnp.stack(ada_parts), "col", axis=3, tiled=True),
        lax.all_gather(b_proj.astype(jnp.float32), "col", axis=1, tiled=True),
        lax.all_gather(b_fc2.astype(jnp.float32), "col", axis=1, tiled=True),
    )
    current = hidden_in.astype(jnp.float32)
    saved = []
    for layer_index in range(layer_count):
        ada = ada_full[layer_index]
        gamma1, gamma2, scale1, scale2, shift1, shift2 = [
            per_token(ada[:, index]) for index in range(6)
        ]
        normed1, rstd1 = normalize(current)
        hidden1 = (normed1 * (1.0 + scale1) + shift1).astype(jnp.bfloat16)
        mixed_qkv, kept1 = project_in(hidden1, full_qkv[layer_index].reshape(width, 3 * d_col))
        bias_two = b_qkv[layer_index].astype(jnp.float32)
        bias_three = jnp.stack((bias_two[0], jnp.zeros_like(bias_two[0]), bias_two[1]))
        mixed_qkv = mixed_qkv + bias_three.reshape(1, 3 * d_col)
        split = mixed_qkv.reshape(seq_row, seq_len, 3, heads_dev, head_width)
        queries, key_rows, value_rows = (split[:, :, 0], split[:, :, 1], split[:, :, 2])
        scale_here = head_scale[layer_index].astype(jnp.float32)
        q_norm, k_norm = unit_pair(queries, key_rows, scale_here)
        q_low = q_norm.astype(jnp.bfloat16)
        k_low = k_norm.astype(jnp.bfloat16)
        v_low = value_rows.astype(jnp.bfloat16)
        attended, log_total = lax.map(attend, (q_low, k_low, v_low, ends))
        attn_low = attended.reshape(tok_row, d_col).astype(jnp.bfloat16)
        branch = project_out(attn_low, whole_proj[layer_index]) + bias_proj_full[layer_index][None]
        middle = current + gamma1 * branch
        normed2, rstd2 = normalize(middle)
        hidden2 = (normed2 * (1.0 + scale2) + shift2).astype(jnp.bfloat16)
        pre_act, kept2 = project_in(hidden2, full_fc1[layer_index])
        pre_act = pre_act + b_fc1[layer_index].astype(jnp.float32)[None]
        act_low = gelu_tanh(pre_act).astype(jnp.bfloat16)
        feed = project_out(act_low, whole_fc2[layer_index]) + bias_fc2_full[layer_index][None]
        saved.append(
            (
                normed1,
                rstd1,
                kept1,
                queries,
                key_rows,
                scale_here,
                q_low,
                k_low,
                v_low,
                log_total,
                attn_low,
                branch,
                normed2,
                rstd2,
                kept2,
                pre_act,
                act_low,
                feed,
            )
        )
        current = middle + gamma2 * feed
    mixed = current.astype(jnp.bfloat16)
    grad_state = grad_out.astype(jnp.float32)
    grads_ada = [None] * layer_count
    grads_w_qkv = [None] * layer_count
    grads_b_qkv = [None] * layer_count
    grads_scale = [None] * layer_count
    grads_w_proj = [None] * layer_count
    grads_b_proj = [None] * layer_count
    grads_w_fc1 = [None] * layer_count
    grads_b_fc1 = [None] * layer_count
    grads_w_fc2 = [None] * layer_count
    grads_b_fc2 = [None] * layer_count
    for layer_index in reversed(range(layer_count)):
        (
            normed1,
            rstd1,
            kept1,
            queries,
            key_rows,
            scale_here,
            q_low,
            k_low,
            v_low,
            log_total,
            attn_low,
            branch,
            normed2,
            rstd2,
            kept2,
            pre_act,
            act_low,
            feed,
        ) = saved[layer_index]
        ada = ada_full[layer_index]
        gamma1, gamma2, scale1, scale2, shift1, shift2 = [
            per_token(ada[:, index]) for index in range(6)
        ]
        d_gamma2 = per_sequence(grad_state * feed)
        grad_feed = (grad_state * gamma2).astype(jnp.bfloat16)
        grads_b_fc2[layer_index] = jnp.sum(grad_feed.astype(jnp.float32), axis=0)
        grad_act, grads_w_fc2[layer_index] = back_out(grad_feed, act_low, full_fc2[layer_index])
        gelu_pull = jax.vjp(gelu_tanh, pre_act)[1]
        grad_pre = gelu_pull(grad_act)[0].astype(jnp.bfloat16)
        grads_b_fc1[layer_index] = jnp.sum(grad_pre.astype(jnp.float32), axis=0)
        whole_one = whole_fc1[layer_index].reshape(width, 1, whole_fc1.shape[2])
        grad_hidden2, grads_w_fc1[layer_index] = back_in(
            grad_pre.reshape(tok_row, 1, grad_pre.shape[1]), kept2, full_fc1[layer_index], whole_one
        )
        d_scale2 = per_sequence(grad_hidden2 * normed2)
        d_shift2 = per_sequence(grad_hidden2)
        grad_middle = grad_state + norm_back(grad_hidden2 * (1.0 + scale2), normed2, rstd2)
        d_gamma1 = per_sequence(grad_middle * branch)
        grad_branch = (grad_middle * gamma1).astype(jnp.bfloat16)
        grads_b_proj[layer_index] = jnp.sum(grad_branch.astype(jnp.float32), axis=0)
        grad_attn, grads_w_proj[layer_index] = back_out(
            grad_branch, attn_low, full_proj[layer_index]
        )
        grad_attn_low = grad_attn.astype(jnp.bfloat16).reshape(
            seq_row, seq_len, heads_dev, head_width
        )
        grad_qn, grad_kn, grad_v = lax.map(
            attend_back, (q_low, k_low, v_low, ends, log_total, grad_attn_low)
        )
        unit_pull = jax.vjp(unit_pair, queries, key_rows, scale_here)[1]
        grad_q, grad_k, grads_scale[layer_index] = unit_pull((grad_qn, grad_kn))
        grad_qkv = (
            jnp.stack((grad_q, grad_k, grad_v), axis=2)
            .reshape(tok_row, 3, d_col)
            .astype(jnp.bfloat16)
        )
        bias_sums = jnp.sum(grad_qkv.astype(jnp.float32), axis=0)
        grads_b_qkv[layer_index] = jnp.stack((bias_sums[0], bias_sums[2]))
        grad_hidden1, weight_qkv = back_in(
            grad_qkv, kept1, full_qkv[layer_index].reshape(width, 3 * d_col), whole_qkv[layer_index]
        )
        grads_w_qkv[layer_index] = weight_qkv.reshape(width, 3, d_col)
        d_scale1 = per_sequence(grad_hidden1 * normed1)
        d_shift1 = per_sequence(grad_hidden1)
        grad_state = grad_middle + norm_back(grad_hidden1 * (1.0 + scale1), normed1, rstd1)
        grads_ada[layer_index] = jnp.stack(
            (d_gamma1, d_gamma2, d_scale1, d_scale2, d_shift1, d_shift2), axis=1
        )
    ada_sums, bias_proj_col, bias_fc2_col = (
        lax.psum_scatter(
            jnp.stack(grads_ada).astype(jnp.bfloat16), "col", scatter_dimension=3, tiled=True
        ).astype(jnp.float32),
        lax.psum_scatter(
            jnp.stack(grads_b_proj).astype(jnp.bfloat16), "col", scatter_dimension=1, tiled=True
        ).astype(jnp.float32),
        lax.psum_scatter(
            jnp.stack(grads_b_fc2).astype(jnp.bfloat16), "col", scatter_dimension=1, tiled=True
        ).astype(jnp.float32),
    )
    grad_ada = ada_sums.astype(jnp.bfloat16)
    weights_ada = []
    for layer_index in range(layer_count):
        weight_ada = lax.dot_general(
            silu_low,
            grad_ada[layer_index].reshape(seq_row, 6 * d_col),
            (((0,), (0,)), ((), ())),
            preferred_element_type=jnp.float32,
        )
        weights_ada.append(weight_ada.reshape(width, 6, d_col))
    bias_ada_local = jnp.sum(grad_ada.astype(jnp.float32), axis=1)
    sum_ada, sum_qkv, sum_fc1, sum_proj, sum_fc2 = (
        lax.psum_scatter(
            jnp.stack(weights_ada).astype(jnp.bfloat16), "row", scatter_dimension=1, tiled=True
        ).astype(jnp.float32),
        lax.psum_scatter(
            jnp.stack(grads_w_qkv).astype(jnp.bfloat16), "row", scatter_dimension=1, tiled=True
        ).astype(jnp.float32),
        lax.psum_scatter(
            jnp.stack(grads_w_fc1).astype(jnp.bfloat16), "row", scatter_dimension=1, tiled=True
        ).astype(jnp.float32),
        lax.psum_scatter(
            jnp.stack(grads_w_proj).astype(jnp.bfloat16), "row", scatter_dimension=2, tiled=True
        ).astype(jnp.float32),
        lax.psum_scatter(
            jnp.stack(grads_w_fc2).astype(jnp.bfloat16), "row", scatter_dimension=2, tiled=True
        ).astype(jnp.float32),
    )
    bias_ada, bias_qkv, scale_grad, bias_proj, bias_fc1, bias_fc2 = lax.psum(
        (
            bias_ada_local,
            jnp.stack(grads_b_qkv),
            jnp.stack(grads_scale),
            bias_proj_col,
            jnp.stack(grads_b_fc1),
            bias_fc2_col,
        ),
        "row",
    )
    return (
        mixed,
        grad_state,
        sum_ada,
        bias_ada,
        sum_qkv,
        bias_qkv,
        scale_grad,
        sum_proj,
        bias_proj,
        sum_fc1,
        bias_fc1,
        sum_fc2,
        bias_fc2,
    )


BF = jnp.bfloat16
F32 = jnp.float32
NT = (((1,), (1,)), ((), ()))
TN = (((0,), (0,)), ((), ()))


def sibling(values):
    return lax.ppermute(values, "core", [(0, 1), (1, 0)])


def across(values, axis):
    return lax.ppermute(values, axis, [(0, 1), (1, 0)])


def trade(values):
    return lax.ppermute(values, ("core", "x"), [(0, 0), (1, 2), (2, 1), (3, 3)])


def turned(values, flag, axis):
    half = values.shape[axis] // 2
    return jnp.where(flag == 1, jnp.roll(values, half, axis), values)


def dot(left, right, dims=(((1,), (0,)), ((), ()))):
    return lax.dot_general(left, right, dims, preferred_element_type=F32)


def gelu_and_slope(values):
    root = 0.7978845608028654
    inner = root * (values + 0.044715 * values * values * values)
    tanh = jnp.tanh(inner)
    slope = 0.5 * (1.0 + tanh) + 0.5 * values * (1.0 - tanh * tanh) * root * (
        1.0 + 3.0 * 0.044715 * values * values
    )
    return 0.5 * values * (1.0 + tanh), slope


def gather_blocks(shard):
    by_z = lax.all_gather(shard, "z", axis=0, tiled=False)
    first, second = by_z[:, :128], by_z[:, 128:]
    a_x = across(first, "x")
    b_y = across(second, "y")
    a_y = across(jnp.stack((first, a_x)), "y")
    b_x = across(jnp.stack((second, b_y)), "x")
    return (
        ((first, a_y[0]), (a_x, a_y[1])),
        ((second, b_y), (b_x[0], b_x[1])),
    )


def joined(blocks):
    rows = []
    for half in blocks:
        for by_x in half:
            rows.append(
                jnp.concatenate(
                    [part.reshape(part.shape[0] * part.shape[1], part.shape[2]) for part in by_x],
                    axis=1,
                )
            )
    return jnp.concatenate(rows, axis=0)


def scatter(send_a, keep_a, send_b, keep_b):
    got_a = across(send_a, "y")
    got_b = across(send_b, "x")
    quarter, low = send_b.shape[0], send_a.shape[1]
    sum_a = (keep_a.astype(F32) + got_a.astype(F32)).astype(BF)
    sum_b = (keep_b.astype(F32) + got_b.astype(F32)).astype(BF)
    got_a = across(sum_a[quarter:], "x")
    got_b = across(sum_b[:, low:], "y")
    sum_a = sum_a[:quarter].astype(F32) + got_a.astype(F32)
    sum_b = sum_b[:, :low].astype(F32) + got_b.astype(F32)
    both = jnp.concatenate(
        [v.astype(BF).reshape(4, quarter // 4, low) for v in (sum_a, sum_b)], axis=1
    )
    return lax.psum_scatter(both, "z", scatter_dimension=0, tiled=False)


def scatter_product(left, right):
    low, mid, quarter = right.shape[1] // 2, left.shape[1] // 2, left.shape[1] // 4
    send_a = dot(left[:, :mid], right[:, low:], TN).astype(BF)
    send_b = dot(left[:, mid + quarter :], right, TN).astype(BF)
    keep_a = dot(left[:, :mid], right[:, :low], TN)
    keep_b = dot(left[:, mid : mid + quarter], right, TN)
    return scatter(send_a, keep_a, send_b, keep_b)


def scatter_attn(d_q, d_k, d_v, attn, hidden1, d_branch, heads, head_width):
    parts = [
        dot(v, w, TN).astype(BF).reshape(heads, 1, head_width, w.shape[1])
        for v, w in ((d_q, hidden1), (d_k, hidden1), (d_v, hidden1), (attn, d_branch))
    ]
    width = hidden1.shape[1]
    low = width // 2
    one = jnp.concatenate(parts[:2], axis=1).reshape(-1, width)
    two = jnp.concatenate(parts[2:], axis=1).reshape(-1, width)
    mid = two.shape[0] // 2
    return scatter(one[:, low:], one[:, :low], two[mid:], two[:mid])


def unit_rows(values):
    rate = lax.rsqrt(jnp.sum(values * values, axis=-1, keepdims=True) + EPS_UNIT)
    return values * rate, rate


def on_pair(
    hidden_in, cond, scale_sizes, w_ada, b_ada, w_qkv, b_qkv, head_scale,
    w_proj, b_proj, w_fc1, b_fc1, w_fc2, b_fc2, grad_out,
):
    y = lax.axis_index("y")
    core = lax.axis_index("core")
    z = lax.axis_index("z")
    x = lax.axis_index("x")
    layer_count = w_ada.shape[0]
    seq_row, width = cond.shape
    rows_dev = hidden_in.shape[0]
    rows_pad = -(-rows_dev // 32) * 32
    seq_len = 2 * rows_dev
    d_col = b_qkv.shape[2]
    head_width = d_col // head_scale.shape[1]
    y_size, z_size, x_size = (lax.axis_size(a) for a in ("y", "z", "x"))
    heads = z_size * x_size
    low = width // 2

    def paired(values, hidden_axis, d_axis):
        half = values.shape[hidden_axis] // 2
        first = lax.slice_in_dim(values, 0, half, axis=hidden_axis)
        second = lax.slice_in_dim(values, half, 2 * half, axis=hidden_axis)
        kept = jnp.where(core == 0, first, second)
        got = sibling(jnp.where(core == 0, second, first))
        return jnp.concatenate(
            (jnp.where(core == 0, kept, got), jnp.where(core == 0, got, kept)), axis=d_axis
        )

    rows_d = w_qkv.shape[1]
    qkv_t = jnp.transpose(w_qkv, (0, 2, 3, 1)).reshape(layer_count, 3, 2, head_width, rows_d)
    qkv_t = jnp.transpose(qkv_t, (0, 2, 1, 3, 4)).reshape(layer_count, 6 * head_width, rows_d)
    proj_t = w_proj
    fc1_t = jnp.transpose(w_fc1, (0, 2, 1))
    hid_dev = w_fc1.shape[2]
    packed = jnp.concatenate(
        (
            qkv_t[:, : 3 * head_width], proj_t[:, :head_width],
            fc1_t[:, : hid_dev // 2], w_fc2[:, : hid_dev // 2],
            qkv_t[:, 3 * head_width :], proj_t[:, head_width:],
            fc1_t[:, hid_dev // 2 :], w_fc2[:, hid_dev // 2 :],
        ),
        axis=1,
    )
    shards = paired(packed, 1, 2)
    attn_rows = 4 * head_width
    cuts = (0, attn_rows, attn_rows + hid_dev // 2, attn_rows + hid_dev)
    blocks = [
        [gather_blocks(shards[l, cuts[i] : cuts[i + 1]]) for i in range(3)]
        for l in range(layer_count)
    ]

    cond_low = jax.nn.silu(cond.astype(F32)).astype(BF)
    silu_rows = lax.all_gather(cond_low, ("y", "core"), axis=0, tiled=True)
    row = y * 2 + core
    silu_own = lax.dynamic_slice_in_dim(silu_rows, row * rows_d, rows_d, axis=1)
    seqs = silu_rows.shape[0]
    part = dot(silu_own, jnp.transpose(w_ada, (1, 0, 2, 3)).reshape(rows_d, layer_count * 6 * d_col))
    part = part + jnp.where(row == 0, b_ada.astype(F32).reshape(1, layer_count * 6 * d_col), 0.0)
    to_all = jnp.transpose(part.reshape(y_size, x_size, z_size, -1), (0, 2, 1, 3))
    to_all = jnp.broadcast_to(to_all[:, None], (y_size, 2) + to_all.shape[1:])
    from_all = lax.all_to_all(
        to_all.reshape(y_size * 2 * z_size * x_size, -1), ("y", "core", "z", "x"),
        split_axis=0, concat_axis=0, tiled=True,
    )
    ada = jnp.sum(from_all.reshape(y_size * 2, z_size * x_size, layer_count, 6, d_col), axis=0)
    ada = turned(jnp.transpose(ada, (1, 2, 0, 3)).reshape(layer_count, 6, width), y, 2)

    small = jnp.concatenate(
        [v.reshape(-1) for v in (b_qkv, b_fc1, b_proj, b_fc2, head_scale)]
    )[None]
    small = lax.all_gather(small, ("z", "x"), axis=0, tiled=True).astype(F32)
    small = small.reshape(z_size, x_size, -1)
    sizes = [v.size for v in (b_qkv, b_fc1, b_proj, b_fc2, head_scale)]
    offs = [sum(sizes[:i]) for i in range(6)]
    s_qkv, s_fc1, s_proj, s_fc2, s_scale = [small[:, :, offs[i] : offs[i + 1]] for i in range(5)]

    def by_core(values, shape, axis):
        values = values.reshape((z_size, x_size) + shape)
        return lax.dynamic_index_in_dim(values, core, axis=axis, keepdims=False)

    def x_first(values):
        return turned(jnp.swapaxes(values, 0, 1), x, 0)

    bias_qkv = x_first(by_core(s_qkv, (layer_count, 2, 2, head_width), 4))
    scales = x_first(by_core(s_scale, (layer_count, 2), 3))
    bias_fc1 = x_first(by_core(s_fc1, (layer_count, 2, hid_dev // 2), 3))
    bias_fc1 = bias_fc1.reshape(x_size, z_size, layer_count, 2, hid_dev // 4)
    bias_fc1 = jnp.transpose(bias_fc1, (2, 3, 0, 1, 4)).reshape(layer_count, -1)
    bias_proj = turned(
        jnp.transpose(s_proj.reshape(z_size * x_size, layer_count, d_col), (1, 0, 2)).reshape(layer_count, width), y, 1
    )
    bias_fc2 = turned(
        jnp.transpose(s_fc2.reshape(z_size * x_size, layer_count, d_col), (1, 0, 2)).reshape(layer_count, width), y, 1
    )

    sizes_f = scale_sizes.astype(F32)
    sizes_f = jnp.where(core == x, sizes_f, sibling(sizes_f))
    own_sizes = lax.dynamic_index_in_dim(sizes_f, z, axis=0, keepdims=False).astype(jnp.int32)
    index = jnp.arange(rows_pad, dtype=jnp.int32)
    valid = index < rows_dev
    places = jnp.concatenate((core * rows_dev + index, (1 - core) * rows_dev + index))
    real = jnp.concatenate((valid, valid))
    starts = jnp.cumsum(own_sizes) - own_sizes
    ends = jnp.sum(jnp.where(starts[None, :] <= places[:, None], own_sizes[None, :], 0), axis=1)
    visible = (places[None, :] < ends[:, None]) & real[None, :]

    def own_tokens(values):
        return jnp.pad(turned(trade(values), y, 1), ((0, rows_pad - rows_dev), (0, 0)))

    def both_halves(values):
        return jnp.concatenate((values, sibling(values)), axis=0)

    def summed(partial):
        got = sibling(partial[rows_pad:].astype(BF))
        return partial[:rows_pad] + got.astype(F32)

    current = own_tokens(hidden_in).astype(F32)
    grad_state = own_tokens(grad_out).astype(F32)
    saved = []
    for l in range(layer_count):
        gamma1, gamma2, scale1, scale2, shift1, shift2 = [ada[l, i][None] for i in range(6)]
        w_attn, w_one, w_two = [joined(b) for b in blocks[l]]
        w_attn = w_attn.reshape(2, heads, 2, head_width, width)
        w_q, w_k, w_v, w_p = [
            w_attn[h, :, j].reshape(heads * head_width, width) for h in range(2) for j in range(2)
        ]
        normed1, rstd1 = normalize(current)
        hidden1 = both_halves((normed1 * (1.0 + scale1) + shift1).astype(BF))
        b_q = bias_qkv[:, :, l, 0].reshape(1, -1)
        b_v = bias_qkv[:, :, l, 1].reshape(1, -1)
        rows = hidden1.shape[0]
        queries = (dot(hidden1, w_q, NT) + b_q).reshape(rows, heads, head_width)
        keys = dot(hidden1, w_k, NT).reshape(rows, heads, head_width)
        v_low = (dot(hidden1, w_v, NT) + b_v).astype(BF).reshape(rows, heads, head_width)
        scale_here = scales[:, :, l].reshape(heads, 1)
        q_unit, q_rate = unit_rows(queries)
        k_unit, k_rate = unit_rows(keys)
        q_low = (q_unit * scale_here).astype(BF)
        k_low = k_unit.astype(BF)
        scores = jnp.einsum("the,she->hts", q_low, k_low, preferred_element_type=F32)
        scores = jnp.where(visible[None], scores, NEG_FILL)
        top = jnp.max(scores, axis=-1, keepdims=True)
        expo = jnp.exp(scores - top)
        total = jnp.sum(expo, axis=-1, keepdims=True)
        probs = (expo / total).astype(BF)
        attended = jnp.einsum("hts,she->the", probs, v_low, preferred_element_type=F32)
        log_total = top + jnp.log(total)
        attn = attended.reshape(rows, heads * head_width).astype(BF)
        branch = summed(dot(attn, w_p)) + bias_proj[l][None]
        middle = current + gamma1 * branch
        normed2, rstd2 = normalize(middle)
        hidden2 = both_halves((normed2 * (1.0 + scale2) + shift2).astype(BF))
        pre = dot(hidden2, w_one, NT) + bias_fc1[l][None]
        act, slope = gelu_and_slope(pre)
        act = act.astype(BF)
        slope = slope.astype(BF)
        feed = summed(dot(act, w_two)) + bias_fc2[l][None]
        saved.append(
            (normed1, rstd1, hidden1, q_unit, q_rate, q_low, k_unit, k_rate, k_low, v_low, log_total,
             attn, branch, normed2, rstd2, hidden2, slope, act, feed, w_q, w_k, w_v, w_p, w_one, w_two)
        )
        current = middle + gamma2 * feed
    mixed = current.astype(BF)

    d_ada = [None] * layer_count
    d_biases = [None] * layer_count
    d_weights = [None] * layer_count
    for l in reversed(range(layer_count)):
        gamma1, gamma2, scale1, scale2, shift1, shift2 = [ada[l, i][None] for i in range(6)]
        (normed1, rstd1, hidden1, q_unit, q_rate, q_low, k_unit, k_rate, k_low, v_low, log_total,
         attn, branch, normed2, rstd2, hidden2, slope, act, feed, w_q, w_k, w_v, w_p, w_one, w_two) = saved[l]
        rows = hidden1.shape[0]
        scale_here = scales[:, :, l].reshape(heads, 1)
        d_gamma2 = jnp.sum(grad_state * feed, axis=0)
        d_feed = (grad_state * gamma2).astype(BF)
        db_fc2 = jnp.sum(d_feed.astype(F32), axis=0)
        d_feed = both_halves(d_feed)
        d_pre = (dot(d_feed, w_two, NT) * slope.astype(F32)).astype(BF)
        g_two = scatter_product(act, d_feed)
        db_fc1 = jnp.sum(d_pre.astype(F32), axis=0)
        d_hidden2 = summed(dot(d_pre, w_one))
        g_one = scatter_product(d_pre, hidden2)
        d_scale2 = jnp.sum(d_hidden2 * normed2, axis=0)
        d_shift2 = jnp.sum(d_hidden2, axis=0)
        d_middle = grad_state + norm_back(d_hidden2 * (1.0 + scale2), normed2, rstd2)
        d_gamma1 = jnp.sum(d_middle * branch, axis=0)
        d_branch = (d_middle * gamma1).astype(BF)
        db_proj = jnp.sum(d_branch.astype(F32), axis=0)
        d_branch = both_halves(d_branch)
        d_attn = dot(d_branch, w_p, NT).astype(BF).reshape(rows, heads, head_width)
        scores = jnp.einsum("the,she->hts", q_low, k_low, preferred_element_type=F32)
        probs = jnp.exp(jnp.where(visible[None], scores, NEG_FILL) - log_total)
        d_probs = jnp.einsum("the,she->hts", d_attn, v_low, preferred_element_type=F32)
        delta = jnp.sum(probs * d_probs, axis=-1, keepdims=True)
        d_scores = (probs * (d_probs - delta)).astype(BF)
        d_qn = jnp.einsum("hts,she->the", d_scores, k_low, preferred_element_type=F32)
        d_kn = jnp.einsum("hts,the->she", d_scores, q_low, preferred_element_type=F32)
        d_v = jnp.einsum("hts,the->she", probs.astype(BF), d_attn, preferred_element_type=F32)
        d_head = jnp.sum(d_qn * q_unit, axis=(0, 2))
        d_qn = d_qn * scale_here
        d_q = q_rate * (d_qn - q_unit * jnp.sum(d_qn * q_unit, axis=-1, keepdims=True))
        d_k = k_rate * (d_kn - k_unit * jnp.sum(d_kn * k_unit, axis=-1, keepdims=True))
        d_q, d_k, d_v = [
            v.astype(BF).reshape(rows, heads * head_width) for v in (d_q, d_k, d_v)
        ]
        db_qkv = jnp.stack(
            (jnp.sum(d_q.astype(F32), axis=0), jnp.sum(d_v.astype(F32), axis=0))
        )
        d_hidden1 = summed(dot(d_q, w_q) + dot(d_k, w_k) + dot(d_v, w_v))
        g_attn = scatter_attn(d_q, d_k, d_v, attn, hidden1, d_branch, heads, head_width)
        d_scale1 = jnp.sum(d_hidden1 * normed1, axis=0)
        d_shift1 = jnp.sum(d_hidden1, axis=0)
        grad_state = d_middle + norm_back(d_hidden1 * (1.0 + scale1), normed1, rstd1)
        d_ada[l] = jnp.stack((d_gamma1, d_gamma2, d_scale1, d_scale2, d_shift1, d_shift2))
        d_biases[l] = (db_qkv, d_head, db_proj, db_fc1, db_fc2)
        d_weights[l] = jnp.concatenate((g_attn, g_one, g_two), axis=0)

    def by_col(values):
        values = turned(values, y, values.ndim - 1)
        lead = values.shape[:-1]
        values = values.reshape(lead + (z_size, x_size, d_col))
        return jnp.moveaxis(values, (-3, -2), (0, 1)).reshape(z_size, x_size, -1)

    def by_hidden(values):
        return jnp.swapaxes(turned(values, x, 0), 0, 1).reshape(z_size, x_size, -1)

    packs = [by_col(jnp.stack(d_ada))]
    for l in range(layer_count):
        db_qkv, d_head, db_proj, db_fc1, db_fc2 = d_biases[l]
        packs.append(by_col(db_proj))
        packs.append(by_col(db_fc2))
        packs.append(by_hidden(jnp.moveaxis(db_qkv.reshape(2, x_size, z_size, head_width), 0, 2)))
        packs.append(
            by_hidden(jnp.moveaxis(db_fc1.reshape(2, x_size, z_size, hid_dev // 4), 0, 2))
        )
        packs.append(by_hidden(d_head.reshape(x_size, z_size, 1)))
    lens = [p.shape[2] for p in packs]
    pack = jnp.concatenate(packs, axis=2)
    pack = jnp.broadcast_to(pack[None], (2 * y_size,) + pack.shape)
    n_dev = 2 * y_size * z_size * x_size
    got = lax.all_to_all(
        pack.reshape(n_dev, -1), ("y", "core", "z", "x"), split_axis=0, concat_axis=0, tiled=True
    ).reshape(y_size, 2, z_size, x_size, -1)
    pos = lens[0]
    d_ada_all = jnp.sum(got[..., :pos], axis=1)
    d_ada_all = jnp.transpose(d_ada_all, (0, 2, 1, 3)).reshape(seqs, -1).astype(BF)
    out_b_ada = jnp.sum(d_ada_all.astype(F32), axis=0).reshape(layer_count, 6, d_col)
    out_w_ada = dot(silu_own, d_ada_all, TN).reshape(rows_d, layer_count, 6, d_col)
    out_w_ada = jnp.transpose(out_w_ada, (1, 0, 2, 3))
    sums = jnp.sum(got[..., pos:], axis=(0, 2, 3))
    outs = {"proj": [], "fc2": [], "qkv": [], "fc1": [], "scale": []}
    pos = 0
    for l in range(layer_count):
        for name, count in zip(("proj", "fc2", "qkv", "fc1", "scale"), lens[1 + 5 * l : 6 + 5 * l]):
            outs[name].append(sums[:, pos : pos + count])
            pos += count
    out_b_proj = jnp.stack([v[0] + v[1] for v in outs["proj"]])
    out_b_fc2 = jnp.stack([v[0] + v[1] for v in outs["fc2"]])
    out_b_qkv = jnp.stack(
        [jnp.swapaxes(v.reshape(2, 2, head_width), 0, 1).reshape(2, d_col) for v in outs["qkv"]]
    )
    out_b_fc1 = jnp.stack([v.reshape(-1) for v in outs["fc1"]])
    out_scale = jnp.stack([v.reshape(-1) for v in outs["scale"]])

    own = jnp.stack(d_weights)
    left, right = own[:, :, : own.shape[2] // 2], own[:, :, own.shape[2] // 2 :]
    kept = jnp.where(core == 0, left, right)
    came = sibling(jnp.where(core == 0, right, left))
    first = jnp.where(core == 0, kept, came).astype(F32)
    second = jnp.where(core == 0, came, kept).astype(F32)
    wq = jnp.stack(
        (first[:, : 3 * head_width], second[:, : 3 * head_width]), axis=1
    ).reshape(layer_count, 2, 3, head_width, rows_d)
    out_w_qkv = jnp.transpose(wq, (0, 4, 2, 1, 3)).reshape(layer_count, rows_d, 3, d_col)
    pick = lambda i, j: jnp.concatenate((first[:, i:j], second[:, i:j]), axis=1)
    out_w_proj = pick(3 * head_width, attn_rows)
    out_w_fc1 = jnp.transpose(pick(cuts[1], cuts[2]), (0, 2, 1))
    out_w_fc2 = pick(cuts[2], cuts[3])

    def given_back(values):
        return trade(turned(values[:rows_dev], y, 1))

    return (
        given_back(mixed), given_back(grad_state), out_w_ada, out_b_ada, out_w_qkv, out_b_qkv,
        out_scale, out_w_proj, out_b_proj, out_w_fc1, out_b_fc1, out_w_fc2, out_b_fc2,
    )


def solution(mesh):
    rows, cols = mesh.devices.shape
    row, col, body, used = "row", "col", on_device, mesh
    if rows == 4 and cols == 8:
        used = jax.sharding.Mesh(
            mesh.devices.reshape(rows // 2, 2, cols // 2, 2), ("y", "core", "z", "x")
        )
        row, col, body = ("y", "core"), ("z", "x"), on_pair
    tokens = P(("row", "col") if used is mesh else row + col, None)
    return jax.shard_map(
        body,
        mesh=used,
        in_specs=(
            tokens,
            P(row, None),
            P(row, None),
            P(None, row, None, col),
            P(None, None, col),
            P(None, row, None, col),
            P(None, None, col),
            P(None, col),
            P(None, col, row),
            P(None, col),
            P(None, row, col),
            P(None, col),
            P(None, col, row),
            P(None, col),
            tokens,
        ),
        out_specs=(
            tokens,
            tokens,
            P(None, row, None, col),
            P(None, None, col),
            P(None, row, None, col),
            P(None, None, col),
            P(None, col),
            P(None, col, row),
            P(None, col),
            P(None, row, col),
            P(None, col),
            P(None, col, row),
            P(None, col),
        ),
        check_vma=False,
    )
```

```python
import jax
import jax.numpy as jnp
from jax import lax
from jax.experimental import pallas as pl
from jax.experimental.pallas import tpu as pltpu
from jax.sharding import PartitionSpec as P

HIGH = lax.Precision.HIGHEST
EPS_NORM = 1e-06
EPS_UNIT = 1e-06
NEG_FILL = -1e30


def block_ends(scale_sizes, seq_len):
    ends = jnp.cumsum(scale_sizes, axis=1)
    starts = ends - scale_sizes
    position = jnp.arange(seq_len, dtype=jnp.int32)
    picked = jnp.where(starts[:, None, :] <= position[None, :, None], scale_sizes[:, None, :], 0)
    return jnp.sum(picked, axis=2)


def normalize(values):
    center = jnp.mean(values, axis=-1, keepdims=True)
    spread = jnp.mean(values * values, axis=-1, keepdims=True) - center * center
    rstd = lax.rsqrt(spread + EPS_NORM)
    return ((values - center) * rstd, rstd)


def norm_back(grad_normed, normed, rstd):
    means = jnp.mean(grad_normed, axis=-1, keepdims=True)
    crosses = jnp.mean(grad_normed * normed, axis=-1, keepdims=True)
    return rstd * (grad_normed - means - normed * crosses)


def unit_pair(queries, key_rows, scale_here):
    q_norm = (
        queries
        * lax.rsqrt(jnp.sum(queries * queries, axis=-1, keepdims=True) + EPS_UNIT)
        * scale_here[:, None]
    )
    k_norm = key_rows * lax.rsqrt(jnp.sum(key_rows * key_rows, axis=-1, keepdims=True) + EPS_UNIT)
    return (q_norm, k_norm)


def project_in(hidden_low, weight):
    return (
        jnp.dot(
            lax.all_gather(hidden_low, "col", axis=0, tiled=True),
            weight,
            preferred_element_type=jnp.float32,
        ),
        hidden_low,
    )


def back_in(grad_three, kept, weight, whole_weight):
    tok_row = grad_three.shape[0]
    grad_low = grad_three.reshape(tok_row, grad_three.shape[1] * grad_three.shape[2])
    own_grads = lax.all_to_all(grad_three, "col", split_axis=0, concat_axis=2, tiled=True)
    grad_hidden = lax.dot_general(
        own_grads, whole_weight, (((1, 2), (1, 2)), ((), ())), preferred_element_type=jnp.float32
    )

    def add_piece(total, piece, start):
        return lax.dot_general(
            piece, grad_low, (((0,), (0,)), ((), ())), preferred_element_type=jnp.float32
        )

    init = jnp.zeros(weight.shape, jnp.float32)
    grad_weight = add_piece(init, lax.all_gather(kept, "col", axis=0, tiled=True), jnp.int32(0))
    return (grad_hidden, grad_weight)


def project_out(act_low, whole_weight):
    own_rows = lax.all_to_all(act_low, "col", split_axis=0, concat_axis=1, tiled=True)
    return jnp.dot(own_rows, whole_weight, preferred_element_type=jnp.float32)


def back_out(grad_low, act_low, weight):

    def add_piece(carry, piece, start):
        part = lax.dot_general(
            piece, weight, (((1,), (1,)), ((), ())), preferred_element_type=jnp.float32
        )
        grad_weight = lax.dot_general(
            act_low, piece, (((0,), (0,)), ((), ())), preferred_element_type=jnp.float32
        )
        return (part, grad_weight)

    init = (
        jnp.zeros((act_low.shape[0], weight.shape[0]), jnp.float32),
        jnp.zeros(weight.shape, jnp.float32),
    )
    return add_piece(init, lax.all_gather(grad_low, "col", axis=0, tiled=True), jnp.int32(0))


def masked_scores(q_rows, k_rows, ends):
    position = jnp.arange(k_rows.shape[0], dtype=jnp.int32)
    scores = jnp.einsum("the,she->hts", q_rows, k_rows, preferred_element_type=jnp.float32)
    visible = position[None, :] < ends[:, None]
    return jnp.where(visible[None], scores, NEG_FILL)


def attend(pieces):
    q_rows, k_rows, v_rows, ends = pieces
    scores = masked_scores(q_rows, k_rows, ends)
    top = jnp.max(scores, axis=-1, keepdims=True)
    expo = jnp.exp(scores - top)
    total = jnp.sum(expo, axis=-1, keepdims=True)
    probs = (expo / total).astype(jnp.bfloat16)
    attended = jnp.einsum("hts,she->the", probs, v_rows, preferred_element_type=jnp.float32)
    return (attended, (top + jnp.log(total))[..., 0])


def attend_back(pieces):
    q_rows, k_rows, v_rows, ends, log_total, grad_rows = pieces
    scores = masked_scores(q_rows, k_rows, ends)
    probs = jnp.exp(scores - log_total[..., None])
    grad_probs = jnp.einsum("the,she->hts", grad_rows, v_rows, preferred_element_type=jnp.float32)
    delta = jnp.sum(probs * grad_probs, axis=-1, keepdims=True)
    grad_scores = (probs * (grad_probs - delta)).astype(jnp.bfloat16)
    grad_q = jnp.einsum("hts,she->the", grad_scores, k_rows, preferred_element_type=jnp.float32)
    grad_k = jnp.einsum("hts,the->she", grad_scores, q_rows, preferred_element_type=jnp.float32)
    grad_v = jnp.einsum(
        "hts,the->she", probs.astype(jnp.bfloat16), grad_rows, preferred_element_type=jnp.float32
    )
    return (grad_q, grad_k, grad_v)


def gelu_tanh(values):
    return jax.nn.gelu(values, approximate=True)


def on_device(
    hidden_in,
    cond,
    scale_sizes,
    w_ada,
    b_ada,
    w_qkv,
    b_qkv,
    head_scale,
    w_proj,
    b_proj,
    w_fc1,
    b_fc1,
    w_fc2,
    b_fc2,
    grad_out,
):
    seq_row, width = cond.shape
    rows_dev = hidden_in.shape[0]
    tok_row = rows_dev * lax.axis_size("col")
    seq_len = tok_row // seq_row
    layer_count = w_ada.shape[0]
    d_col = b_qkv.shape[2]
    heads_dev = head_scale.shape[1]
    head_width = d_col // heads_dev
    full_ada, full_qkv, full_fc1, full_proj, full_fc2 = (
        lax.all_gather(w_ada, "row", axis=1, tiled=True),
        lax.all_gather(w_qkv, "row", axis=1, tiled=True),
        lax.all_gather(w_fc1, "row", axis=1, tiled=True),
        lax.all_gather(w_proj, "row", axis=2, tiled=True),
        lax.all_gather(w_fc2, "row", axis=2, tiled=True),
    )
    whole_proj, whole_fc2, whole_qkv, whole_fc1 = (
        lax.all_gather(full_proj, "col", axis=1, tiled=True),
        lax.all_gather(full_fc2, "col", axis=1, tiled=True),
        lax.all_gather(full_qkv, "col", axis=3, tiled=True),
        lax.all_gather(full_fc1, "col", axis=2, tiled=True),
    )
    ends = block_ends(scale_sizes, seq_len)
    silu_low = jax.nn.silu(cond.astype(jnp.float32)).astype(jnp.bfloat16)
    places = lax.axis_index("col") * rows_dev + jnp.arange(rows_dev, dtype=jnp.int32)
    member = (places[:, None] // seq_len == jnp.arange(seq_row, dtype=jnp.int32)[None, :]).astype(
        jnp.float32
    )

    def per_token(values):
        return jnp.dot(member, values, precision=HIGH)

    def per_sequence(values):
        return lax.dot_general(member, values, (((0,), (0,)), ((), ())), precision=HIGH)

    ada_parts = []
    for layer_index in range(layer_count):
        part = jnp.dot(
            silu_low,
            full_ada[layer_index].reshape(width, 6 * d_col),
            preferred_element_type=jnp.float32,
        )
        ada_parts.append(
            part.reshape(seq_row, 6, d_col) + b_ada[layer_index].astype(jnp.float32)[None]
        )
    ada_full, bias_proj_full, bias_fc2_full = (
        lax.all_gather(jnp.stack(ada_parts), "col", axis=3, tiled=True),
        lax.all_gather(b_proj.astype(jnp.float32), "col", axis=1, tiled=True),
        lax.all_gather(b_fc2.astype(jnp.float32), "col", axis=1, tiled=True),
    )
    current = hidden_in.astype(jnp.float32)
    saved = []
    for layer_index in range(layer_count):
        ada = ada_full[layer_index]
        gamma1, gamma2, scale1, scale2, shift1, shift2 = [
            per_token(ada[:, index]) for index in range(6)
        ]
        normed1, rstd1 = normalize(current)
        hidden1 = (normed1 * (1.0 + scale1) + shift1).astype(jnp.bfloat16)
        mixed_qkv, kept1 = project_in(hidden1, full_qkv[layer_index].reshape(width, 3 * d_col))
        bias_two = b_qkv[layer_index].astype(jnp.float32)
        bias_three = jnp.stack((bias_two[0], jnp.zeros_like(bias_two[0]), bias_two[1]))
        mixed_qkv = mixed_qkv + bias_three.reshape(1, 3 * d_col)
        split = mixed_qkv.reshape(seq_row, seq_len, 3, heads_dev, head_width)
        queries, key_rows, value_rows = (split[:, :, 0], split[:, :, 1], split[:, :, 2])
        scale_here = head_scale[layer_index].astype(jnp.float32)
        q_norm, k_norm = unit_pair(queries, key_rows, scale_here)
        q_low = q_norm.astype(jnp.bfloat16)
        k_low = k_norm.astype(jnp.bfloat16)
        v_low = value_rows.astype(jnp.bfloat16)
        attended, log_total = lax.map(attend, (q_low, k_low, v_low, ends))
        attn_low = attended.reshape(tok_row, d_col).astype(jnp.bfloat16)
        branch = project_out(attn_low, whole_proj[layer_index]) + bias_proj_full[layer_index][None]
        middle = current + gamma1 * branch
        normed2, rstd2 = normalize(middle)
        hidden2 = (normed2 * (1.0 + scale2) + shift2).astype(jnp.bfloat16)
        pre_act, kept2 = project_in(hidden2, full_fc1[layer_index])
        pre_act = pre_act + b_fc1[layer_index].astype(jnp.float32)[None]
        act_low = gelu_tanh(pre_act).astype(jnp.bfloat16)
        feed = project_out(act_low, whole_fc2[layer_index]) + bias_fc2_full[layer_index][None]
        saved.append(
            (
                normed1,
                rstd1,
                kept1,
                queries,
                key_rows,
                scale_here,
                q_low,
                k_low,
                v_low,
                log_total,
                attn_low,
                branch,
                normed2,
                rstd2,
                kept2,
                pre_act,
                act_low,
                feed,
            )
        )
        current = middle + gamma2 * feed
    mixed = current.astype(jnp.bfloat16)
    grad_state = grad_out.astype(jnp.float32)
    grads_ada = [None] * layer_count
    grads_w_qkv = [None] * layer_count
    grads_b_qkv = [None] * layer_count
    grads_scale = [None] * layer_count
    grads_w_proj = [None] * layer_count
    grads_b_proj = [None] * layer_count
    grads_w_fc1 = [None] * layer_count
    grads_b_fc1 = [None] * layer_count
    grads_w_fc2 = [None] * layer_count
    grads_b_fc2 = [None] * layer_count
    for layer_index in reversed(range(layer_count)):
        (
            normed1,
            rstd1,
            kept1,
            queries,
            key_rows,
            scale_here,
            q_low,
            k_low,
            v_low,
            log_total,
            attn_low,
            branch,
            normed2,
            rstd2,
            kept2,
            pre_act,
            act_low,
            feed,
        ) = saved[layer_index]
        ada = ada_full[layer_index]
        gamma1, gamma2, scale1, scale2, shift1, shift2 = [
            per_token(ada[:, index]) for index in range(6)
        ]
        d_gamma2 = per_sequence(grad_state * feed)
        grad_feed = (grad_state * gamma2).astype(jnp.bfloat16)
        grads_b_fc2[layer_index] = jnp.sum(grad_feed.astype(jnp.float32), axis=0)
        grad_act, grads_w_fc2[layer_index] = back_out(grad_feed, act_low, full_fc2[layer_index])
        gelu_pull = jax.vjp(gelu_tanh, pre_act)[1]
        grad_pre = gelu_pull(grad_act)[0].astype(jnp.bfloat16)
        grads_b_fc1[layer_index] = jnp.sum(grad_pre.astype(jnp.float32), axis=0)
        whole_one = whole_fc1[layer_index].reshape(width, 1, whole_fc1.shape[2])
        grad_hidden2, grads_w_fc1[layer_index] = back_in(
            grad_pre.reshape(tok_row, 1, grad_pre.shape[1]), kept2, full_fc1[layer_index], whole_one
        )
        d_scale2 = per_sequence(grad_hidden2 * normed2)
        d_shift2 = per_sequence(grad_hidden2)
        grad_middle = grad_state + norm_back(grad_hidden2 * (1.0 + scale2), normed2, rstd2)
        d_gamma1 = per_sequence(grad_middle * branch)
        grad_branch = (grad_middle * gamma1).astype(jnp.bfloat16)
        grads_b_proj[layer_index] = jnp.sum(grad_branch.astype(jnp.float32), axis=0)
        grad_attn, grads_w_proj[layer_index] = back_out(
            grad_branch, attn_low, full_proj[layer_index]
        )
        grad_attn_low = grad_attn.astype(jnp.bfloat16).reshape(
            seq_row, seq_len, heads_dev, head_width
        )
        grad_qn, grad_kn, grad_v = lax.map(
            attend_back, (q_low, k_low, v_low, ends, log_total, grad_attn_low)
        )
        unit_pull = jax.vjp(unit_pair, queries, key_rows, scale_here)[1]
        grad_q, grad_k, grads_scale[layer_index] = unit_pull((grad_qn, grad_kn))
        grad_qkv = (
            jnp.stack((grad_q, grad_k, grad_v), axis=2)
            .reshape(tok_row, 3, d_col)
            .astype(jnp.bfloat16)
        )
        bias_sums = jnp.sum(grad_qkv.astype(jnp.float32), axis=0)
        grads_b_qkv[layer_index] = jnp.stack((bias_sums[0], bias_sums[2]))
        grad_hidden1, weight_qkv = back_in(
            grad_qkv, kept1, full_qkv[layer_index].reshape(width, 3 * d_col), whole_qkv[layer_index]
        )
        grads_w_qkv[layer_index] = weight_qkv.reshape(width, 3, d_col)
        d_scale1 = per_sequence(grad_hidden1 * normed1)
        d_shift1 = per_sequence(grad_hidden1)
        grad_state = grad_middle + norm_back(grad_hidden1 * (1.0 + scale1), normed1, rstd1)
        grads_ada[layer_index] = jnp.stack(
            (d_gamma1, d_gamma2, d_scale1, d_scale2, d_shift1, d_shift2), axis=1
        )
    ada_sums, bias_proj_col, bias_fc2_col = (
        lax.psum_scatter(
            jnp.stack(grads_ada).astype(jnp.bfloat16), "col", scatter_dimension=3, tiled=True
        ).astype(jnp.float32),
        lax.psum_scatter(
            jnp.stack(grads_b_proj).astype(jnp.bfloat16), "col", scatter_dimension=1, tiled=True
        ).astype(jnp.float32),
        lax.psum_scatter(
            jnp.stack(grads_b_fc2).astype(jnp.bfloat16), "col", scatter_dimension=1, tiled=True
        ).astype(jnp.float32),
    )
    grad_ada = ada_sums.astype(jnp.bfloat16)
    weights_ada = []
    for layer_index in range(layer_count):
        weight_ada = lax.dot_general(
            silu_low,
            grad_ada[layer_index].reshape(seq_row, 6 * d_col),
            (((0,), (0,)), ((), ())),
            preferred_element_type=jnp.float32,
        )
        weights_ada.append(weight_ada.reshape(width, 6, d_col))
    bias_ada_local = jnp.sum(grad_ada.astype(jnp.float32), axis=1)
    sum_ada, sum_qkv, sum_fc1, sum_proj, sum_fc2 = (
        lax.psum_scatter(
            jnp.stack(weights_ada).astype(jnp.bfloat16), "row", scatter_dimension=1, tiled=True
        ).astype(jnp.float32),
        lax.psum_scatter(
            jnp.stack(grads_w_qkv).astype(jnp.bfloat16), "row", scatter_dimension=1, tiled=True
        ).astype(jnp.float32),
        lax.psum_scatter(
            jnp.stack(grads_w_fc1).astype(jnp.bfloat16), "row", scatter_dimension=1, tiled=True
        ).astype(jnp.float32),
        lax.psum_scatter(
            jnp.stack(grads_w_proj).astype(jnp.bfloat16), "row", scatter_dimension=2, tiled=True
        ).astype(jnp.float32),
        lax.psum_scatter(
            jnp.stack(grads_w_fc2).astype(jnp.bfloat16), "row", scatter_dimension=2, tiled=True
        ).astype(jnp.float32),
    )
    bias_ada, bias_qkv, scale_grad, bias_proj, bias_fc1, bias_fc2 = lax.psum(
        (
            bias_ada_local,
            jnp.stack(grads_b_qkv),
            jnp.stack(grads_scale),
            bias_proj_col,
            jnp.stack(grads_b_fc1),
            bias_fc2_col,
        ),
        "row",
    )
    return (
        mixed,
        grad_state,
        sum_ada,
        bias_ada,
        sum_qkv,
        bias_qkv,
        scale_grad,
        sum_proj,
        bias_proj,
        sum_fc1,
        bias_fc1,
        sum_fc2,
        bias_fc2,
    )


BF = jnp.bfloat16
F32 = jnp.float32
NN = (((1,), (0,)), ((), ()))
NT = (((1,), (1,)), ((), ()))
TN = (((0,), (0,)), ((), ()))
VMEM_BYTES = 60 * 1024 * 1024


def sibling(values):
    return lax.ppermute(values, "core", [(0, 1), (1, 0)])


def across(values, axis):
    return lax.ppermute(values, axis, [(0, 1), (1, 0)])


def trade(values):
    return lax.ppermute(values, ("core", "x"), [(0, 0), (1, 2), (2, 1), (3, 3)])


def turned(values, flag, axis):
    half = values.shape[axis] // 2
    return jnp.where(flag == 1, jnp.roll(values, half, axis), values)


def dot(left, right, dims=NN):
    return lax.dot_general(left, right, dims, preferred_element_type=F32)


def shape_of(dims, kind):
    return jax.ShapeDtypeStruct(dims, kind)


def call(body, grid, in_specs, out_specs, out_shape, scratch, flops, moved, args):
    return pl.pallas_call(
        body,
        grid=grid,
        in_specs=in_specs,
        out_specs=out_specs,
        out_shape=out_shape,
        scratch_shapes=scratch,
        compiler_params=pltpu.CompilerParams(
            dimension_semantics=("arbitrary",) * len(grid), vmem_limit_bytes=VMEM_BYTES
        ),
        cost_estimate=pl.CostEstimate(flops=flops, bytes_accessed=moved, transcendentals=0),
    )(*args)


def fixed(dims):
    return pl.BlockSpec(dims, lambda *_: (0,) * len(dims))


def row_loop(total, size, body, unroll=1):
    @pl.loop(0, total // size, unroll=unroll)
    def _(step):
        body(pl.ds(pl.multiple_of(step * size, size), size))


def weight_specs(low):
    return [
        pl.BlockSpec((low, low), lambda t: (jnp.minimum(t, 1), 0)),
        pl.BlockSpec((low, low), lambda t: (jnp.maximum(t - 2, 0), 0)),
        pl.BlockSpec((low, low), lambda t: (jnp.minimum(t, 1), 0)),
        fixed((low, low)),
        fixed((low, low)),
    ]


def with_tile(step, refs, body):
    g, gx, gy, ga, gb = refs

    @pl.when(step < 2)
    def _():
        body(g[...], gy[...])

    @pl.when(step == 2)
    def _():
        body(gx[...], ga[...])

    @pl.when(step == 3)
    def _():
        body(gx[...], gb[...])


def join_into(joined, own, other):
    rows = own.shape[0]
    joined[:rows, :] = own[...]
    joined[rows:, :] = other[...]


def fc_up(own, other, blocks, bias):
    rows, width = own.shape
    low, both = width // 2, 2 * rows
    hid = 4 * low

    def body(own_ref, other_ref, g, gx, gy, ga, gb, bias_ref, joined, act, slope):
        step = pl.program_id(0)

        @pl.when(step == 0)
        def _():
            join_into(joined, own_ref, other_ref)

        def product(first, second):
            for lanes in (slice(0, low // 2), slice(low // 2, low)):
                for sl in (slice(0, rows), slice(rows, both)):
                    pre = dot(joined[sl, :low], first[lanes, :], NT)
                    pre = pre + dot(joined[sl, low:], second[lanes, :], NT) + bias_ref[:, lanes]
                    root = 0.7978845608028654
                    square = pre * pre
                    tanh = jnp.tanh(pre * (root + (root * 0.044715) * square))
                    half = 0.5 + 0.5 * tanh
                    act[sl, lanes] = (pre * half).astype(BF)
                    inner = pre * ((0.5 * root) + (1.5 * 0.044715 * root) * square)
                    slope[sl, lanes] = (half + (1.0 - tanh * tanh) * inner).astype(BF)

        with_tile(step, (g, gx, gy, ga, gb), product)

    return call(
        body,
        (4,),
        [fixed((rows, width))] * 2 + weight_specs(low) + [pl.BlockSpec((1, low), lambda t: (0, t))],
        [fixed((both, width))] + [pl.BlockSpec((both, low), lambda t: (0, t))] * 2,
        [shape_of((both, width), BF), shape_of((both, hid), BF), shape_of((both, hid), BF)],
        [],
        2 * both * width * hid,
        2 * hid * width + 6 * both * width + 4 * both * hid,
        (own, other, *blocks, bias),
    )


def fc_back(own, other, up_blocks, down_blocks, slope, act, hidden):
    rows, width = own.shape
    low, both = width // 2, 2 * rows
    hid = 4 * low

    def body(own_ref, other_ref, ug, ugx, ugy, uga, ugb, dg, dgx, dgy, dga, dgb, slope_ref, act_ref, hid_ref,
             sums, out_own, out_other, *rest):
        two_refs, one_refs, (joined, grad, acc) = rest[:5], rest[5:10], rest[10:]
        step = pl.program_id(0)

        @pl.when(step == 0)
        def _():
            join_into(joined, own_ref, other_ref)

        def product(up_one, up_two, down_one, down_two, first, last, near, far):
            for i, sl in enumerate((slice(rows, both), slice(0, rows))):
                value = dot(joined[sl, :low], up_one[...], NT) + dot(joined[sl, low:], up_two[...], NT)
                value = (value * slope_ref[sl, :].astype(F32)).astype(BF)
                grad[sl, :] = value
                total = jnp.sum(value.astype(F32).reshape(rows // 8, 8, low), axis=0)
                sums[...] = total if i == 0 else sums[...] + total
                for lanes, down in ((slice(0, low), down_one), (slice(low, width), down_two)):
                    part = dot(value, down[...])
                    if not first:
                        part = part + acc[sl, lanes]
                    if not last:
                        acc[sl, lanes] = part
                    elif i == 0:
                        out_other[:, lanes] = part.astype(BF)
                    else:
                        out_own[:, lanes] = part
            for refs, left, right in ((two_refs, act_ref, joined), (one_refs, grad, hid_ref)):
                refs[near][...] = dot(left[...], right[:, :low], TN).astype(BF)
                refs[far][...] = dot(left[...], right[:, low:], TN).astype(BF)

        @pl.when(step == 0)
        def _():
            product(ug, ugy, dg, dgy, True, False, 0, 2)

        @pl.when(step == 1)
        def _():
            product(ug, ugy, dg, dgy, False, False, 0, 2)

        @pl.when(step == 2)
        def _():
            product(ugx, uga, dgx, dga, False, False, 1, 3)

        @pl.when(step == 3)
        def _():
            product(ugx, ugb, dgx, dgb, False, True, 1, 4)

    tiles = pl.BlockSpec((both, low), lambda t: (0, t))
    early = pl.BlockSpec((low, low), lambda t: (jnp.minimum(t, 1), 0))
    late = pl.BlockSpec((low, low), lambda t: (jnp.maximum(t - 2, 0), 0))
    whole, part = shape_of((2 * low, low), BF), shape_of((low, low), BF)
    found = call(
        body,
        (4,),
        [fixed((rows, width))] * 2 + weight_specs(low) + weight_specs(low) + [tiles, tiles, fixed((both, width))],
        [pl.BlockSpec((8, low), lambda t: (0, t)), fixed((rows, width)), fixed((rows, width))]
        + [early, late, early, fixed((low, low)), fixed((low, low))] * 2,
        [shape_of((8, hid), F32), shape_of((rows, width), F32), shape_of((rows, width), BF)]
        + [whole, whole, whole, part, part] * 2,
        [pltpu.VMEM((both, width), BF), pltpu.VMEM((both, low), BF), pltpu.VMEM((both, width), F32)],
        8 * both * width * hid,
        8 * hid * width + 6 * both * width + 4 * both * hid + 6 * rows * width,
        (own, other, *up_blocks, *down_blocks, slope, act, hidden),
    )
    return found[:3], found[3:8], found[8:]


def fc_down(left, blocks):
    both, hid = left.shape
    rows, low = both // 2, hid // 4
    width = 2 * low

    def body(left_ref, g, gx, gy, ga, gb, own, other, acc):
        step = pl.program_id(0)

        def product(one, two, first, last):
            for i, sl in enumerate((slice(rows, both), slice(0, rows))):
                for lanes, right in ((slice(0, low), one), (slice(low, width), two)):
                    part = dot(left_ref[sl, :], right[...])
                    if not first:
                        part = part + acc[sl, lanes]
                    if not last:
                        acc[sl, lanes] = part
                    elif i == 0:
                        other[:, lanes] = part.astype(BF)
                    else:
                        own[:, lanes] = part

        @pl.when(step == 0)
        def _():
            product(g, gy, True, False)

        @pl.when(step == 1)
        def _():
            product(g, gy, False, False)

        @pl.when(step == 2)
        def _():
            product(gx, ga, False, False)

        @pl.when(step == 3)
        def _():
            product(gx, gb, False, True)

    return call(
        body,
        (4,),
        [pl.BlockSpec((both, low), lambda t: (0, t))] + weight_specs(low),
        [fixed((rows, width))] * 2,
        [shape_of((rows, width), F32), shape_of((rows, width), BF)],
        [pltpu.VMEM((both, width), F32)],
        2 * both * width * hid,
        2 * hid * width + 2 * both * hid + 6 * rows * width,
        (left, *blocks),
    )


def head_ones(size, head_width):
    first = lax.broadcasted_iota(jnp.int32, (size, size), 0) // head_width
    second = lax.broadcasted_iota(jnp.int32, (size, size), 1) // head_width
    return (first == second).astype(BF)


def qkv_up(own, other, blocks, vectors, ones):
    rows, width = own.shape
    low, both = width // 2, 2 * rows
    tile = low // 2

    def body(own_ref, other_ref, g, gx, gy, ga, gb, vec, ones_ref, joined, q_raw, k_raw, q_low, k_low, v_low, acc):
        step = pl.program_id(0)
        part = step % 3

        @pl.when(step == 0)
        def _():
            join_into(joined, own_ref, other_ref)

        def product(first, second):
            acc[...] = dot(joined[:, :low], first, NT) + dot(joined[:, low:], second, NT)

        @pl.when(step < 3)
        def _():
            product(g[...], gy[...])

        @pl.when(jnp.logical_and(step >= 3, part < 2))
        def _():
            product(gx[...], ga[...])

        @pl.when(step == 5)
        def _():
            product(gx[...], gb[...])

        def unit(value):
            square = dot((value * value).astype(BF), ones_ref[...])
            return value * lax.rsqrt(square + EPS_UNIT)

        @pl.when(part == 0)
        def _():
            def finish(sl):
                value = acc[sl, :] + vec[0:1, :]
                q_raw[sl, :] = value.astype(BF)
                q_low[sl, :] = (unit(value) * vec[2:3, :]).astype(BF)

            row_loop(both, both // 4, finish)

        @pl.when(part == 1)
        def _():
            def finish(sl):
                value = acc[sl, :]
                k_raw[sl, :] = value.astype(BF)
                k_low[sl, :] = unit(value).astype(BF)

            row_loop(both, both // 4, finish)

        @pl.when(part == 2)
        def _():
            v_low[...] = (acc[...] + vec[1:2, :]).astype(BF)

    half = lambda t: t // 3
    kept = pl.BlockSpec((both, tile), lambda t: (0, half(t)))
    heads = shape_of((both, low), BF)
    return call(
        body,
        (6,),
        [fixed((rows, width))] * 2
        + [
            pl.BlockSpec((tile, low), lambda t: (jnp.minimum(t, 2), 0)),
            pl.BlockSpec((tile, low), lambda t: (jnp.maximum(t - 3, 0), 0)),
            pl.BlockSpec((tile, low), lambda t: (jnp.minimum(t, 2), 0)),
            pl.BlockSpec((tile, low), lambda t: (jnp.clip(t - 3, 0, 1), 0)),
            fixed((tile, low)),
            pl.BlockSpec((8, tile), lambda t: (0, half(t))),
            fixed((tile, tile)),
        ],
        [fixed((both, width))] + [kept] * 5,
        [shape_of((both, width), BF)] + [heads] * 5,
        [pltpu.VMEM((both, tile), F32)],
        2 * both * width * 3 * low,
        2 * 3 * low * width + 6 * both * width + 10 * both * low,
        (own, other, *blocks, vectors, ones),
    )


def attn_mix(q_low, k_low, v_low, end_col, place_row, head_width):
    both, low = q_low.shape
    pair = 2 * head_width
    chunk = both // 4

    def body(q_ref, k_ref, v_ref, end_ref, place_ref, out_ref, rest_ref, log_ref):
        place = place_ref[0:1, :]
        ones = jnp.ones((both, head_width), BF)
        for h in range(2):
            lanes = slice(h * head_width, (h + 1) * head_width)
            keys = k_ref[:, lanes]
            values = jnp.concatenate((v_ref[:, lanes], ones), axis=1)
            for c in range(4):
                sl = slice(c * chunk, (c + 1) * chunk)
                scores = dot(q_ref[sl, lanes], keys, NT)
                expo = jnp.where(place < end_ref[sl, :], jnp.exp(scores), 0.0).astype(BF)
                mixed = dot(expo, values)
                total = mixed[:, head_width:]
                value = mixed[:, :head_width] / total
                out_ref[sl, lanes] = value.astype(BF)
                rest_ref[sl, lanes] = (value - value.astype(BF).astype(F32)).astype(BF)
                log_ref[sl, lanes] = jnp.log(total)

    block = pl.BlockSpec((both, pair), lambda t: (0, t))
    return call(
        body,
        (low // pair,),
        [block] * 3 + [fixed((both, 1)), fixed((8, both))],
        [block] * 3,
        [shape_of((both, low), BF)] * 2 + [shape_of((both, low), F32)],
        [],
        4 * both * both * low,
        14 * both * low,
        (q_low, k_low, v_low, end_col, place_row),
    )


def attn_back(own, other, blocks, q_low, k_low, v_low, attn, rest, logs, q_raw, k_raw, hidden, scale_row,
              place_col, end_row, head_width):
    rows, width = own.shape
    both, low = q_low.shape
    pair = 2 * head_width
    chunk = both // 4
    steps = low // pair

    def body(own_ref, other_ref, *refs):
        w_refs, refs = refs[:16], refs[16:]
        (q_ref, k_ref, v_ref, attn_ref, rest_ref, log_ref, qr_ref, kr_ref, hid_ref, scale_ref, place_ref, end_ref,
         sums, out_own, out_other, keep, by_x, by_y, far_a, far_b, joined, weights, ds_ref, three_ref, acc) = refs
        step = pl.program_id(0)

        @pl.when(step == 0)
        def _():
            join_into(joined, own_ref, other_ref)

        for side, when in ((0, step < 2), (1, step >= 2)):
            @pl.when(when)
            def _():
                for i in range(4):
                    rows_i = slice(i * pair, (i + 1) * pair)
                    weights[rows_i, :low] = w_refs[4 * i + 2 * side][...]
                    weights[rows_i, low:] = w_refs[4 * i + 2 * side + 1][...]

        grad_pair = dot(joined[...], weights[3 * pair :, :], NT).astype(BF)
        ends = end_ref[0:1, :]
        lane = lax.broadcasted_iota(jnp.int32, (both, head_width), 1)
        ones = jnp.ones((both, head_width), BF)

        def spread(value):
            high = value.astype(BF)
            rest = value - high.astype(F32)
            mid = rest.astype(BF)
            small = (rest - mid.astype(F32)).astype(BF)
            zero = jnp.zeros_like(high)
            return jnp.where(lane == 0, high, jnp.where(lane == 1, mid, jnp.where(lane == 2, small, zero)))

        def unit_back(raw, grad_unit):
            raw = raw.astype(F32)
            rate = lax.rsqrt(jnp.sum(raw * raw, axis=1, keepdims=True) + EPS_UNIT)
            unit = raw * rate
            cross = jnp.sum(grad_unit * unit, axis=1, keepdims=True)
            return rate * (grad_unit - unit * cross), unit

        for h in range(2):
            lanes = slice(h * head_width, (h + 1) * head_width)
            queries, keys, values, grads = q_ref[:, lanes], k_ref[:, lanes], v_ref[:, lanes], grad_pair[:, lanes]
            mixed = attn_ref[:, lanes].astype(F32) + rest_ref[:, lanes].astype(F32)
            delta = jnp.sum(grads.astype(F32) * mixed, axis=1, keepdims=True)
            q_wide = jnp.concatenate((queries, spread(-log_ref[:, lanes])), axis=1)
            g_wide = jnp.concatenate((grads, spread(jnp.broadcast_to(-delta, (both, head_width)))), axis=1)
            k_wide = jnp.concatenate((keys, ones), axis=1)
            v_wide = jnp.concatenate((values, ones), axis=1)
            dk_parts, dv_parts = [], []
            for c in range(4):
                sl = slice(c * chunk, (c + 1) * chunk)
                scores = dot(k_wide[sl], q_wide, NT)
                probs = jnp.where(place_ref[sl, :] < ends, jnp.exp(scores), 0.0)
                d_probs = dot(v_wide[sl], g_wide, NT)
                d_scores = (probs * d_probs).astype(BF)
                ds_ref[sl, :] = d_scores
                dv_parts.append(dot(probs.astype(BF), grads))
                dk_parts.append(dot(d_scores, queries))
            d_qn = dot(keys, ds_ref[...], TN).T
            d_kn = jnp.concatenate(dk_parts, axis=0)
            d_v = jnp.concatenate(dv_parts, axis=0).astype(BF)
            d_q, unit_q = unit_back(qr_ref[:, lanes], d_qn * scale_ref[0:1, lanes])
            d_k, _ = unit_back(kr_ref[:, lanes], d_kn)
            d_q, d_k = d_q.astype(BF), d_k.astype(BF)
            for i, value in enumerate((d_q, d_k, d_v)):
                three_ref[:, i * pair + h * head_width : i * pair + (h + 1) * head_width] = value
            for i, value in enumerate((d_q.astype(F32), d_v.astype(F32), d_qn * unit_q)):
                sums[i : i + 1, lanes] = jnp.sum(value, axis=0, keepdims=True)

        for lanes in (slice(0, low), slice(low, width)):
            part = dot(three_ref[...], weights[: 3 * pair, lanes])

            @pl.when(step == 0)
            def _():
                acc[:, lanes] = part

            @pl.when(jnp.logical_and(step > 0, step < steps - 1))
            def _():
                acc[:, lanes] += part

            @pl.when(step == steps - 1)
            def _():
                total = acc[:, lanes] + part
                out_own[:, lanes] = total[:rows]
                out_other[:, lanes] = total[rows:].astype(BF)

        for i, lanes in enumerate((slice(0, low), slice(low, width))):
            three = dot(three_ref[...], hid_ref[:, lanes], TN).astype(BF)
            proj = dot(attn_ref[...], joined[:, lanes], TN).astype(BF)
            grads = [three[j * pair : (j + 1) * pair] for j in range(3)] + [proj]

            @pl.when(step < 2)
            def _():
                target = keep if i == 0 else by_y
                for j in range(4):
                    target[j, 0] = grads[j]

            @pl.when(step >= 2)
            def _():
                for j in range(4):
                    if i == 0:
                        by_x[j, 0] = grads[j]
                    else:
                        (far_a if j < 2 else far_b)[j % 2, 0] = grads[j]

    def early(row):
        return pl.BlockSpec((pair, low), lambda t: (row + jnp.minimum(t, 1), 0))

    def late(row):
        return pl.BlockSpec((pair, low), lambda t: (row + jnp.maximum(t - 2, 0), 0))

    g, gx, gy, ga, gb = blocks
    w_specs, w_args = [], []
    for i in range(4):
        w_specs += [early(2 * i), early(2 * i), late(2 * i), late(2 * (i % 2))]
        w_args += [g, gy, gx, ga if i < 2 else gb]
    block = pl.BlockSpec((both, pair), lambda t: (0, t))
    row = pl.BlockSpec((8, pair), lambda t: (0, t))
    first = pl.BlockSpec((4, 1, pair, low), lambda t: (0, jnp.minimum(t, 1), 0, 0))
    second = pl.BlockSpec((4, 1, pair, low), lambda t: (0, jnp.maximum(t - 2, 0), 0, 0))
    halves = pl.BlockSpec((2, 1, pair, low), lambda t: (0, jnp.maximum(t - 2, 0), 0, 0))
    whole, half = shape_of((4, 2, pair, low), BF), shape_of((2, 2, pair, low), BF)
    found = call(
        body,
        (steps,),
        [fixed((rows, width))] * 2 + w_specs + [block] * 8
        + [fixed((both, width)), row, fixed((both, 1)), fixed((8, both))],
        [row, fixed((rows, width)), fixed((rows, width)), first, second, first, halves, halves],
        [shape_of((8, low), F32), shape_of((rows, width), F32), shape_of((rows, width), BF)]
        + [whole, whole, whole, half, half],
        [
            pltpu.VMEM((both, width), BF), pltpu.VMEM((4 * pair, width), BF), pltpu.VMEM((both, both), BF),
            pltpu.VMEM((both, 3 * pair), BF), pltpu.VMEM((both, width), F32),
        ],
        10 * both * both * low + 16 * both * width * low,
        24 * both * low + 8 * both * width,
        (own, other, *w_args, q_low, k_low, v_low, attn, rest, logs, q_raw, k_raw, hidden, scale_row,
         place_col, end_row),
    )
    return found[:3], found[3:]


def attn_down(attn, blocks):
    both, low = attn.shape
    rows, width, tile = both // 2, 2 * low, low // 2

    def body(attn_ref, g, gx, gy, gb, own, other):
        for lanes, first, second in ((slice(0, low), g, gx), (slice(low, width), gy, gb)):
            value = dot(attn_ref[:, :tile], first[...]) + dot(attn_ref[:, tile:], second[...])
            own[:, lanes] = value[:rows]
            other[:, lanes] = value[rows:].astype(BF)

    last = pl.BlockSpec((tile, low), lambda t: (3, 0))
    g, gx, gy, _, gb = blocks
    return call(
        body,
        (1,),
        [fixed((both, low)), last, last, last, pl.BlockSpec((tile, low), lambda t: (1, 0))],
        [fixed((rows, width))] * 2,
        [shape_of((rows, width), F32), shape_of((rows, width), BF)],
        [],
        2 * both * width * low,
        2 * low * width + 2 * both * low + 6 * rows * width,
        (attn, g, gx, gy, gb),
    )


def mix(own, got, state, vectors, last):
    rows, width = own.shape
    part = rows // 2

    def body(own_ref, got_ref, state_ref, vec, branch_ref, next_ref, hid_ref):
        def one(sl):
            branch = own_ref[sl, :] + got_ref[sl, :].astype(F32) + vec[0:1, :]
            branch_ref[sl, :] = branch.astype(BF)
            value = state_ref[sl, :] + vec[1:2, :] * branch
            next_ref[sl, :] = value
            if last:
                hid_ref[sl, :] = value.astype(BF)
            else:
                mean = jnp.mean(value, axis=1, keepdims=True)
                spread = jnp.mean(value * value, axis=1, keepdims=True) - mean * mean
                normed = (value - mean) * lax.rsqrt(spread + EPS_NORM)
                hid_ref[sl, :] = (normed * vec[2:3, :] + vec[3:4, :]).astype(BF)

        row_loop(part, 16, one, unroll=11)

    block = pl.BlockSpec((part, width), lambda t: (t, 0))
    return call(
        body,
        (2,),
        [block] * 3 + [fixed((8, width))],
        [block] * 3,
        [shape_of((rows, width), BF), shape_of((rows, width), F32), shape_of((rows, width), BF)],
        [],
        20 * rows * width,
        18 * rows * width,
        (own, got, state, vectors),
    )


def mix_back(own, got, state, grad, branch, vectors):
    rows, width = own.shape
    part = rows // 2

    def body(own_ref, got_ref, state_ref, grad_ref, branch_ref, vec, next_ref, low_ref, sums):
        @pl.when(pl.program_id(0) == 0)
        def _():
            sums[...] = jnp.zeros_like(sums)

        def add(i, value):
            sums[8 * i : 8 * i + 8, :] += value[:8] + value[8:]

        def one(sl):
            d_hid = own_ref[sl, :] + got_ref[sl, :].astype(F32)
            value = state_ref[sl, :]
            mean = jnp.mean(value, axis=1, keepdims=True)
            spread = jnp.mean(value * value, axis=1, keepdims=True) - mean * mean
            rate = lax.rsqrt(spread + EPS_NORM)
            normed = (value - mean) * rate
            add(0, d_hid * normed)
            add(1, d_hid)
            d_norm = d_hid * vec[0:1, :]
            means = jnp.mean(d_norm, axis=1, keepdims=True)
            crosses = jnp.mean(d_norm * normed, axis=1, keepdims=True)
            total = grad_ref[sl, :] + rate * (d_norm - means - normed * crosses)
            next_ref[sl, :] = total
            add(2, total * branch_ref[sl, :].astype(F32))
            low = (total * vec[1:2, :]).astype(BF)
            low_ref[sl, :] = low
            add(3, low.astype(F32))

        row_loop(part, 16, one, unroll=11)

    block = pl.BlockSpec((part, width), lambda t: (t, 0))
    return call(
        body,
        (2,),
        [block] * 5 + [fixed((8, width))],
        [block] * 2 + [fixed((32, width))],
        [shape_of((rows, width), F32), shape_of((rows, width), BF), shape_of((32, width), F32)],
        [],
        30 * rows * width,
        20 * rows * width,
        (own, got, state, grad, branch, vectors),
    )


def gather_blocks(rows):
    half = rows.shape[0] // 2
    by_x = across(rows, "x")
    by_y = across(rows, "y")
    first = across(by_x[:half], "y")
    second = across(by_y[half:], "x")
    return rows, by_x, by_y, first, second


def scatter_blocks(blocks, parts, z_size):
    keep, by_x, by_y, far_a, far_b = [v.reshape(-1, v.shape[-1]) for v in blocks]
    half = far_a.shape[0]
    got_a, got_b = across(far_a, "y"), across(far_b, "x")

    def added(block, got, start):
        part = block[start : start + half].astype(F32) + got.astype(F32)
        return lax.dynamic_update_slice_in_dim(block, part.astype(BF), start, 0)

    got_x = across(added(by_x, got_a, 0), "x")
    got_y = across(added(by_y, got_b, half), "y")
    total = keep.astype(F32) + got_x.astype(F32) + got_y.astype(F32)
    total = jnp.swapaxes(total.astype(BF).reshape(parts, z_size, -1, keep.shape[1]), 0, 1)
    total = total.reshape(z_size, -1, keep.shape[1])
    return lax.psum_scatter(total, "z", scatter_dimension=0, tiled=False)


def eight_rows(*rows):
    rows = [r.reshape(1, -1) for r in rows]
    return jnp.concatenate(rows + [jnp.zeros_like(rows[0])] * (8 - len(rows)), axis=0)


def on_pair(
    hidden_in, cond, scale_sizes, w_ada, b_ada, w_qkv, b_qkv, head_scale,
    w_proj, b_proj, w_fc1, b_fc1, w_fc2, b_fc2, grad_out,
):
    y = lax.axis_index("y")
    core = lax.axis_index("core")
    z = lax.axis_index("z")
    x = lax.axis_index("x")
    layer_count = w_ada.shape[0]
    seq_row, width = cond.shape
    rows_dev = hidden_in.shape[0]
    rows_pad = -(-rows_dev // 32) * 32
    d_col = b_qkv.shape[2]
    head_width = d_col // head_scale.shape[1]
    y_size, z_size, x_size = (lax.axis_size(a) for a in ("y", "z", "x"))
    heads = z_size * x_size
    low = width // 2
    rows_d = w_qkv.shape[1]
    hid_dev = w_fc1.shape[2]
    hid_core = hid_dev // 2

    qkv_t = jnp.transpose(w_qkv, (0, 2, 3, 1)).reshape(layer_count, 3, 2, head_width, rows_d)
    qkv_t = jnp.transpose(qkv_t, (0, 2, 1, 3, 4)).reshape(layer_count, 6 * head_width, rows_d)
    fc1_t = jnp.transpose(w_fc1, (0, 2, 1))
    three, four = 3 * head_width, 4 * head_width
    halves = [
        jnp.concatenate(parts, axis=1)
        for parts in (
            (qkv_t[:, :three], w_proj[:, :head_width], fc1_t[:, :hid_core], w_fc2[:, :hid_core]),
            (qkv_t[:, three:], w_proj[:, head_width:], fc1_t[:, hid_core:], w_fc2[:, hid_core:]),
        )
    ]
    kept = jnp.where(core == 0, halves[0], halves[1])
    came = sibling(jnp.where(core == 0, halves[1], halves[0]))
    shards = jnp.concatenate(
        (jnp.where(core == 0, kept, came), jnp.where(core == 0, came, kept)), axis=2
    )
    cuts = (0, four, four + hid_core, four + 2 * hid_core)

    def gather(l, i):
        by_z = lax.all_gather(shards[l, cuts[i] : cuts[i + 1]], "z", axis=0, tiled=False)
        if i == 0:
            by_z = jnp.swapaxes(by_z.reshape(z_size, 4, head_width, low), 0, 1)
        return gather_blocks(by_z.reshape(-1, low))

    blocks = [[gather(l, i) for i in range(3)] for l in range(layer_count)]

    cond_low = jax.nn.silu(cond.astype(F32)).astype(BF)
    silu_rows = lax.all_gather(cond_low, ("y", "core"), axis=0, tiled=True)
    row = y * 2 + core
    silu_own = lax.dynamic_slice_in_dim(silu_rows, row * rows_d, rows_d, axis=1)
    seqs = silu_rows.shape[0]
    ada_size = layer_count * 6 * d_col
    part = dot(silu_own, jnp.transpose(w_ada, (1, 0, 2, 3)).reshape(rows_d, ada_size))
    part = part + jnp.where(row == 0, b_ada.astype(F32).reshape(1, ada_size), 0.0)
    smalls = (b_qkv, b_fc1, b_proj, b_fc2, head_scale)
    sizes = [v.size for v in smalls]
    offs = [sum(sizes[:i]) for i in range(6)]
    n_rows = y_size * 2
    quarter = -(-offs[5] // (n_rows * 128)) * 128
    small = jnp.concatenate([v.reshape(-1).astype(F32) for v in smalls])
    small = jnp.pad(small, (0, n_rows * quarter - offs[5])).reshape(n_rows, quarter)
    small = lax.dynamic_index_in_dim(small, row, axis=0, keepdims=True)
    part = jnp.concatenate((part, jnp.broadcast_to(small, (seqs, quarter))), axis=1)
    to_all = jnp.swapaxes(part.reshape(y_size, x_size, z_size, -1), 1, 2)
    to_all = jnp.broadcast_to(to_all[:, None], (y_size, 2) + to_all.shape[1:])
    from_all = lax.all_to_all(
        to_all.reshape(n_rows * z_size * x_size, -1), ("y", "core", "z", "x"),
        split_axis=0, concat_axis=0, tiled=True,
    ).reshape(n_rows, z_size, x_size, -1)
    ada = jnp.sum(from_all[..., :ada_size], axis=0).reshape(z_size * x_size, layer_count, 6, d_col)
    ada = turned(jnp.transpose(ada, (1, 2, 0, 3)).reshape(layer_count, 6, width), y, 2)
    small = jnp.transpose(from_all[..., ada_size:], (1, 2, 0, 3)).reshape(z_size, x_size, -1)
    s_qkv, s_fc1, s_proj, s_fc2, s_scale = [small[:, :, offs[i] : offs[i + 1]] for i in range(5)]

    def by_core(values, shape, axis):
        values = values.reshape((z_size, x_size) + shape)
        values = lax.dynamic_index_in_dim(values, core, axis=axis, keepdims=False)
        return turned(jnp.swapaxes(values, 0, 1), x, 0)

    def by_d(values):
        values = jnp.swapaxes(values.reshape(z_size * x_size, layer_count, d_col), 0, 1)
        return turned(values.reshape(layer_count, width), y, 1)

    bias_qkv = by_core(s_qkv, (layer_count, 2, 2, head_width), 4)
    bias_qkv = jnp.transpose(bias_qkv, (2, 3, 0, 1, 4)).reshape(layer_count, 2, low)
    scales = by_core(s_scale, (layer_count, 2), 3)
    scales = jnp.transpose(scales, (2, 0, 1)).reshape(layer_count, heads)
    scales = jnp.repeat(scales, head_width, axis=1)
    bias_fc1 = by_core(s_fc1, (layer_count, 2, hid_core), 3)
    bias_fc1 = jnp.transpose(bias_fc1, (2, 0, 1, 3)).reshape(layer_count, 1, -1)
    bias_proj, bias_fc2 = by_d(s_proj), by_d(s_fc2)

    sizes_f = scale_sizes.astype(F32)
    sizes_f = jnp.where(core == x, sizes_f, sibling(sizes_f))
    own_sizes = lax.dynamic_index_in_dim(sizes_f, z, axis=0, keepdims=False).astype(jnp.int32)
    index = jnp.arange(rows_pad, dtype=jnp.int32)
    places = jnp.concatenate((core * rows_dev + index, (1 - core) * rows_dev + index))
    starts = jnp.cumsum(own_sizes) - own_sizes
    ends = jnp.sum(jnp.where(starts[None, :] <= places[:, None], own_sizes[None, :], 0), axis=1)
    real = jnp.concatenate((index, index)) < rows_dev
    key_places = jnp.where(real, places, 1 << 20).astype(F32)
    ends = ends.astype(F32)
    place_col, end_col = key_places[:, None], ends[:, None]
    place_row, end_row = eight_rows(key_places), eight_rows(ends)
    ones = head_ones(low // 2, head_width)

    def own_tokens(values):
        return jnp.pad(turned(trade(values), y, 1), ((0, rows_pad - rows_dev), (0, 0)))

    state = own_tokens(hidden_in).astype(F32)
    grad = own_tokens(grad_out).astype(F32)
    hidden = (normalize(state)[0] * (1.0 + ada[0, 2][None]) + ada[0, 4][None]).astype(BF)
    saved = []
    for l in range(layer_count):
        gamma1, gamma2, scale1, scale2, shift1, shift2 = [ada[l, i] for i in range(6)]
        vectors = eight_rows(bias_qkv[l, 0], bias_qkv[l, 1], scales[l])
        joined1, q_raw, k_raw, q_low, k_low, v_low = qkv_up(
            hidden, sibling(hidden), blocks[l][0], vectors, ones
        )
        attn, rest, logs = attn_mix(q_low, k_low, v_low, end_col, place_row, head_width)
        own, send = attn_down(attn, blocks[l][0])
        branch, middle, hidden = mix(
            own, sibling(send), state, eight_rows(bias_proj[l], gamma1, 1.0 + scale2, shift2), False
        )
        joined2, act, slope = fc_up(hidden, sibling(hidden), blocks[l][1], bias_fc1[l])
        own, send = fc_down(act, blocks[l][2])
        last = l == layer_count - 1
        after = ada[l if last else l + 1]
        feed, later, hidden = mix(
            own, sibling(send), middle, eight_rows(bias_fc2[l], gamma2, 1.0 + after[2], after[4]), last
        )
        saved.append(
            (joined1, q_raw, k_raw, q_low, k_low, v_low, logs, attn, rest, branch, middle, joined2, act, slope, feed, state)
        )
        state = later
    mixed = hidden

    top = layer_count - 1
    d_ada = [[None] * 6 for _ in range(layer_count)]
    d_biases = [[None] * 5 for _ in range(layer_count)]
    d_weights = [None] * layer_count
    fold = lambda sums: jnp.sum(sums.reshape(-1, 8, sums.shape[1]), axis=1)
    d_low = (grad * ada[top, 1][None]).astype(BF)
    d_ada[top][1] = jnp.sum(grad * saved[top][-2].astype(F32), axis=0)
    d_biases[top][1] = jnp.sum(d_low.astype(F32), axis=0)
    for l in reversed(range(layer_count)):
        gamma1, gamma2, scale1, scale2, shift1, shift2 = [ada[l, i] for i in range(6)]
        (joined1, q_raw, k_raw, q_low, k_low, v_low, logs, attn, rest, branch, middle, joined2, act, slope, feed, state) = saved[l]
        (sums_pre, own, send), two, one = fc_back(
            d_low, sibling(d_low), blocks[l][2], blocks[l][1], slope, act, joined2
        )
        g_two = scatter_blocks(two, 1, z_size)
        g_one = scatter_blocks(one, 1, z_size)
        d_middle, d_low, sums = mix_back(
            own, sibling(send), middle, grad, branch, eight_rows(1.0 + scale2, gamma1)
        )
        d_ada[l][3], d_ada[l][5], d_ada[l][0], d_biases[l][0] = fold(sums)
        (sums_qkv, own, send), four_parts = attn_back(
            d_low, sibling(d_low), blocks[l][0], q_low, k_low, v_low, attn, rest, logs, q_raw, k_raw, joined1,
            eight_rows(scales[l]), place_col, end_row, head_width,
        )
        g_attn = scatter_blocks(four_parts, 4, z_size)
        before = max(l - 1, 0)
        grad, d_low, sums = mix_back(
            own, sibling(send), state, d_middle, saved[before][-2], eight_rows(1.0 + scale1, ada[before, 1])
        )
        sums = fold(sums)
        d_ada[l][2], d_ada[l][4] = sums[0], sums[1]
        if l > 0:
            d_ada[l - 1][1], d_biases[l - 1][1] = sums[2], sums[3]
        d_head = jnp.sum(sums_qkv[2].reshape(heads, head_width), axis=1)
        d_biases[l][2:] = sums_qkv[:2], fold(sums_pre)[0], d_head
        d_weights[l] = jnp.concatenate((g_attn, g_one, g_two), axis=0)

    def by_col(values):
        values = turned(values, y, values.ndim - 1)
        values = values.reshape(values.shape[:-1] + (z_size, x_size, d_col))
        return jnp.moveaxis(values, (-3, -2), (0, 1)).reshape(z_size, x_size, -1)

    def by_hidden(values):
        return jnp.swapaxes(turned(values, x, 0), 0, 1).reshape(z_size, x_size, -1)

    packs = [by_col(jnp.stack([jnp.stack(v) for v in d_ada]))]
    for l in range(layer_count):
        db_proj, db_fc2, db_qkv, db_fc1, d_head = d_biases[l]
        packs.append(by_col(db_proj))
        packs.append(by_col(db_fc2))
        packs.append(by_hidden(jnp.moveaxis(db_qkv.reshape(2, x_size, z_size, head_width), 0, 2)))
        packs.append(by_hidden(db_fc1.reshape(x_size, z_size, hid_core)))
        packs.append(by_hidden(d_head.reshape(x_size, z_size, 1)))
    lens = [p.shape[2] for p in packs]
    pack = jnp.concatenate(packs, axis=2)
    pack = jnp.broadcast_to(pack[None], (n_rows,) + pack.shape)
    got = lax.all_to_all(
        pack.reshape(n_rows * z_size * x_size, -1), ("y", "core", "z", "x"),
        split_axis=0, concat_axis=0, tiled=True,
    ).reshape(y_size, 2, z_size, x_size, -1)
    pos = lens[0]
    d_ada_all = jnp.sum(got[..., :pos], axis=1)
    d_ada_all = jnp.swapaxes(d_ada_all, 1, 2).reshape(seqs, -1).astype(BF)
    out_b_ada = jnp.sum(d_ada_all.astype(F32), axis=0).reshape(layer_count, 6, d_col)
    out_w_ada = dot(silu_own, d_ada_all, TN).reshape(rows_d, layer_count, 6, d_col)
    out_w_ada = jnp.swapaxes(out_w_ada, 0, 1)
    sums = jnp.sum(got[..., pos:], axis=(0, 2, 3))
    outs = [[] for _ in range(5)]
    pos = 0
    for l in range(layer_count):
        for i in range(5):
            count = lens[1 + 5 * l + i]
            outs[i].append(sums[:, pos : pos + count])
            pos += count
    out_b_proj = jnp.stack([v[0] + v[1] for v in outs[0]])
    out_b_fc2 = jnp.stack([v[0] + v[1] for v in outs[1]])
    out_b_qkv = jnp.stack(
        [jnp.swapaxes(v.reshape(2, 2, head_width), 0, 1).reshape(2, d_col) for v in outs[2]]
    )
    out_b_fc1 = jnp.stack([v.reshape(-1) for v in outs[3]])
    out_scale = jnp.stack([v.reshape(-1) for v in outs[4]])

    own = jnp.stack(d_weights)
    kept = jnp.where(core == 0, own[:, :, :rows_d], own[:, :, rows_d:])
    came = sibling(jnp.where(core == 0, own[:, :, rows_d:], own[:, :, :rows_d]))
    first = jnp.where(core == 0, kept, came).astype(F32)
    second = jnp.where(core == 0, came, kept).astype(F32)
    wq = jnp.stack((first[:, :three], second[:, :three]), axis=1)
    wq = wq.reshape(layer_count, 2, 3, head_width, rows_d)
    out_w_qkv = jnp.transpose(wq, (0, 4, 2, 1, 3)).reshape(layer_count, rows_d, 3, d_col)

    def pick(i, j):
        return jnp.concatenate((first[:, i:j], second[:, i:j]), axis=1)

    def given_back(values):
        return trade(turned(values[:rows_dev], y, 1))

    return (
        given_back(mixed), given_back(grad), out_w_ada, out_b_ada, out_w_qkv, out_b_qkv, out_scale,
        pick(three, four), out_b_proj, jnp.swapaxes(pick(cuts[1], cuts[2]), 1, 2), out_b_fc1,
        pick(cuts[2], cuts[3]), out_b_fc2,
    )


def solution(mesh):
    rows, cols = mesh.devices.shape
    row, col, body, used = ("row",), ("col",), on_device, mesh
    if rows == 4 and cols == 8:
        used = jax.sharding.Mesh(
            mesh.devices.reshape(rows // 2, 2, cols // 2, 2), ("y", "core", "z", "x")
        )
        row, col, body = ("y", "core"), ("z", "x"), on_pair
    tokens = P(row + col, None)
    out_weights = (
        P(None, row, None, col),
        P(None, None, col),
        P(None, row, None, col),
        P(None, None, col),
        P(None, col),
        P(None, col, row),
        P(None, col),
        P(None, row, col),
        P(None, col),
        P(None, col, row),
        P(None, col),
    )
    return jax.shard_map(
        body,
        mesh=used,
        in_specs=(tokens, P(row, None), P(row, None)) + out_weights + (tokens,),
        out_specs=(tokens, tokens) + out_weights,
        check_vma=False,
    )
```

```python
import jax
import jax.numpy as jnp
from jax import lax
from jax.experimental import pallas as pl
from jax.experimental.pallas import tpu as pltpu
from jax.sharding import PartitionSpec as P

HIGH = lax.Precision.HIGHEST
EPS_NORM = 1e-06
EPS_UNIT = 1e-06
NEG_FILL = -1e30


def block_ends(scale_sizes, seq_len):
    ends = jnp.cumsum(scale_sizes, axis=1)
    starts = ends - scale_sizes
    position = jnp.arange(seq_len, dtype=jnp.int32)
    picked = jnp.where(starts[:, None, :] <= position[None, :, None], scale_sizes[:, None, :], 0)
    return jnp.sum(picked, axis=2)


def normalize(values):
    center = jnp.mean(values, axis=-1, keepdims=True)
    spread = jnp.mean(values * values, axis=-1, keepdims=True) - center * center
    rstd = lax.rsqrt(spread + EPS_NORM)
    return ((values - center) * rstd, rstd)


def norm_back(grad_normed, normed, rstd):
    means = jnp.mean(grad_normed, axis=-1, keepdims=True)
    crosses = jnp.mean(grad_normed * normed, axis=-1, keepdims=True)
    return rstd * (grad_normed - means - normed * crosses)


def unit_pair(queries, key_rows, scale_here):
    q_norm = (
        queries
        * lax.rsqrt(jnp.sum(queries * queries, axis=-1, keepdims=True) + EPS_UNIT)
        * scale_here[:, None]
    )
    k_norm = key_rows * lax.rsqrt(jnp.sum(key_rows * key_rows, axis=-1, keepdims=True) + EPS_UNIT)
    return (q_norm, k_norm)


def project_in(hidden_low, weight):
    return (
        jnp.dot(
            lax.all_gather(hidden_low, "col", axis=0, tiled=True),
            weight,
            preferred_element_type=jnp.float32,
        ),
        hidden_low,
    )


def back_in(grad_three, kept, weight, whole_weight):
    tok_row = grad_three.shape[0]
    grad_low = grad_three.reshape(tok_row, grad_three.shape[1] * grad_three.shape[2])
    own_grads = lax.all_to_all(grad_three, "col", split_axis=0, concat_axis=2, tiled=True)
    grad_hidden = lax.dot_general(
        own_grads, whole_weight, (((1, 2), (1, 2)), ((), ())), preferred_element_type=jnp.float32
    )

    def add_piece(total, piece, start):
        return lax.dot_general(
            piece, grad_low, (((0,), (0,)), ((), ())), preferred_element_type=jnp.float32
        )

    init = jnp.zeros(weight.shape, jnp.float32)
    grad_weight = add_piece(init, lax.all_gather(kept, "col", axis=0, tiled=True), jnp.int32(0))
    return (grad_hidden, grad_weight)


def project_out(act_low, whole_weight):
    own_rows = lax.all_to_all(act_low, "col", split_axis=0, concat_axis=1, tiled=True)
    return jnp.dot(own_rows, whole_weight, preferred_element_type=jnp.float32)


def back_out(grad_low, act_low, weight):

    def add_piece(carry, piece, start):
        part = lax.dot_general(
            piece, weight, (((1,), (1,)), ((), ())), preferred_element_type=jnp.float32
        )
        grad_weight = lax.dot_general(
            act_low, piece, (((0,), (0,)), ((), ())), preferred_element_type=jnp.float32
        )
        return (part, grad_weight)

    init = (
        jnp.zeros((act_low.shape[0], weight.shape[0]), jnp.float32),
        jnp.zeros(weight.shape, jnp.float32),
    )
    return add_piece(init, lax.all_gather(grad_low, "col", axis=0, tiled=True), jnp.int32(0))


def masked_scores(q_rows, k_rows, ends):
    position = jnp.arange(k_rows.shape[0], dtype=jnp.int32)
    scores = jnp.einsum("the,she->hts", q_rows, k_rows, preferred_element_type=jnp.float32)
    visible = position[None, :] < ends[:, None]
    return jnp.where(visible[None], scores, NEG_FILL)


def attend(pieces):
    q_rows, k_rows, v_rows, ends = pieces
    scores = masked_scores(q_rows, k_rows, ends)
    top = jnp.max(scores, axis=-1, keepdims=True)
    expo = jnp.exp(scores - top)
    total = jnp.sum(expo, axis=-1, keepdims=True)
    probs = (expo / total).astype(jnp.bfloat16)
    attended = jnp.einsum("hts,she->the", probs, v_rows, preferred_element_type=jnp.float32)
    return (attended, (top + jnp.log(total))[..., 0])


def attend_back(pieces):
    q_rows, k_rows, v_rows, ends, log_total, grad_rows = pieces
    scores = masked_scores(q_rows, k_rows, ends)
    probs = jnp.exp(scores - log_total[..., None])
    grad_probs = jnp.einsum("the,she->hts", grad_rows, v_rows, preferred_element_type=jnp.float32)
    delta = jnp.sum(probs * grad_probs, axis=-1, keepdims=True)
    grad_scores = (probs * (grad_probs - delta)).astype(jnp.bfloat16)
    grad_q = jnp.einsum("hts,she->the", grad_scores, k_rows, preferred_element_type=jnp.float32)
    grad_k = jnp.einsum("hts,the->she", grad_scores, q_rows, preferred_element_type=jnp.float32)
    grad_v = jnp.einsum(
        "hts,the->she", probs.astype(jnp.bfloat16), grad_rows, preferred_element_type=jnp.float32
    )
    return (grad_q, grad_k, grad_v)


def gelu_tanh(values):
    return jax.nn.gelu(values, approximate=True)


def on_device(
    hidden_in,
    cond,
    scale_sizes,
    w_ada,
    b_ada,
    w_qkv,
    b_qkv,
    head_scale,
    w_proj,
    b_proj,
    w_fc1,
    b_fc1,
    w_fc2,
    b_fc2,
    grad_out,
):
    seq_row, width = cond.shape
    rows_dev = hidden_in.shape[0]
    tok_row = rows_dev * lax.axis_size("col")
    seq_len = tok_row // seq_row
    layer_count = w_ada.shape[0]
    d_col = b_qkv.shape[2]
    heads_dev = head_scale.shape[1]
    head_width = d_col // heads_dev
    full_ada, full_qkv, full_fc1, full_proj, full_fc2 = (
        lax.all_gather(w_ada, "row", axis=1, tiled=True),
        lax.all_gather(w_qkv, "row", axis=1, tiled=True),
        lax.all_gather(w_fc1, "row", axis=1, tiled=True),
        lax.all_gather(w_proj, "row", axis=2, tiled=True),
        lax.all_gather(w_fc2, "row", axis=2, tiled=True),
    )
    whole_proj, whole_fc2, whole_qkv, whole_fc1 = (
        lax.all_gather(full_proj, "col", axis=1, tiled=True),
        lax.all_gather(full_fc2, "col", axis=1, tiled=True),
        lax.all_gather(full_qkv, "col", axis=3, tiled=True),
        lax.all_gather(full_fc1, "col", axis=2, tiled=True),
    )
    ends = block_ends(scale_sizes, seq_len)
    silu_low = jax.nn.silu(cond.astype(jnp.float32)).astype(jnp.bfloat16)
    places = lax.axis_index("col") * rows_dev + jnp.arange(rows_dev, dtype=jnp.int32)
    member = (places[:, None] // seq_len == jnp.arange(seq_row, dtype=jnp.int32)[None, :]).astype(
        jnp.float32
    )

    def per_token(values):
        return jnp.dot(member, values, precision=HIGH)

    def per_sequence(values):
        return lax.dot_general(member, values, (((0,), (0,)), ((), ())), precision=HIGH)

    ada_parts = []
    for layer_index in range(layer_count):
        part = jnp.dot(
            silu_low,
            full_ada[layer_index].reshape(width, 6 * d_col),
            preferred_element_type=jnp.float32,
        )
        ada_parts.append(
            part.reshape(seq_row, 6, d_col) + b_ada[layer_index].astype(jnp.float32)[None]
        )
    ada_full, bias_proj_full, bias_fc2_full = (
        lax.all_gather(jnp.stack(ada_parts), "col", axis=3, tiled=True),
        lax.all_gather(b_proj.astype(jnp.float32), "col", axis=1, tiled=True),
        lax.all_gather(b_fc2.astype(jnp.float32), "col", axis=1, tiled=True),
    )
    current = hidden_in.astype(jnp.float32)
    saved = []
    for layer_index in range(layer_count):
        ada = ada_full[layer_index]
        gamma1, gamma2, scale1, scale2, shift1, shift2 = [
            per_token(ada[:, index]) for index in range(6)
        ]
        normed1, rstd1 = normalize(current)
        hidden1 = (normed1 * (1.0 + scale1) + shift1).astype(jnp.bfloat16)
        mixed_qkv, kept1 = project_in(hidden1, full_qkv[layer_index].reshape(width, 3 * d_col))
        bias_two = b_qkv[layer_index].astype(jnp.float32)
        bias_three = jnp.stack((bias_two[0], jnp.zeros_like(bias_two[0]), bias_two[1]))
        mixed_qkv = mixed_qkv + bias_three.reshape(1, 3 * d_col)
        split = mixed_qkv.reshape(seq_row, seq_len, 3, heads_dev, head_width)
        queries, key_rows, value_rows = (split[:, :, 0], split[:, :, 1], split[:, :, 2])
        scale_here = head_scale[layer_index].astype(jnp.float32)
        q_norm, k_norm = unit_pair(queries, key_rows, scale_here)
        q_low = q_norm.astype(jnp.bfloat16)
        k_low = k_norm.astype(jnp.bfloat16)
        v_low = value_rows.astype(jnp.bfloat16)
        attended, log_total = lax.map(attend, (q_low, k_low, v_low, ends))
        attn_low = attended.reshape(tok_row, d_col).astype(jnp.bfloat16)
        branch = project_out(attn_low, whole_proj[layer_index]) + bias_proj_full[layer_index][None]
        middle = current + gamma1 * branch
        normed2, rstd2 = normalize(middle)
        hidden2 = (normed2 * (1.0 + scale2) + shift2).astype(jnp.bfloat16)
        pre_act, kept2 = project_in(hidden2, full_fc1[layer_index])
        pre_act = pre_act + b_fc1[layer_index].astype(jnp.float32)[None]
        act_low = gelu_tanh(pre_act).astype(jnp.bfloat16)
        feed = project_out(act_low, whole_fc2[layer_index]) + bias_fc2_full[layer_index][None]
        saved.append(
            (
                normed1,
                rstd1,
                kept1,
                queries,
                key_rows,
                scale_here,
                q_low,
                k_low,
                v_low,
                log_total,
                attn_low,
                branch,
                normed2,
                rstd2,
                kept2,
                pre_act,
                act_low,
                feed,
            )
        )
        current = middle + gamma2 * feed
    mixed = current.astype(jnp.bfloat16)
    grad_state = grad_out.astype(jnp.float32)
    grads_ada = [None] * layer_count
    grads_w_qkv = [None] * layer_count
    grads_b_qkv = [None] * layer_count
    grads_scale = [None] * layer_count
    grads_w_proj = [None] * layer_count
    grads_b_proj = [None] * layer_count
    grads_w_fc1 = [None] * layer_count
    grads_b_fc1 = [None] * layer_count
    grads_w_fc2 = [None] * layer_count
    grads_b_fc2 = [None] * layer_count
    for layer_index in reversed(range(layer_count)):
        (
            normed1,
            rstd1,
            kept1,
            queries,
            key_rows,
            scale_here,
            q_low,
            k_low,
            v_low,
            log_total,
            attn_low,
            branch,
            normed2,
            rstd2,
            kept2,
            pre_act,
            act_low,
            feed,
        ) = saved[layer_index]
        ada = ada_full[layer_index]
        gamma1, gamma2, scale1, scale2, shift1, shift2 = [
            per_token(ada[:, index]) for index in range(6)
        ]
        d_gamma2 = per_sequence(grad_state * feed)
        grad_feed = (grad_state * gamma2).astype(jnp.bfloat16)
        grads_b_fc2[layer_index] = jnp.sum(grad_feed.astype(jnp.float32), axis=0)
        grad_act, grads_w_fc2[layer_index] = back_out(grad_feed, act_low, full_fc2[layer_index])
        gelu_pull = jax.vjp(gelu_tanh, pre_act)[1]
        grad_pre = gelu_pull(grad_act)[0].astype(jnp.bfloat16)
        grads_b_fc1[layer_index] = jnp.sum(grad_pre.astype(jnp.float32), axis=0)
        whole_one = whole_fc1[layer_index].reshape(width, 1, whole_fc1.shape[2])
        grad_hidden2, grads_w_fc1[layer_index] = back_in(
            grad_pre.reshape(tok_row, 1, grad_pre.shape[1]), kept2, full_fc1[layer_index], whole_one
        )
        d_scale2 = per_sequence(grad_hidden2 * normed2)
        d_shift2 = per_sequence(grad_hidden2)
        grad_middle = grad_state + norm_back(grad_hidden2 * (1.0 + scale2), normed2, rstd2)
        d_gamma1 = per_sequence(grad_middle * branch)
        grad_branch = (grad_middle * gamma1).astype(jnp.bfloat16)
        grads_b_proj[layer_index] = jnp.sum(grad_branch.astype(jnp.float32), axis=0)
        grad_attn, grads_w_proj[layer_index] = back_out(
            grad_branch, attn_low, full_proj[layer_index]
        )
        grad_attn_low = grad_attn.astype(jnp.bfloat16).reshape(
            seq_row, seq_len, heads_dev, head_width
        )
        grad_qn, grad_kn, grad_v = lax.map(
            attend_back, (q_low, k_low, v_low, ends, log_total, grad_attn_low)
        )
        unit_pull = jax.vjp(unit_pair, queries, key_rows, scale_here)[1]
        grad_q, grad_k, grads_scale[layer_index] = unit_pull((grad_qn, grad_kn))
        grad_qkv = (
            jnp.stack((grad_q, grad_k, grad_v), axis=2)
            .reshape(tok_row, 3, d_col)
            .astype(jnp.bfloat16)
        )
        bias_sums = jnp.sum(grad_qkv.astype(jnp.float32), axis=0)
        grads_b_qkv[layer_index] = jnp.stack((bias_sums[0], bias_sums[2]))
        grad_hidden1, weight_qkv = back_in(
            grad_qkv, kept1, full_qkv[layer_index].reshape(width, 3 * d_col), whole_qkv[layer_index]
        )
        grads_w_qkv[layer_index] = weight_qkv.reshape(width, 3, d_col)
        d_scale1 = per_sequence(grad_hidden1 * normed1)
        d_shift1 = per_sequence(grad_hidden1)
        grad_state = grad_middle + norm_back(grad_hidden1 * (1.0 + scale1), normed1, rstd1)
        grads_ada[layer_index] = jnp.stack(
            (d_gamma1, d_gamma2, d_scale1, d_scale2, d_shift1, d_shift2), axis=1
        )
    ada_sums, bias_proj_col, bias_fc2_col = (
        lax.psum_scatter(
            jnp.stack(grads_ada).astype(jnp.bfloat16), "col", scatter_dimension=3, tiled=True
        ).astype(jnp.float32),
        lax.psum_scatter(
            jnp.stack(grads_b_proj).astype(jnp.bfloat16), "col", scatter_dimension=1, tiled=True
        ).astype(jnp.float32),
        lax.psum_scatter(
            jnp.stack(grads_b_fc2).astype(jnp.bfloat16), "col", scatter_dimension=1, tiled=True
        ).astype(jnp.float32),
    )
    grad_ada = ada_sums.astype(jnp.bfloat16)
    weights_ada = []
    for layer_index in range(layer_count):
        weight_ada = lax.dot_general(
            silu_low,
            grad_ada[layer_index].reshape(seq_row, 6 * d_col),
            (((0,), (0,)), ((), ())),
            preferred_element_type=jnp.float32,
        )
        weights_ada.append(weight_ada.reshape(width, 6, d_col))
    bias_ada_local = jnp.sum(grad_ada.astype(jnp.float32), axis=1)
    sum_ada, sum_qkv, sum_fc1, sum_proj, sum_fc2 = (
        lax.psum_scatter(
            jnp.stack(weights_ada).astype(jnp.bfloat16), "row", scatter_dimension=1, tiled=True
        ).astype(jnp.float32),
        lax.psum_scatter(
            jnp.stack(grads_w_qkv).astype(jnp.bfloat16), "row", scatter_dimension=1, tiled=True
        ).astype(jnp.float32),
        lax.psum_scatter(
            jnp.stack(grads_w_fc1).astype(jnp.bfloat16), "row", scatter_dimension=1, tiled=True
        ).astype(jnp.float32),
        lax.psum_scatter(
            jnp.stack(grads_w_proj).astype(jnp.bfloat16), "row", scatter_dimension=2, tiled=True
        ).astype(jnp.float32),
        lax.psum_scatter(
            jnp.stack(grads_w_fc2).astype(jnp.bfloat16), "row", scatter_dimension=2, tiled=True
        ).astype(jnp.float32),
    )
    bias_ada, bias_qkv, scale_grad, bias_proj, bias_fc1, bias_fc2 = lax.psum(
        (
            bias_ada_local,
            jnp.stack(grads_b_qkv),
            jnp.stack(grads_scale),
            bias_proj_col,
            jnp.stack(grads_b_fc1),
            bias_fc2_col,
        ),
        "row",
    )
    return (
        mixed,
        grad_state,
        sum_ada,
        bias_ada,
        sum_qkv,
        bias_qkv,
        scale_grad,
        sum_proj,
        bias_proj,
        sum_fc1,
        bias_fc1,
        sum_fc2,
        bias_fc2,
    )


BF = jnp.bfloat16
F32 = jnp.float32
NN = (((1,), (0,)), ((), ()))
NT = (((1,), (1,)), ((), ()))
TN = (((0,), (0,)), ((), ()))
VMEM_BYTES = 60 * 1024 * 1024


def sibling(values):
    return lax.ppermute(values, "core", [(0, 1), (1, 0)])


def across(values, axis):
    return lax.ppermute(values, axis, [(0, 1), (1, 0)])


def trade(values, moves):
    return jnp.where(moves, lax.ppermute(values, ("core", "x"), [(1, 2), (2, 1)]), values)


def turned(values, flag, axis):
    half = values.shape[axis] // 2
    return jnp.where(flag == 1, jnp.roll(values, half, axis), values)


def dot(left, right, dims=NN):
    return lax.dot_general(left, right, dims, preferred_element_type=F32)


def shape_of(dims, kind):
    return jax.ShapeDtypeStruct(dims, kind)


def call(body, grid, in_specs, out_specs, out_shape, scratch, flops, moved, args):
    return pl.pallas_call(
        body,
        grid=grid,
        in_specs=in_specs,
        out_specs=out_specs,
        out_shape=out_shape,
        scratch_shapes=scratch,
        compiler_params=pltpu.CompilerParams(
            dimension_semantics=("arbitrary",) * len(grid), vmem_limit_bytes=VMEM_BYTES
        ),
        cost_estimate=pl.CostEstimate(flops=flops // 64, bytes_accessed=moved // 64, transcendentals=0),
    )(*args)


def fixed(dims):
    return pl.BlockSpec(dims, lambda *_: (0,) * len(dims))


def row_loop(total, size, body, unroll=1):
    @pl.loop(0, total // size, unroll=unroll)
    def _(step):
        body(pl.ds(pl.multiple_of(step * size, size), size))


def early(dims, row=0):
    return pl.BlockSpec(dims, lambda t: (row + jnp.minimum(t, 1), 0))


def late(dims, row=0):
    return pl.BlockSpec(dims, lambda t: (row + jnp.maximum(t - 2, 0), 0))


def weight_specs(low, blocks=None):
    if blocks is not None and blocks[0].ndim == 4:
        shape = (2, None, low // 2, low)

        def spec(block, first):
            pick = (lambda t: jnp.minimum(t, 1)) if first else (lambda t: jnp.maximum(t - 2, 0))
            return pl.BlockSpec(shape, lambda t: (pick(t), block, 0, 0))

        return [spec(0, True), spec(2, False), spec(1, True), spec(3, False)]
    return [early((low, low)), late((low, low)), early((low, low)), late((low, low))]


def matrix(ref):
    value = ref[...]
    return value.reshape(-1, value.shape[-1])


def with_tile(step, refs, body):
    g, gx, gy, gd = refs

    @pl.when(step < 2)
    def _():
        body(g, gy)

    @pl.when(step >= 2)
    def _():
        body(gx, gd)


def join_into(joined, own, other):
    rows = own.shape[0]
    joined[:rows, :] = own[...]
    joined[rows:, :] = other[...]


def fc_up(own, other, blocks, bias):
    rows, width = own.shape
    low, both = width // 2, 2 * rows
    hid = 4 * low

    def body(own_ref, other_ref, g, gx, gy, gd, bias_ref, joined, act, slope):
        step = pl.program_id(0)

        @pl.when(step == 0)
        def _():
            join_into(joined, own_ref, other_ref)

        def product(first, second):
            for lanes in (slice(0, low // 2), slice(low // 2, low)):
                for sl in (slice(0, rows), slice(rows, both)):
                    pre = dot(joined[sl, :low], first[lanes, :], NT)
                    pre = pre + dot(joined[sl, low:], second[lanes, :], NT) + bias_ref[:, lanes]
                    root = 0.7978845608028654
                    square = pre * pre
                    tanh = jnp.tanh(pre * (root + (root * 0.044715) * square))
                    half = 0.5 + 0.5 * tanh
                    act[sl, lanes] = (pre * half).astype(BF)
                    inner = pre * ((0.5 * root) + (1.5 * 0.044715 * root) * square)
                    slope[sl, lanes] = (half + (1.0 - tanh * tanh) * inner).astype(BF)

        with_tile(step, (g, gx, gy, gd), product)

    return call(
        body,
        (4,),
        [fixed((rows, width))] * 2 + weight_specs(low) + [pl.BlockSpec((1, low), lambda t: (0, t))],
        [fixed((both, width))] + [pl.BlockSpec((both, low), lambda t: (0, t))] * 2,
        [shape_of((both, width), BF), shape_of((both, hid), BF), shape_of((both, hid), BF)],
        [],
        2 * both * width * hid,
        2 * hid * width + 6 * both * width + 4 * both * hid,
        (own, other, *blocks, bias),
    )


def fc_back(own, other, up_blocks, down_blocks, slope, act, hidden, by_z):
    rows, width = own.shape
    low, both = width // 2, 2 * rows
    hid = 4 * low

    def body(own_ref, other_ref, ug, ugx, ugy, ugd, dg, dgx, dgy, dgd, slope_ref, act_ref, hid_ref,
             sums, out_own, out_other, *rest):
        two_refs, one_refs, (joined, grad, acc) = rest[: -7], rest[-7:-3], rest[-3:]
        step = pl.program_id(0)

        @pl.when(step == 0)
        def _():
            join_into(joined, own_ref, other_ref)

        def product(up_one, up_two, down_one, down_two, first, last, near, far):
            for i, sl in enumerate((slice(rows, both), slice(0, rows))):
                value = dot(joined[sl, :low], matrix(up_one), NT) + dot(joined[sl, low:], matrix(up_two), NT)
                value = (value * slope_ref[sl, :].astype(F32)).astype(BF)
                grad[sl, :] = value
                total = jnp.sum(value.astype(F32).reshape(rows // 8, 8, low), axis=0)
                sums[...] = total if i == 0 else sums[...] + total
                for lanes, down in ((slice(0, low), down_one), (slice(low, width), down_two)):
                    part = dot(value, matrix(down))
                    if not first:
                        part = part + acc[sl, lanes]
                    if not last:
                        acc[sl, lanes] = part
                    elif i == 0:
                        out_other[:, lanes] = part.astype(BF)
                    else:
                        out_own[:, lanes] = part
            for refs, left, right in ((two_refs, act_ref, joined), (one_refs, grad, hid_ref)):
                for j, lanes in ((near, slice(0, low)), (far, slice(low, width))):
                    value = dot(left[...], right[:, lanes], TN).astype(BF)
                    if len(refs) == 1:
                        refs[0][:, j // 2] = value.reshape(2, low // 2, low)
                    else:
                        refs[j][...] = value

        @pl.when(step == 0)
        def _():
            product(ug, ugy, dg, dgy, True, False, 0, 2)

        @pl.when(step == 1)
        def _():
            product(ug, ugy, dg, dgy, False, False, 0, 2)

        @pl.when(step == 2)
        def _():
            product(ugx, ugd, dgx, dgd, False, False, 1, 3)

        @pl.when(step == 3)
        def _():
            product(ugx, ugd, dgx, dgd, False, True, 1, 3)

    tiles = pl.BlockSpec((both, low), lambda t: (0, t))
    whole = shape_of((2 * low, low), BF)
    z_specs = [pl.BlockSpec((2, 2, low // 2, low), lambda t: (t % 2, t // 2, 0, 0))]
    found = call(
        body,
        (4,),
        [fixed((rows, width))] * 2 + weight_specs(low, up_blocks) + weight_specs(low, down_blocks) + [tiles, tiles, fixed((both, width))],
        [pl.BlockSpec((8, low), lambda t: (0, t)), fixed((rows, width)), fixed((rows, width))]
        + (z_specs if by_z else weight_specs(low)) + weight_specs(low),
        [shape_of((8, hid), F32), shape_of((rows, width), F32), shape_of((rows, width), BF)]
        + ([shape_of((4, 4, low // 2, low), BF)] if by_z else [whole] * 4) + [whole] * 4,
        [pltpu.VMEM((both, width), BF), pltpu.VMEM((both, low), BF), pltpu.VMEM((both, width), F32)],
        8 * both * width * hid,
        8 * hid * width + 6 * both * width + 4 * both * hid + 6 * rows * width,
        (own, other, *up_blocks, *down_blocks, slope, act, hidden),
    )
    return found[:3], found[3:-4], found[-4:]


def fc_down(left, blocks):
    both, hid = left.shape
    rows, low = both // 2, hid // 4
    width = 2 * low

    def body(left_ref, g, gx, gy, gd, own, other, acc):
        step = pl.program_id(0)

        def product(one, two, first, last):
            for i, sl in enumerate((slice(rows, both), slice(0, rows))):
                for lanes, right in ((slice(0, low), one), (slice(low, width), two)):
                    part = dot(left_ref[sl, :], matrix(right))
                    if not first:
                        part = part + acc[sl, lanes]
                    if not last:
                        acc[sl, lanes] = part
                    elif i == 0:
                        other[:, lanes] = part.astype(BF)
                    else:
                        own[:, lanes] = part

        @pl.when(step == 0)
        def _():
            product(g, gy, True, False)

        @pl.when(step == 1)
        def _():
            product(g, gy, False, False)

        @pl.when(step == 2)
        def _():
            product(gx, gd, False, False)

        @pl.when(step == 3)
        def _():
            product(gx, gd, False, True)

    return call(
        body,
        (4,),
        [pl.BlockSpec((both, low), lambda t: (0, t))] + weight_specs(low, blocks),
        [fixed((rows, width))] * 2,
        [shape_of((rows, width), F32), shape_of((rows, width), BF)],
        [pltpu.VMEM((both, width), F32)],
        2 * both * width * hid,
        2 * hid * width + 2 * both * hid + 6 * rows * width,
        (left, *blocks),
    )


def head_ones(size, head_width):
    first = lax.broadcasted_iota(jnp.int32, (size, size), 0) // head_width
    second = lax.broadcasted_iota(jnp.int32, (size, size), 1) // head_width
    return (first == second).astype(BF)


def qkv_up(own, other, blocks, vectors, ones):
    rows, width = own.shape
    low, both = width // 2, 2 * rows
    tile = low // 2

    def body(own_ref, other_ref, g, gx, gy, gd, vec, ones_ref, joined, q_raw, k_raw, q_low, k_low, v_low, acc):
        step = pl.program_id(0)
        part = step % 3

        @pl.when(step == 0)
        def _():
            join_into(joined, own_ref, other_ref)

        def product(first, second):
            acc[...] = dot(joined[:, :low], first, NT) + dot(joined[:, low:], second, NT)

        @pl.when(step < 3)
        def _():
            product(g[...], gy[...])

        @pl.when(step >= 3)
        def _():
            product(gx[...], gd[...])

        def unit(value):
            square = dot((value * value).astype(BF), ones_ref[...])
            return value * lax.rsqrt(square + EPS_UNIT)

        @pl.when(part == 0)
        def _():
            def finish(sl):
                value = acc[sl, :] + vec[0:1, :]
                q_raw[sl, :] = value.astype(BF)
                q_low[sl, :] = (unit(value) * vec[2:3, :]).astype(BF)

            row_loop(both, both // 4, finish)

        @pl.when(part == 1)
        def _():
            def finish(sl):
                value = acc[sl, :]
                k_raw[sl, :] = value.astype(BF)
                k_low[sl, :] = unit(value).astype(BF)

            row_loop(both, both // 4, finish)

        @pl.when(part == 2)
        def _():
            v_low[...] = (acc[...] + vec[1:2, :]).astype(BF)

    half = lambda t: t // 3
    kept = pl.BlockSpec((both, tile), lambda t: (0, half(t)))
    heads = shape_of((both, low), BF)
    return call(
        body,
        (6,),
        [fixed((rows, width))] * 2
        + [
            pl.BlockSpec((tile, low), lambda t: (jnp.minimum(t, 2), 0)),
            pl.BlockSpec((tile, low), lambda t: (jnp.maximum(t - 3, 0), 0)),
            pl.BlockSpec((tile, low), lambda t: (jnp.minimum(t, 2), 0)),
            pl.BlockSpec((tile, low), lambda t: (jnp.maximum(t - 3, 0), 0)),
            pl.BlockSpec((8, tile), lambda t: (0, half(t))),
            fixed((tile, tile)),
        ],
        [fixed((both, width))] + [kept] * 5,
        [shape_of((both, width), BF)] + [heads] * 5,
        [pltpu.VMEM((both, tile), F32)],
        2 * both * width * 3 * low,
        2 * 3 * low * width + 6 * both * width + 10 * both * low,
        (own, other, *blocks, vectors, ones),
    )


def attn_mix(q_low, k_low, v_low, end_col, place_row, head_width):
    both, low = q_low.shape
    pair = 2 * head_width
    chunk = both // 4

    def body(q_ref, k_ref, v_ref, end_ref, place_ref, out_ref, rest_ref, log_ref):
        place = place_ref[0:1, :]
        lane = lax.broadcasted_iota(jnp.int32, (both, pair), 1)
        value = v_ref[...]
        ones = jnp.ones_like(value)
        wide = [
            jnp.concatenate((jnp.where(lane // head_width == h, value, ones), ones), axis=1) for h in range(2)
        ]
        first = lane[:chunk] < head_width
        for c in range(4):
            sl = slice(c * chunk, (c + 1) * chunk)
            queries = q_ref[sl, :]
            found = []
            for h in range(2):
                own = jnp.where(first if h == 0 else ~first, queries, jnp.zeros_like(queries))
                scores = dot(own, k_ref[...], NT)
                expo = jnp.where(place < end_ref[sl, :], jnp.exp(scores), 0.0).astype(BF)
                found.append(dot(expo, wide[h]))
            out = jnp.where(first, found[0][:, :pair] / found[0][:, pair:], found[1][:, :pair] / found[1][:, pair:])
            low_out = out.astype(BF)
            out_ref[sl, :] = low_out
            rest_ref[sl, :] = (out - low_out.astype(F32)).astype(BF)
            log_ref[sl, :] = jnp.log(jnp.where(first, found[1][:, pair:], found[0][:, pair:]))

    block = pl.BlockSpec((both, pair), lambda t: (0, t))
    return call(
        body,
        (low // pair,),
        [block] * 3 + [fixed((both, 1)), fixed((8, both))],
        [block] * 3,
        [shape_of((both, low), BF)] * 2 + [shape_of((both, low), F32)],
        [],
        4 * both * both * low,
        14 * both * low,
        (q_low, k_low, v_low, end_col, place_row),
    )


def attn_back(own, other, blocks, q_low, k_low, v_low, attn, rest, logs, q_raw, k_raw, hidden, scale_row,
              place_col, end_row, head_width):
    rows, width = own.shape
    both, low = q_low.shape
    pair = 2 * head_width
    chunk = both // 4
    steps = low // pair

    def body(own_ref, other_ref, *refs):
        w_refs, refs = refs[:16], refs[16:]
        (q_ref, k_ref, v_ref, attn_ref, rest_ref, log_ref, qr_ref, kr_ref, hid_ref, scale_ref, place_ref, end_ref,
         sums, out_own, out_other, keep, by_x, by_y, far, joined, weights, ds_ref, three_ref, acc) = refs
        step = pl.program_id(0)

        @pl.when(step == 0)
        def _():
            join_into(joined, own_ref, other_ref)

        for side, when in ((0, step < 2), (1, step >= 2)):
            @pl.when(when)
            def _():
                for i in range(4):
                    rows_i = slice(i * pair, (i + 1) * pair)
                    weights[rows_i, :low] = w_refs[4 * i + 2 * side][...]
                    weights[rows_i, low:] = w_refs[4 * i + 2 * side + 1][...]

        grad = dot(joined[...], weights[3 * pair :, :], NT).astype(BF)
        ends = end_ref[0:1, :]
        lane = lax.broadcasted_iota(jnp.int32, (both, pair), 1)
        inner = lane % head_width
        row_head = lax.broadcasted_iota(jnp.int32, (pair, pair), 0) // head_width
        lane_head = lax.broadcasted_iota(jnp.int32, (pair, pair), 1) // head_width
        same = (row_head == lane_head).astype(BF)
        swap = (row_head != lane_head).astype(BF)
        swap_twice = jnp.concatenate((swap, swap), axis=0)

        def spread(value):
            high = value.astype(BF)
            left = value - high.astype(F32)
            mid = left.astype(BF)
            small = (left - mid.astype(F32)).astype(BF)
            zero = jnp.zeros_like(high)
            return jnp.where(inner == 0, high, jnp.where(inner == 1, mid, jnp.where(inner == 2, small, zero)))

        def unit_back(raw, grad_unit):
            raw = raw.astype(F32)
            rate = lax.rsqrt(dot((raw * raw).astype(BF), same) + EPS_UNIT)
            unit = raw * rate
            cross = dot((grad_unit * unit).astype(BF), same)
            return rate * (grad_unit - unit * cross), unit

        product = grad.astype(F32) * (attn_ref[...].astype(F32) + rest_ref[...].astype(F32))
        high = product.astype(BF)
        small = (product - high.astype(F32)).astype(BF)
        delta = dot(jnp.concatenate((high, small), axis=1), swap_twice)
        log_terms, delta_terms = spread(-log_ref[...]), spread(-delta)
        queries, keys, values = q_ref[...], k_ref[...], v_ref[...]
        zero, one = jnp.zeros_like(keys), jnp.ones_like(keys)
        dk_parts, dv_parts = [None] * 4, [None] * 4
        d_qt = None
        for h in range(2):
            mine = lane // head_width == h
            q_own, g_own, k_own = [jnp.where(mine, v, zero) for v in (queries, grad, keys)]
            q_wide, g_wide = jnp.where(mine, queries, log_terms), jnp.where(mine, grad, delta_terms)
            k_wide, v_wide = jnp.where(mine, keys, one), jnp.where(mine, values, one)
            for c in range(4):
                sl = slice(c * chunk, (c + 1) * chunk)
                scores = dot(k_wide[sl], q_wide, NT)
                probs = jnp.where(place_ref[sl, :] < ends, jnp.exp(scores), 0.0)
                d_scores = (probs * dot(v_wide[sl], g_wide, NT)).astype(BF)
                ds_ref[sl, :] = d_scores
                d_v, d_k = dot(probs.astype(BF), g_own), dot(d_scores, q_own)
                dv_parts[c] = d_v if h == 0 else dv_parts[c] + d_v
                dk_parts[c] = d_k if h == 0 else dk_parts[c] + d_k
            part = dot(k_own, ds_ref[...], TN)
            d_qt = part if h == 0 else d_qt + part
        d_qn = d_qt.T
        d_q, unit_q = unit_back(qr_ref[...], d_qn * scale_ref[0:1, :])
        d_k, _ = unit_back(kr_ref[...], jnp.concatenate(dk_parts, axis=0))
        d_q, d_k, d_v = d_q.astype(BF), d_k.astype(BF), jnp.concatenate(dv_parts, axis=0).astype(BF)
        for i, value in enumerate((d_q, d_k, d_v)):
            three_ref[:, i * pair : (i + 1) * pair] = value
        for i, value in enumerate((d_q.astype(F32), d_v.astype(F32), d_qn * unit_q)):
            sums[i : i + 1, :] = jnp.sum(value, axis=0, keepdims=True)

        for lanes in (slice(0, low), slice(low, width)):
            part = dot(three_ref[...], weights[: 3 * pair, lanes])

            @pl.when(step == 0)
            def _():
                acc[:, lanes] = part

            @pl.when(jnp.logical_and(step > 0, step < steps - 1))
            def _():
                acc[:, lanes] += part

            @pl.when(step == steps - 1)
            def _():
                total = acc[:, lanes] + part
                out_own[:, lanes] = total[:rows]
                out_other[:, lanes] = total[rows:].astype(BF)

        for i, lanes in enumerate((slice(0, low), slice(low, width))):
            three = dot(three_ref[...], hid_ref[:, lanes], TN).astype(BF)
            proj = dot(attn_ref[...], joined[:, lanes], TN).astype(BF)
            grads = [three[j * pair : (j + 1) * pair] for j in range(3)] + [proj]

            @pl.when(step < 2)
            def _():
                for j in range(4):
                    (keep, by_y)[i][j, 0] = grads[j]

            @pl.when(step >= 2)
            def _():
                for j in range(4):
                    (by_x, far)[i][j, 0] = grads[j]

    g, gx, gy, gd = blocks
    w_specs, w_args = [], []
    for i in range(4):
        w_specs += [f((pair, low), 2 * i) for f in (early, early, late, late)]
        w_args += [g, gy, gx, gd]
    block = pl.BlockSpec((both, pair), lambda t: (0, t))
    row = pl.BlockSpec((8, pair), lambda t: (0, t))
    first = pl.BlockSpec((4, 1, pair, low), lambda t: (0, jnp.minimum(t, 1), 0, 0))
    second = pl.BlockSpec((4, 1, pair, low), lambda t: (0, jnp.maximum(t - 2, 0), 0, 0))
    found = call(
        body,
        (steps,),
        [fixed((rows, width))] * 2 + w_specs + [block] * 8
        + [fixed((both, width)), row, fixed((both, 1)), fixed((8, both))],
        [row, fixed((rows, width)), fixed((rows, width)), first, second, first, second],
        [shape_of((8, low), F32), shape_of((rows, width), F32), shape_of((rows, width), BF)]
        + [shape_of((4, 2, pair, low), BF)] * 4,
        [
            pltpu.VMEM((both, width), BF), pltpu.VMEM((4 * pair, width), BF), pltpu.VMEM((both, both), BF),
            pltpu.VMEM((both, 3 * pair), BF), pltpu.VMEM((both, width), F32),
        ],
        10 * both * both * low + 16 * both * width * low,
        24 * both * low + 8 * both * width,
        (own, other, *w_args, q_low, k_low, v_low, attn, rest, logs, q_raw, k_raw, hidden, scale_row,
         place_col, end_row),
    )
    return found[:3], found[3:]


def attn_down(attn, blocks):
    both, low = attn.shape
    rows, width, tile = both // 2, 2 * low, low // 2

    def body(attn_ref, g, gx, gy, gd, own, other):
        for lanes, first, second in ((slice(0, low), g, gx), (slice(low, width), gy, gd)):
            value = dot(attn_ref[:, :tile], first[...]) + dot(attn_ref[:, tile:], second[...])
            own[:, lanes] = value[:rows]
            other[:, lanes] = value[rows:].astype(BF)

    last = pl.BlockSpec((tile, low), lambda t: (3, 0))
    return call(
        body,
        (1,),
        [fixed((both, low))] + [last] * 4,
        [fixed((rows, width))] * 2,
        [shape_of((rows, width), F32), shape_of((rows, width), BF)],
        [],
        2 * both * width * low,
        2 * low * width + 2 * both * low + 6 * rows * width,
        (attn, *blocks),
    )


def mix(own, got, state, vectors, last):
    rows, width = own.shape
    part = rows // 2

    def body(own_ref, got_ref, state_ref, vec, branch_ref, next_ref, hid_ref):
        def one(sl):
            branch = own_ref[sl, :] + got_ref[sl, :].astype(F32) + vec[0:1, :]
            branch_ref[sl, :] = branch.astype(BF)
            value = state_ref[sl, :] + vec[1:2, :] * branch
            next_ref[sl, :] = value
            if last:
                hid_ref[sl, :] = value.astype(BF)
            else:
                mean = jnp.mean(value, axis=1, keepdims=True)
                spread = jnp.mean(value * value, axis=1, keepdims=True) - mean * mean
                normed = (value - mean) * lax.rsqrt(spread + EPS_NORM)
                hid_ref[sl, :] = (normed * vec[2:3, :] + vec[3:4, :]).astype(BF)

        row_loop(part, 16, one, unroll=11)

    block = pl.BlockSpec((part, width), lambda t: (t, 0))
    return call(
        body,
        (2,),
        [block] * 3 + [fixed((8, width))],
        [block] * 3,
        [shape_of((rows, width), BF), shape_of((rows, width), F32), shape_of((rows, width), BF)],
        [],
        20 * rows * width,
        18 * rows * width,
        (own, got, state, vectors),
    )


def mix_back(own, got, state, grad, branch, vectors):
    rows, width = own.shape
    part = rows // 2

    def body(own_ref, got_ref, state_ref, grad_ref, branch_ref, vec, next_ref, low_ref, sums):
        @pl.when(pl.program_id(0) == 0)
        def _():
            sums[...] = jnp.zeros_like(sums)

        def add(i, value):
            sums[8 * i : 8 * i + 8, :] += value[:8] + value[8:]

        def one(sl):
            d_hid = own_ref[sl, :] + got_ref[sl, :].astype(F32)
            value = state_ref[sl, :]
            mean = jnp.mean(value, axis=1, keepdims=True)
            spread = jnp.mean(value * value, axis=1, keepdims=True) - mean * mean
            rate = lax.rsqrt(spread + EPS_NORM)
            normed = (value - mean) * rate
            add(0, d_hid * normed)
            add(1, d_hid)
            d_norm = d_hid * vec[0:1, :]
            means = jnp.mean(d_norm, axis=1, keepdims=True)
            crosses = jnp.mean(d_norm * normed, axis=1, keepdims=True)
            total = grad_ref[sl, :] + rate * (d_norm - means - normed * crosses)
            next_ref[sl, :] = total
            add(2, total * branch_ref[sl, :].astype(F32))
            low = (total * vec[1:2, :]).astype(BF)
            low_ref[sl, :] = low
            add(3, low.astype(F32))

        row_loop(part, 16, one, unroll=11)

    block = pl.BlockSpec((part, width), lambda t: (t, 0))
    return call(
        body,
        (2,),
        [block] * 5 + [fixed((8, width))],
        [block] * 2 + [fixed((32, width))],
        [shape_of((rows, width), F32), shape_of((rows, width), BF), shape_of((32, width), F32)],
        [],
        30 * rows * width,
        20 * rows * width,
        (own, got, state, grad, branch, vectors),
    )


def tie(value, *others):
    return lax.optimization_barrier((value,) + others)[0]


def add_low(*values):
    return sum(v.astype(F32) for v in values).astype(BF)


def flat(blocks):
    return [v.reshape(-1, v.shape[-1]) for v in blocks]


def near_parts(blocks, got_a, got_b):
    _, near_x, near_y, _ = blocks
    half, low = got_a.shape

    def body(x_ref, y_ref, a_ref, b_ref, x_out, y_out):
        x_out[...] = (x_ref[...].astype(F32) + a_ref[...].astype(F32)).astype(BF)
        y_out[...] = (y_ref[...].astype(F32) + b_ref[...].astype(F32)).astype(BF)

    front = pl.BlockSpec((half, low), lambda t: (0, 0))
    back = pl.BlockSpec((half, low), lambda t: (1, 0))
    return pl.pallas_call(
        body,
        grid=(1,),
        in_specs=[front, back, front, front],
        out_specs=[front, back],
        out_shape=[shape_of(near_x.shape, BF), shape_of(near_y.shape, BF)],
        input_output_aliases={0: 0, 1: 1},
        compiler_params=pltpu.CompilerParams(vmem_limit_bytes=VMEM_BYTES),
        cost_estimate=pl.CostEstimate(flops=2 * half * low, bytes_accessed=12 * half * low, transcendentals=0),
    )(near_x, near_y, got_a, got_b)


def settle(keep, got_x, got_y, parts, z_size):
    total = add_low(keep, got_x, got_y)
    total = jnp.swapaxes(total.reshape(parts, z_size, -1, keep.shape[1]), 0, 1)
    total = total.reshape(z_size, -1, keep.shape[1])
    return lax.psum_scatter(total, "z", scatter_dimension=0, tiled=False)


def eight_rows(*rows):
    rows = [r.reshape(1, -1) for r in rows]
    return jnp.concatenate(rows + [jnp.zeros_like(rows[0])] * (8 - len(rows)), axis=0)


def on_pair(
    hidden_in, cond, scale_sizes, w_ada, b_ada, w_qkv, b_qkv, head_scale,
    w_proj, b_proj, w_fc1, b_fc1, w_fc2, b_fc2, grad_out,
):
    y = lax.axis_index("y")
    core = lax.axis_index("core")
    z = lax.axis_index("z")
    x = lax.axis_index("x")
    layer_count = w_ada.shape[0]
    seq_row, width = cond.shape
    rows_dev = hidden_in.shape[0]
    rows_pad = -(-rows_dev // 32) * 32
    d_col = b_qkv.shape[2]
    head_width = d_col // head_scale.shape[1]
    y_size, z_size, x_size = (lax.axis_size(a) for a in ("y", "z", "x"))
    heads = z_size * x_size
    low = width // 2
    rows_d = w_qkv.shape[1]
    hid_dev = w_fc1.shape[2]
    hid_core = hid_dev // 2

    qkv_t = jnp.transpose(w_qkv, (0, 2, 3, 1)).reshape(layer_count, 3, 2, head_width, rows_d)
    qkv_t = jnp.transpose(qkv_t, (0, 2, 1, 3, 4)).reshape(layer_count, 6 * head_width, rows_d)
    fc1_t = jnp.transpose(w_fc1, (0, 2, 1))
    three, four = 3 * head_width, 4 * head_width
    halves = [
        jnp.concatenate(parts, axis=1)
        for parts in (
            (qkv_t[:, :three], w_proj[:, :head_width], fc1_t[:, :hid_core], w_fc2[:, :hid_core]),
            (qkv_t[:, three:], w_proj[:, head_width:], fc1_t[:, hid_core:], w_fc2[:, hid_core:]),
        )
    ]
    kept = jnp.where(core == 0, halves[0], halves[1])
    came = sibling(jnp.where(core == 0, halves[1], halves[0]))
    shards = jnp.concatenate(
        (jnp.where(core == 0, kept, came), jnp.where(core == 0, came, kept)), axis=2
    )
    cuts = (0, four, four + hid_core, four + 2 * hid_core)

    def z_gather(l, i):
        by_z = lax.all_gather(shards[l, cuts[i] : cuts[i + 1]], "z", axis=0, tiled=False)
        if i == 0:
            by_z = jnp.swapaxes(by_z.reshape(z_size, 4, head_width, low), 0, 1)
        return by_z.reshape(-1, low)

    def send(rows):
        return rows, across(rows, "x"), across(rows, "y")

    def send_on(state):
        _, by_x, by_y = state
        half = by_x.shape[0] // 2
        return across(by_x[:half], "y"), across(by_y[half:], "x")

    def whole(state, halves):
        return (*state, jnp.concatenate(halves))

    def together(*values):
        return lax.optimization_barrier(values)

    late = shards[1, cuts[2] :]
    late_x, late_y = across(late, "x"), across(late, "y")
    chunks = [z_gather(l, i) for l in range(layer_count) for i in range(3)][:5]
    late_far = across(late_x, "y")
    late_blocks = lax.all_gather(jnp.stack((late, late_y, late_x, late_far)), "z", axis=0, tiled=False)
    sent = send(tie(chunks[0], late_far, late_y))

    cond_low = jax.nn.silu(cond.astype(F32)).astype(BF)
    silu_rows = lax.all_gather(cond_low, ("y", "core"), axis=0, tiled=True)
    row = y * 2 + core
    silu_own = lax.dynamic_slice_in_dim(silu_rows, row * rows_d, rows_d, axis=1)
    seqs = silu_rows.shape[0]
    ada_size = layer_count * 6 * d_col
    part = dot(silu_own, jnp.transpose(w_ada, (1, 0, 2, 3)).reshape(rows_d, ada_size))
    part = part + jnp.where(row == 0, b_ada.astype(F32).reshape(1, ada_size), 0.0)
    smalls = (b_qkv, b_fc1, b_proj, b_fc2, head_scale)
    sizes = [v.size for v in smalls]
    offs = [sum(sizes[:i]) for i in range(6)]
    n_rows = y_size * 2
    quarter = -(-offs[5] // (n_rows * 128)) * 128
    small = jnp.concatenate([v.reshape(-1).astype(F32) for v in smalls])
    small = jnp.pad(small, (0, n_rows * quarter - offs[5])).reshape(n_rows, quarter)
    small = lax.dynamic_index_in_dim(small, row, axis=0, keepdims=True)
    part = jnp.concatenate((part, jnp.broadcast_to(small, (seqs, quarter))), axis=1)
    to_all = jnp.swapaxes(part.reshape(y_size, x_size, z_size, -1), 1, 2)
    to_all = jnp.broadcast_to(to_all[:, None], (y_size, 2) + to_all.shape[1:])
    from_all = lax.all_to_all(
        to_all.reshape(n_rows * z_size * x_size, -1), ("y", "core", "z", "x"),
        split_axis=0, concat_axis=0, tiled=True,
    ).reshape(n_rows, z_size, x_size, -1)
    ada = jnp.sum(from_all[..., :ada_size], axis=0).reshape(z_size * x_size, layer_count, 6, d_col)
    ada = turned(jnp.transpose(ada, (1, 2, 0, 3)).reshape(layer_count, 6, width), y, 2)
    small = jnp.transpose(from_all[..., ada_size:], (1, 2, 0, 3)).reshape(z_size, x_size, -1)
    s_qkv, s_fc1, s_proj, s_fc2, s_scale = [small[:, :, offs[i] : offs[i + 1]] for i in range(5)]

    def by_core(values, shape, axis):
        values = values.reshape((z_size, x_size) + shape)
        values = lax.dynamic_index_in_dim(values, core, axis=axis, keepdims=False)
        return turned(jnp.swapaxes(values, 0, 1), x, 0)

    def by_d(values):
        values = jnp.swapaxes(values.reshape(z_size * x_size, layer_count, d_col), 0, 1)
        return turned(values.reshape(layer_count, width), y, 1)

    bias_qkv = by_core(s_qkv, (layer_count, 2, 2, head_width), 4)
    bias_qkv = jnp.transpose(bias_qkv, (2, 3, 0, 1, 4)).reshape(layer_count, 2, low)
    scales = by_core(s_scale, (layer_count, 2), 3)
    scales = jnp.transpose(scales, (2, 0, 1)).reshape(layer_count, heads)
    scales = jnp.repeat(scales, head_width, axis=1)
    bias_fc1 = by_core(s_fc1, (layer_count, 2, hid_core), 3)
    bias_fc1 = jnp.transpose(bias_fc1, (2, 0, 1, 3)).reshape(layer_count, 1, -1)
    bias_proj, bias_fc2 = by_d(s_proj), by_d(s_fc2)

    sizes_f = scale_sizes.astype(F32)
    sizes_f = jnp.where(core == x, sizes_f, sibling(sizes_f))
    own_sizes = lax.dynamic_index_in_dim(sizes_f, z, axis=0, keepdims=False).astype(jnp.int32)
    index = jnp.arange(rows_pad, dtype=jnp.int32)
    places = jnp.concatenate((core * rows_dev + index, (1 - core) * rows_dev + index))
    starts = jnp.cumsum(own_sizes) - own_sizes
    ends = jnp.sum(jnp.where(starts[None, :] <= places[:, None], own_sizes[None, :], 0), axis=1)
    real = jnp.concatenate((index, index)) < rows_dev
    key_places = jnp.where(real, places, 1 << 20).astype(F32)
    ends = ends.astype(F32)
    place_col, end_col = key_places[:, None], ends[:, None]
    place_row, end_row = eight_rows(key_places), eight_rows(ends)
    ones = head_ones(low // 2, head_width)

    def own_tokens(values):
        return jnp.pad(turned(trade(values, core != x), y, 1), ((0, rows_pad - rows_dev), (0, 0)))

    state = own_tokens(hidden_in).astype(F32)
    grad = own_tokens(grad_out).astype(F32)
    hidden = (normalize(state)[0] * (1.0 + ada[0, 2][None]) + ada[0, 4][None]).astype(BF)
    weights = [None] * 5 + [(late_blocks,) * 4]

    def attn_start(l, hidden):
        vectors = eight_rows(bias_qkv[l, 0], bias_qkv[l, 1], scales[l])
        found = qkv_up(hidden, sibling(hidden), weights[3 * l], vectors, ones)
        return found

    def attn_end(l, attn, state):
        own, send_own = attn_down(attn, weights[3 * l])
        branch, middle, hidden = mix(
            own, sibling(send_own), state,
            eight_rows(bias_proj[l], ada[l, 0], 1.0 + ada[l, 3], ada[l, 5]), False,
        )
        return branch, middle, hidden

    def fc_start(l, hidden):
        return fc_up(hidden, sibling(hidden), weights[3 * l + 1], bias_fc1[l])

    def fc_end(l, act, middle):
        own, send_own = fc_down(act, weights[3 * l + 2])
        last = l == layer_count - 1
        after = ada[l if last else l + 1]
        return mix(
            own, sibling(send_own), middle,
            eight_rows(bias_fc2[l], ada[l, 1], 1.0 + after[2], after[4]), last,
        )

    *sent, hidden, grad = together(*sent, hidden, grad)
    halves = send_on(sent)
    *halves, chunks[1], hidden = together(*halves, chunks[1], hidden)
    weights[0], sent = whole(sent, halves), send(chunks[1])
    found0 = attn_start(0, hidden)
    attn0, rest0, logs0 = attn_mix(*found0[3:6], end_col, place_row, head_width)
    *sent, attn0 = together(*sent, attn0)
    halves = send_on(sent)
    branch0, middle0, hidden2 = attn_end(0, attn0, state)
    *halves, chunks[2], hidden2 = together(*halves, chunks[2], hidden2)
    weights[1], sent = whole(sent, halves), send(chunks[2])
    joined2, act, slope = fc_start(0, hidden2)
    *sent, act = together(*sent, act)
    halves = send_on(sent)
    *halves, chunks[3], act = together(*halves, chunks[3], act)
    weights[2], sent = whole(sent, halves), send(chunks[3])
    feed, state1, hidden = fc_end(0, act, middle0)
    saved = [(*found0, logs0, attn0, rest0, branch0, middle0, joined2, act, slope, feed, state)]
    *sent, hidden = together(*sent, hidden)
    halves = send_on(sent)
    *halves, chunks[4], hidden = together(*halves, chunks[4], hidden)
    weights[3], sent = whole(sent, halves), send(chunks[4])
    found1 = attn_start(1, hidden)
    attn1, rest1, logs1 = attn_mix(*found1[3:6], end_col, place_row, head_width)
    *sent, attn1 = together(*sent, attn1)
    halves = send_on(sent)
    branch1, middle1, hidden2 = attn_end(1, attn1, state1)
    *halves, hidden2 = together(*halves, hidden2)
    weights[4] = whole(sent, halves)
    joined2, act, slope = fc_start(1, hidden2)
    feed, state2, mixed = fc_end(1, act, middle1)
    saved.append((*found1, logs1, attn1, rest1, branch1, middle1, joined2, act, slope, feed, state1))

    top = layer_count - 1
    d_ada = [[None] * 6 for _ in range(layer_count)]
    d_biases = [[None] * 5 for _ in range(layer_count)]
    d_weights = [None] * layer_count
    fold = lambda sums: jnp.sum(sums.reshape(-1, 8, sums.shape[1]), axis=1)
    d_low = (grad * ada[top, 1][None]).astype(BF)
    d_ada[top][1] = jnp.sum(grad * saved[1][-2].astype(F32), axis=0)
    d_biases[top][1] = jnp.sum(d_low.astype(F32), axis=0)
    def fc_turn(l, d_low):
        act, slope, joined2 = saved[l][-4], saved[l][-3], saved[l][-5]
        return fc_back(
            d_low, sibling(d_low), weights[3 * l + 2], weights[3 * l + 1], slope, act, joined2, l == 1
        )

    def fc_norm(l, found, grad):
        sums_pre, own, send_own = found
        d_middle, d_low, sums = mix_back(
            own, sibling(send_own), saved[l][10], grad, saved[l][9], eight_rows(1.0 + ada[l, 3], ada[l, 0])
        )
        d_ada[l][3], d_ada[l][5], d_ada[l][0], d_biases[l][0] = fold(sums)
        d_biases[l][3] = fold(sums_pre)[0]
        return d_middle, d_low

    def attn_turn(l, d_low):
        joined1, q_raw, k_raw, q_low, k_low, v_low, logs, attn, rest = saved[l][:9]
        return attn_back(
            d_low, sibling(d_low), weights[3 * l], q_low, k_low, v_low, attn, rest, logs, q_raw, k_raw, joined1,
            eight_rows(scales[l]), place_col, end_row, head_width,
        )

    def attn_norm(l, found, got_own, d_middle):
        sums_qkv, own, _ = found
        before = max(l - 1, 0)
        grad, d_low, sums = mix_back(
            own, got_own, saved[l][-1], d_middle, saved[before][-2],
            eight_rows(1.0 + ada[l, 2], ada[before, 1]),
        )
        sums = fold(sums)
        d_ada[l][2], d_ada[l][4] = sums[0], sums[1]
        if l > 0:
            d_ada[l - 1][1], d_biases[l - 1][1] = sums[2], sums[3]
        d_biases[l][2] = sums_qkv[:2]
        d_biases[l][4] = jnp.sum(sums_qkv[2].reshape(heads, head_width), axis=1)
        return grad, d_low

    def halves_of(blocks):
        return across(blocks[3][:low], "y"), across(blocks[3][low:], "x")

    def given_back(values):
        return trade(turned(values[:rows_dev], y, 1).astype(BF), core != x)

    mixed = given_back(mixed)
    found, two, one = fc_turn(1, d_low)
    mixed, *found = together(mixed, *found)
    two_sum = lax.psum_scatter(two[0], "z", scatter_dimension=0, tiled=False)
    got_a, got_b = halves_of(one)
    d_middle, d_low = fc_norm(1, found, grad)
    got_a, got_b, d_low = together(got_a, got_b, d_low)
    near_x, near_y = near_parts(one, got_a, got_b)
    one_x, one_y = across(near_x, "x"), across(near_y, "y")
    found, four_parts = attn_turn(1, d_low)
    one_x, one_y, *found = together(one_x, one_y, *found)
    last = flat(four_parts)
    got_a, got_b = halves_of(last)
    grad, d_low = attn_norm(1, found, sibling(found[2]), d_middle)
    got_a, got_b, d_low = together(got_a, got_b, d_low)
    near_x, near_y = near_parts(last, got_a, got_b)
    last_x, last_y = across(near_x, "x"), across(near_y, "y")
    g_one1 = settle(one[0], one_x, one_y, 1, z_size)
    found, two, one = fc_turn(0, d_low)
    last_x, last_y, two_sum, *found = together(last_x, last_y, two_sum, *found)
    got_a, got_b = halves_of(one)
    d_middle, d_low = fc_norm(0, found, grad)
    got_a, got_b, d_low = together(got_a, got_b, d_low)
    near_x, near_y = near_parts(one, got_a, got_b)
    one_x, one_y = across(near_x, "x"), across(near_y, "y")
    far_a, far_b = halves_of(two)
    g_attn1 = settle(last[0], last_x, last_y, 4, z_size)
    found, four_parts = attn_turn(0, d_low)
    one_x, one_y, far_a, far_b, *found = together(one_x, one_y, far_a, far_b, *found)
    last = flat(four_parts)
    got_a, got_b = halves_of(last)
    got_own = sibling(found[2])
    near_x, near_y = near_parts(two, far_a, far_b)
    got_own, near_x, near_y = together(got_own, near_x, near_y)
    two_x, two_y = across(near_x, "x"), across(near_y, "y")
    grad, d_low = attn_norm(0, found, got_own, d_middle)
    got_a, got_b, one_x, grad = together(got_a, got_b, one_x, grad)
    g_one0 = settle(one[0], one_x, one_y, 1, z_size)
    two_x, two_y, got_a = together(two_x, two_y, got_a)
    near_x, near_y = near_parts(last, got_a, got_b)
    last_x, last_y = across(near_x, "x"), across(near_y, "y")
    g_two0 = settle(two[0], two_x, two_y, 1, z_size)
    last_x, last_y, two_sum = together(last_x, last_y, two_sum)
    late_far, late_y = across(two_sum[3], "y"), across(two_sum[1], "y")
    g_attn0 = settle(last[0], last_x, last_y, 4, z_size)
    late_x = across(add_low(two_sum[2], late_far), "x")
    g_two1 = add_low(two_sum[0], late_x, late_y)
    d_weights = [jnp.concatenate(v, axis=0) for v in ((g_attn0, g_one0, g_two0), (g_attn1, g_one1, g_two1))]

    def by_col(values):
        values = turned(values, y, values.ndim - 1)
        values = values.reshape(values.shape[:-1] + (z_size, x_size, d_col))
        return jnp.moveaxis(values, (-3, -2), (0, 1)).reshape(z_size, x_size, -1)

    def by_hidden(values):
        return jnp.swapaxes(turned(values, x, 0), 0, 1).reshape(z_size, x_size, -1)

    packs = [by_col(jnp.stack([jnp.stack(v) for v in d_ada]))]
    for l in range(layer_count):
        db_proj, db_fc2, db_qkv, db_fc1, d_head = d_biases[l]
        packs.append(by_col(db_proj))
        packs.append(by_col(db_fc2))
        packs.append(by_hidden(jnp.moveaxis(db_qkv.reshape(2, x_size, z_size, head_width), 0, 2)))
        packs.append(by_hidden(db_fc1.reshape(x_size, z_size, hid_core)))
        packs.append(by_hidden(d_head.reshape(x_size, z_size, 1)))
    lens = [p.shape[2] for p in packs]
    pack = jnp.concatenate(packs, axis=2)
    pack = jnp.broadcast_to(pack[None], (n_rows,) + pack.shape)
    got = lax.all_to_all(
        pack.reshape(n_rows * z_size * x_size, -1), ("y", "core", "z", "x"),
        split_axis=0, concat_axis=0, tiled=True,
    ).reshape(y_size, 2, z_size, x_size, -1)
    pos = lens[0]
    d_ada_all = jnp.sum(got[..., :pos], axis=1)
    d_ada_all = jnp.swapaxes(d_ada_all, 1, 2).reshape(seqs, -1).astype(BF)
    out_b_ada = jnp.sum(d_ada_all.astype(F32), axis=0).reshape(layer_count, 6, d_col)
    out_w_ada = dot(silu_own, d_ada_all, TN).reshape(rows_d, layer_count, 6, d_col)
    out_w_ada = jnp.swapaxes(out_w_ada, 0, 1)
    sums = jnp.sum(got[..., pos:], axis=(0, 2, 3))
    outs = [[] for _ in range(5)]
    pos = 0
    for l in range(layer_count):
        for i in range(5):
            count = lens[1 + 5 * l + i]
            outs[i].append(sums[:, pos : pos + count])
            pos += count
    out_b_proj = jnp.stack([v[0] + v[1] for v in outs[0]])
    out_b_fc2 = jnp.stack([v[0] + v[1] for v in outs[1]])
    out_b_qkv = jnp.stack(
        [jnp.swapaxes(v.reshape(2, 2, head_width), 0, 1).reshape(2, d_col) for v in outs[2]]
    )
    out_b_fc1 = jnp.stack([v.reshape(-1) for v in outs[3]])
    out_scale = jnp.stack([v.reshape(-1) for v in outs[4]])

    own = jnp.stack(d_weights)
    kept = jnp.where(core == 0, own[:, :, :rows_d], own[:, :, rows_d:])
    came = sibling(jnp.where(core == 0, own[:, :, rows_d:], own[:, :, :rows_d]))
    first = jnp.where(core == 0, kept, came).astype(F32)
    second = jnp.where(core == 0, came, kept).astype(F32)
    wq = jnp.stack((first[:, :three], second[:, :three]), axis=1)
    wq = wq.reshape(layer_count, 2, 3, head_width, rows_d)
    out_w_qkv = jnp.transpose(wq, (0, 4, 2, 1, 3)).reshape(layer_count, rows_d, 3, d_col)

    def pick(i, j):
        return jnp.concatenate((first[:, i:j], second[:, i:j]), axis=1)

    return (
        mixed, given_back(grad).astype(F32), out_w_ada, out_b_ada, out_w_qkv, out_b_qkv, out_scale,
        pick(three, four), out_b_proj, jnp.swapaxes(pick(cuts[1], cuts[2]), 1, 2), out_b_fc1,
        pick(cuts[2], cuts[3]), out_b_fc2,
    )


def solution(mesh):
    rows, cols = mesh.devices.shape
    row, col, body, used = ("row",), ("col",), on_device, mesh
    if rows == 4 and cols == 8:
        used = jax.sharding.Mesh(
            mesh.devices.reshape(rows // 2, 2, cols // 2, 2), ("y", "core", "z", "x")
        )
        row, col, body = ("y", "core"), ("z", "x"), on_pair
    tokens = P(row + col, None)
    out_weights = (
        P(None, row, None, col),
        P(None, None, col),
        P(None, row, None, col),
        P(None, None, col),
        P(None, col),
        P(None, col, row),
        P(None, col),
        P(None, row, col),
        P(None, col),
        P(None, col, row),
        P(None, col),
    )
    return jax.shard_map(
        body,
        mesh=used,
        in_specs=(tokens, P(row, None), P(row, None)) + out_weights + (tokens,),
        out_specs=(tokens, tokens) + out_weights,
        check_vma=False,
    )
```

```python
import jax
import jax.numpy as jnp
from jax import lax
from jax.experimental import pallas as pl
from jax.experimental.pallas import tpu as pltpu
from jax.sharding import PartitionSpec as P

HIGH = lax.Precision.HIGHEST
EPS_NORM = 1e-06
EPS_UNIT = 1e-06
NEG_FILL = -1e30


def block_ends(scale_sizes, seq_len):
    ends = jnp.cumsum(scale_sizes, axis=1)
    starts = ends - scale_sizes
    position = jnp.arange(seq_len, dtype=jnp.int32)
    picked = jnp.where(starts[:, None, :] <= position[None, :, None], scale_sizes[:, None, :], 0)
    return jnp.sum(picked, axis=2)


def normalize(values):
    center = jnp.mean(values, axis=-1, keepdims=True)
    spread = jnp.mean(values * values, axis=-1, keepdims=True) - center * center
    rstd = lax.rsqrt(spread + EPS_NORM)
    return ((values - center) * rstd, rstd)


def norm_back(grad_normed, normed, rstd):
    means = jnp.mean(grad_normed, axis=-1, keepdims=True)
    crosses = jnp.mean(grad_normed * normed, axis=-1, keepdims=True)
    return rstd * (grad_normed - means - normed * crosses)


def unit_pair(queries, key_rows, scale_here):
    q_norm = (
        queries
        * lax.rsqrt(jnp.sum(queries * queries, axis=-1, keepdims=True) + EPS_UNIT)
        * scale_here[:, None]
    )
    k_norm = key_rows * lax.rsqrt(jnp.sum(key_rows * key_rows, axis=-1, keepdims=True) + EPS_UNIT)
    return (q_norm, k_norm)


def project_in(hidden_low, weight):
    return (
        jnp.dot(
            lax.all_gather(hidden_low, "col", axis=0, tiled=True),
            weight,
            preferred_element_type=jnp.float32,
        ),
        hidden_low,
    )


def back_in(grad_three, kept, weight, whole_weight):
    tok_row = grad_three.shape[0]
    grad_low = grad_three.reshape(tok_row, grad_three.shape[1] * grad_three.shape[2])
    own_grads = lax.all_to_all(grad_three, "col", split_axis=0, concat_axis=2, tiled=True)
    grad_hidden = lax.dot_general(
        own_grads, whole_weight, (((1, 2), (1, 2)), ((), ())), preferred_element_type=jnp.float32
    )

    def add_piece(total, piece, start):
        return lax.dot_general(
            piece, grad_low, (((0,), (0,)), ((), ())), preferred_element_type=jnp.float32
        )

    init = jnp.zeros(weight.shape, jnp.float32)
    grad_weight = add_piece(init, lax.all_gather(kept, "col", axis=0, tiled=True), jnp.int32(0))
    return (grad_hidden, grad_weight)


def project_out(act_low, whole_weight):
    own_rows = lax.all_to_all(act_low, "col", split_axis=0, concat_axis=1, tiled=True)
    return jnp.dot(own_rows, whole_weight, preferred_element_type=jnp.float32)


def back_out(grad_low, act_low, weight):

    def add_piece(carry, piece, start):
        part = lax.dot_general(
            piece, weight, (((1,), (1,)), ((), ())), preferred_element_type=jnp.float32
        )
        grad_weight = lax.dot_general(
            act_low, piece, (((0,), (0,)), ((), ())), preferred_element_type=jnp.float32
        )
        return (part, grad_weight)

    init = (
        jnp.zeros((act_low.shape[0], weight.shape[0]), jnp.float32),
        jnp.zeros(weight.shape, jnp.float32),
    )
    return add_piece(init, lax.all_gather(grad_low, "col", axis=0, tiled=True), jnp.int32(0))


def masked_scores(q_rows, k_rows, ends):
    position = jnp.arange(k_rows.shape[0], dtype=jnp.int32)
    scores = jnp.einsum("the,she->hts", q_rows, k_rows, preferred_element_type=jnp.float32)
    visible = position[None, :] < ends[:, None]
    return jnp.where(visible[None], scores, NEG_FILL)


def attend(pieces):
    q_rows, k_rows, v_rows, ends = pieces
    scores = masked_scores(q_rows, k_rows, ends)
    top = jnp.max(scores, axis=-1, keepdims=True)
    expo = jnp.exp(scores - top)
    total = jnp.sum(expo, axis=-1, keepdims=True)
    probs = (expo / total).astype(jnp.bfloat16)
    attended = jnp.einsum("hts,she->the", probs, v_rows, preferred_element_type=jnp.float32)
    return (attended, (top + jnp.log(total))[..., 0])


def attend_back(pieces):
    q_rows, k_rows, v_rows, ends, log_total, grad_rows = pieces
    scores = masked_scores(q_rows, k_rows, ends)
    probs = jnp.exp(scores - log_total[..., None])
    grad_probs = jnp.einsum("the,she->hts", grad_rows, v_rows, preferred_element_type=jnp.float32)
    delta = jnp.sum(probs * grad_probs, axis=-1, keepdims=True)
    grad_scores = (probs * (grad_probs - delta)).astype(jnp.bfloat16)
    grad_q = jnp.einsum("hts,she->the", grad_scores, k_rows, preferred_element_type=jnp.float32)
    grad_k = jnp.einsum("hts,the->she", grad_scores, q_rows, preferred_element_type=jnp.float32)
    grad_v = jnp.einsum(
        "hts,the->she", probs.astype(jnp.bfloat16), grad_rows, preferred_element_type=jnp.float32
    )
    return (grad_q, grad_k, grad_v)


def gelu_tanh(values):
    return jax.nn.gelu(values, approximate=True)


def on_device(
    hidden_in,
    cond,
    scale_sizes,
    w_ada,
    b_ada,
    w_qkv,
    b_qkv,
    head_scale,
    w_proj,
    b_proj,
    w_fc1,
    b_fc1,
    w_fc2,
    b_fc2,
    grad_out,
):
    seq_row, width = cond.shape
    rows_dev = hidden_in.shape[0]
    tok_row = rows_dev * lax.axis_size("col")
    seq_len = tok_row // seq_row
    layer_count = w_ada.shape[0]
    d_col = b_qkv.shape[2]
    heads_dev = head_scale.shape[1]
    head_width = d_col // heads_dev
    full_ada, full_qkv, full_fc1, full_proj, full_fc2 = (
        lax.all_gather(w_ada, "row", axis=1, tiled=True),
        lax.all_gather(w_qkv, "row", axis=1, tiled=True),
        lax.all_gather(w_fc1, "row", axis=1, tiled=True),
        lax.all_gather(w_proj, "row", axis=2, tiled=True),
        lax.all_gather(w_fc2, "row", axis=2, tiled=True),
    )
    whole_proj, whole_fc2, whole_qkv, whole_fc1 = (
        lax.all_gather(full_proj, "col", axis=1, tiled=True),
        lax.all_gather(full_fc2, "col", axis=1, tiled=True),
        lax.all_gather(full_qkv, "col", axis=3, tiled=True),
        lax.all_gather(full_fc1, "col", axis=2, tiled=True),
    )
    ends = block_ends(scale_sizes, seq_len)
    silu_low = jax.nn.silu(cond.astype(jnp.float32)).astype(jnp.bfloat16)
    places = lax.axis_index("col") * rows_dev + jnp.arange(rows_dev, dtype=jnp.int32)
    member = (places[:, None] // seq_len == jnp.arange(seq_row, dtype=jnp.int32)[None, :]).astype(
        jnp.float32
    )

    def per_token(values):
        return jnp.dot(member, values, precision=HIGH)

    def per_sequence(values):
        return lax.dot_general(member, values, (((0,), (0,)), ((), ())), precision=HIGH)

    ada_parts = []
    for layer_index in range(layer_count):
        part = jnp.dot(
            silu_low,
            full_ada[layer_index].reshape(width, 6 * d_col),
            preferred_element_type=jnp.float32,
        )
        ada_parts.append(
            part.reshape(seq_row, 6, d_col) + b_ada[layer_index].astype(jnp.float32)[None]
        )
    ada_full, bias_proj_full, bias_fc2_full = (
        lax.all_gather(jnp.stack(ada_parts), "col", axis=3, tiled=True),
        lax.all_gather(b_proj.astype(jnp.float32), "col", axis=1, tiled=True),
        lax.all_gather(b_fc2.astype(jnp.float32), "col", axis=1, tiled=True),
    )
    current = hidden_in.astype(jnp.float32)
    saved = []
    for layer_index in range(layer_count):
        ada = ada_full[layer_index]
        gamma1, gamma2, scale1, scale2, shift1, shift2 = [
            per_token(ada[:, index]) for index in range(6)
        ]
        normed1, rstd1 = normalize(current)
        hidden1 = (normed1 * (1.0 + scale1) + shift1).astype(jnp.bfloat16)
        mixed_qkv, kept1 = project_in(hidden1, full_qkv[layer_index].reshape(width, 3 * d_col))
        bias_two = b_qkv[layer_index].astype(jnp.float32)
        bias_three = jnp.stack((bias_two[0], jnp.zeros_like(bias_two[0]), bias_two[1]))
        mixed_qkv = mixed_qkv + bias_three.reshape(1, 3 * d_col)
        split = mixed_qkv.reshape(seq_row, seq_len, 3, heads_dev, head_width)
        queries, key_rows, value_rows = (split[:, :, 0], split[:, :, 1], split[:, :, 2])
        scale_here = head_scale[layer_index].astype(jnp.float32)
        q_norm, k_norm = unit_pair(queries, key_rows, scale_here)
        q_low = q_norm.astype(jnp.bfloat16)
        k_low = k_norm.astype(jnp.bfloat16)
        v_low = value_rows.astype(jnp.bfloat16)
        attended, log_total = lax.map(attend, (q_low, k_low, v_low, ends))
        attn_low = attended.reshape(tok_row, d_col).astype(jnp.bfloat16)
        branch = project_out(attn_low, whole_proj[layer_index]) + bias_proj_full[layer_index][None]
        middle = current + gamma1 * branch
        normed2, rstd2 = normalize(middle)
        hidden2 = (normed2 * (1.0 + scale2) + shift2).astype(jnp.bfloat16)
        pre_act, kept2 = project_in(hidden2, full_fc1[layer_index])
        pre_act = pre_act + b_fc1[layer_index].astype(jnp.float32)[None]
        act_low = gelu_tanh(pre_act).astype(jnp.bfloat16)
        feed = project_out(act_low, whole_fc2[layer_index]) + bias_fc2_full[layer_index][None]
        saved.append(
            (
                normed1,
                rstd1,
                kept1,
                queries,
                key_rows,
                scale_here,
                q_low,
                k_low,
                v_low,
                log_total,
                attn_low,
                branch,
                normed2,
                rstd2,
                kept2,
                pre_act,
                act_low,
                feed,
            )
        )
        current = middle + gamma2 * feed
    mixed = current.astype(jnp.bfloat16)
    grad_state = grad_out.astype(jnp.float32)
    grads_ada = [None] * layer_count
    grads_w_qkv = [None] * layer_count
    grads_b_qkv = [None] * layer_count
    grads_scale = [None] * layer_count
    grads_w_proj = [None] * layer_count
    grads_b_proj = [None] * layer_count
    grads_w_fc1 = [None] * layer_count
    grads_b_fc1 = [None] * layer_count
    grads_w_fc2 = [None] * layer_count
    grads_b_fc2 = [None] * layer_count
    for layer_index in reversed(range(layer_count)):
        (
            normed1,
            rstd1,
            kept1,
            queries,
            key_rows,
            scale_here,
            q_low,
            k_low,
            v_low,
            log_total,
            attn_low,
            branch,
            normed2,
            rstd2,
            kept2,
            pre_act,
            act_low,
            feed,
        ) = saved[layer_index]
        ada = ada_full[layer_index]
        gamma1, gamma2, scale1, scale2, shift1, shift2 = [
            per_token(ada[:, index]) for index in range(6)
        ]
        d_gamma2 = per_sequence(grad_state * feed)
        grad_feed = (grad_state * gamma2).astype(jnp.bfloat16)
        grads_b_fc2[layer_index] = jnp.sum(grad_feed.astype(jnp.float32), axis=0)
        grad_act, grads_w_fc2[layer_index] = back_out(grad_feed, act_low, full_fc2[layer_index])
        gelu_pull = jax.vjp(gelu_tanh, pre_act)[1]
        grad_pre = gelu_pull(grad_act)[0].astype(jnp.bfloat16)
        grads_b_fc1[layer_index] = jnp.sum(grad_pre.astype(jnp.float32), axis=0)
        whole_one = whole_fc1[layer_index].reshape(width, 1, whole_fc1.shape[2])
        grad_hidden2, grads_w_fc1[layer_index] = back_in(
            grad_pre.reshape(tok_row, 1, grad_pre.shape[1]), kept2, full_fc1[layer_index], whole_one
        )
        d_scale2 = per_sequence(grad_hidden2 * normed2)
        d_shift2 = per_sequence(grad_hidden2)
        grad_middle = grad_state + norm_back(grad_hidden2 * (1.0 + scale2), normed2, rstd2)
        d_gamma1 = per_sequence(grad_middle * branch)
        grad_branch = (grad_middle * gamma1).astype(jnp.bfloat16)
        grads_b_proj[layer_index] = jnp.sum(grad_branch.astype(jnp.float32), axis=0)
        grad_attn, grads_w_proj[layer_index] = back_out(
            grad_branch, attn_low, full_proj[layer_index]
        )
        grad_attn_low = grad_attn.astype(jnp.bfloat16).reshape(
            seq_row, seq_len, heads_dev, head_width
        )
        grad_qn, grad_kn, grad_v = lax.map(
            attend_back, (q_low, k_low, v_low, ends, log_total, grad_attn_low)
        )
        unit_pull = jax.vjp(unit_pair, queries, key_rows, scale_here)[1]
        grad_q, grad_k, grads_scale[layer_index] = unit_pull((grad_qn, grad_kn))
        grad_qkv = (
            jnp.stack((grad_q, grad_k, grad_v), axis=2)
            .reshape(tok_row, 3, d_col)
            .astype(jnp.bfloat16)
        )
        bias_sums = jnp.sum(grad_qkv.astype(jnp.float32), axis=0)
        grads_b_qkv[layer_index] = jnp.stack((bias_sums[0], bias_sums[2]))
        grad_hidden1, weight_qkv = back_in(
            grad_qkv, kept1, full_qkv[layer_index].reshape(width, 3 * d_col), whole_qkv[layer_index]
        )
        grads_w_qkv[layer_index] = weight_qkv.reshape(width, 3, d_col)
        d_scale1 = per_sequence(grad_hidden1 * normed1)
        d_shift1 = per_sequence(grad_hidden1)
        grad_state = grad_middle + norm_back(grad_hidden1 * (1.0 + scale1), normed1, rstd1)
        grads_ada[layer_index] = jnp.stack(
            (d_gamma1, d_gamma2, d_scale1, d_scale2, d_shift1, d_shift2), axis=1
        )
    ada_sums, bias_proj_col, bias_fc2_col = (
        lax.psum_scatter(
            jnp.stack(grads_ada).astype(jnp.bfloat16), "col", scatter_dimension=3, tiled=True
        ).astype(jnp.float32),
        lax.psum_scatter(
            jnp.stack(grads_b_proj).astype(jnp.bfloat16), "col", scatter_dimension=1, tiled=True
        ).astype(jnp.float32),
        lax.psum_scatter(
            jnp.stack(grads_b_fc2).astype(jnp.bfloat16), "col", scatter_dimension=1, tiled=True
        ).astype(jnp.float32),
    )
    grad_ada = ada_sums.astype(jnp.bfloat16)
    weights_ada = []
    for layer_index in range(layer_count):
        weight_ada = lax.dot_general(
            silu_low,
            grad_ada[layer_index].reshape(seq_row, 6 * d_col),
            (((0,), (0,)), ((), ())),
            preferred_element_type=jnp.float32,
        )
        weights_ada.append(weight_ada.reshape(width, 6, d_col))
    bias_ada_local = jnp.sum(grad_ada.astype(jnp.float32), axis=1)
    sum_ada, sum_qkv, sum_fc1, sum_proj, sum_fc2 = (
        lax.psum_scatter(
            jnp.stack(weights_ada).astype(jnp.bfloat16), "row", scatter_dimension=1, tiled=True
        ).astype(jnp.float32),
        lax.psum_scatter(
            jnp.stack(grads_w_qkv).astype(jnp.bfloat16), "row", scatter_dimension=1, tiled=True
        ).astype(jnp.float32),
        lax.psum_scatter(
            jnp.stack(grads_w_fc1).astype(jnp.bfloat16), "row", scatter_dimension=1, tiled=True
        ).astype(jnp.float32),
        lax.psum_scatter(
            jnp.stack(grads_w_proj).astype(jnp.bfloat16), "row", scatter_dimension=2, tiled=True
        ).astype(jnp.float32),
        lax.psum_scatter(
            jnp.stack(grads_w_fc2).astype(jnp.bfloat16), "row", scatter_dimension=2, tiled=True
        ).astype(jnp.float32),
    )
    bias_ada, bias_qkv, scale_grad, bias_proj, bias_fc1, bias_fc2 = lax.psum(
        (
            bias_ada_local,
            jnp.stack(grads_b_qkv),
            jnp.stack(grads_scale),
            bias_proj_col,
            jnp.stack(grads_b_fc1),
            bias_fc2_col,
        ),
        "row",
    )
    return (
        mixed,
        grad_state,
        sum_ada,
        bias_ada,
        sum_qkv,
        bias_qkv,
        scale_grad,
        sum_proj,
        bias_proj,
        sum_fc1,
        bias_fc1,
        sum_fc2,
        bias_fc2,
    )


BF = jnp.bfloat16
F32 = jnp.float32
NN = (((1,), (0,)), ((), ()))
NT = (((1,), (1,)), ((), ()))
TN = (((0,), (0,)), ((), ()))
VMEM_BYTES = 60 * 1024 * 1024


def sibling(values):
    return lax.ppermute(values, "core", [(0, 1), (1, 0)])


def across(values, axis):
    return lax.ppermute(values, axis, [(0, 1), (1, 0)])


def trade(values, moves):
    return jnp.where(moves, lax.ppermute(values, ("core", "x"), [(1, 2), (2, 1)]), values)


def turned(values, flag, axis):
    half = values.shape[axis] // 2
    return jnp.where(flag == 1, jnp.roll(values, half, axis), values)


def dot(left, right, dims=NN):
    return lax.dot_general(left, right, dims, preferred_element_type=F32)


def shape_of(dims, kind):
    return jax.ShapeDtypeStruct(dims, kind)


def call(body, grid, in_specs, out_specs, out_shape, scratch, flops, moved, args):
    return pl.pallas_call(
        body,
        grid=grid,
        in_specs=in_specs,
        out_specs=out_specs,
        out_shape=out_shape,
        scratch_shapes=scratch,
        compiler_params=pltpu.CompilerParams(
            dimension_semantics=("arbitrary",) * len(grid), vmem_limit_bytes=VMEM_BYTES
        ),
        cost_estimate=pl.CostEstimate(flops=flops // 64, bytes_accessed=moved // 64, transcendentals=0),
    )(*args)


def fixed(dims):
    return pl.BlockSpec(dims, lambda *_: (0,) * len(dims))


def row_loop(total, size, body, unroll=1):
    @pl.loop(0, total // size, unroll=unroll)
    def _(step):
        body(pl.ds(pl.multiple_of(step * size, size), size))


def early(dims, row=0):
    return pl.BlockSpec(dims, lambda t: (row + jnp.minimum(t, 1), 0))


def late(dims, row=0):
    return pl.BlockSpec(dims, lambda t: (row + jnp.maximum(t - 2, 0), 0))


def weight_specs(low, blocks=None):
    if blocks is not None and blocks[0].ndim == 4:
        shape = (2, None, low // 2, low)

        def spec(block, pick):
            return pl.BlockSpec(shape, lambda t: (pick(t), block, 0, 0))

        first, second = lambda t: jnp.minimum(t, 1), lambda t: jnp.maximum(t - 2, 0)
        return [spec(0, first), spec(2, second), spec(1, first), spec(3, lambda t: 0), spec(3, lambda t: 1)]
    return [early((low, low)), late((low, low)), early((low, low)), fixed((low, low)), fixed((low, low))]


def matrix(ref):
    value = ref[...]
    return value.reshape(-1, value.shape[-1])


def with_tile(step, refs, body):
    g, gx, gy, ga, gb = refs

    @pl.when(step < 2)
    def _():
        body(g, gy)

    @pl.when(step == 2)
    def _():
        body(gx, ga)

    @pl.when(step == 3)
    def _():
        body(gx, gb)


def join_into(joined, own, other):
    rows = own.shape[0]
    joined[:rows, :] = own[...]
    joined[rows:, :] = other[...]


def fc_up(own, other, blocks, bias):
    rows, width = own.shape
    low, both = width // 2, 2 * rows
    hid = 4 * low

    def body(own_ref, other_ref, g, gx, gy, ga, gb, bias_ref, joined, act, slope):
        step = pl.program_id(0)

        @pl.when(step == 0)
        def _():
            join_into(joined, own_ref, other_ref)

        def product(first, second):
            for lanes in (slice(0, low // 2), slice(low // 2, low)):
                for sl in (slice(0, rows), slice(rows, both)):
                    pre = dot(joined[sl, :low], first[lanes, :], NT)
                    pre = pre + dot(joined[sl, low:], second[lanes, :], NT) + bias_ref[:, lanes]
                    root = 0.7978845608028654
                    square = pre * pre
                    tanh = jnp.tanh(pre * (root + (root * 0.044715) * square))
                    half = 0.5 + 0.5 * tanh
                    act[sl, lanes] = (pre * half).astype(BF)
                    inner = pre * ((0.5 * root) + (1.5 * 0.044715 * root) * square)
                    slope[sl, lanes] = (half + (1.0 - tanh * tanh) * inner).astype(BF)

        with_tile(step, (g, gx, gy, ga, gb), product)

    return call(
        body,
        (4,),
        [fixed((rows, width))] * 2 + weight_specs(low) + [pl.BlockSpec((1, low), lambda t: (0, t))],
        [fixed((both, width))] + [pl.BlockSpec((both, low), lambda t: (0, t))] * 2,
        [shape_of((both, width), BF), shape_of((both, hid), BF), shape_of((both, hid), BF)],
        [],
        2 * both * width * hid,
        2 * hid * width + 6 * both * width + 4 * both * hid,
        (own, other, *blocks, bias),
    )


def fc_back(own, other, up_blocks, down_blocks, slope, act, hidden, by_z):
    rows, width = own.shape
    low, both = width // 2, 2 * rows
    hid = 4 * low

    def body(own_ref, other_ref, ug, ugx, ugy, uga, ugb, dg, dgx, dgy, dga, dgb, slope_ref, act_ref, hid_ref,
             sums, out_own, out_other, *rest):
        joined, grad, acc = rest[-3:]
        if by_z:
            two_refs, one_refs = rest[:1], rest[1:-3]
        else:
            far_a, far_b = rest[6], rest[7]
            two_refs = (*rest[:3], far_a.at[1], far_b.at[1])
            one_refs = (*rest[3:6], far_a.at[0], far_b.at[0])
        step = pl.program_id(0)

        @pl.when(step == 0)
        def _():
            join_into(joined, own_ref, other_ref)

        def product(up_one, up_two, down_one, down_two, first, last, near, far):
            for i, sl in enumerate((slice(rows, both), slice(0, rows))):
                value = dot(joined[sl, :low], matrix(up_one), NT) + dot(joined[sl, low:], matrix(up_two), NT)
                value = (value * slope_ref[sl, :].astype(F32)).astype(BF)
                grad[sl, :] = value
                total = jnp.sum(value.astype(F32).reshape(rows // 8, 8, low), axis=0)
                sums[...] = total if i == 0 else sums[...] + total
                for lanes, down in ((slice(0, low), down_one), (slice(low, width), down_two)):
                    part = dot(value, matrix(down))
                    if not first:
                        part = part + acc[sl, lanes]
                    if not last:
                        acc[sl, lanes] = part
                    elif i == 0:
                        out_other[:, lanes] = part.astype(BF)
                    else:
                        out_own[:, lanes] = part
            for refs, left, right in ((two_refs, act_ref, joined), (one_refs, grad, hid_ref)):
                for j, lanes in ((near, slice(0, low)), (far, slice(low, width))):
                    value = dot(left[...], right[:, lanes], TN).astype(BF)
                    if len(refs) == 1:
                        refs[0][:, min(j, 3) // 2] = value.reshape(2, low // 2, low)
                    else:
                        refs[j][...] = value

        @pl.when(step == 0)
        def _():
            product(ug, ugy, dg, dgy, True, False, 0, 2)

        @pl.when(step == 1)
        def _():
            product(ug, ugy, dg, dgy, False, False, 0, 2)

        @pl.when(step == 2)
        def _():
            product(ugx, uga, dgx, dga, False, False, 1, 3)

        @pl.when(step == 3)
        def _():
            product(ugx, ugb, dgx, dgb, False, True, 1, 4)

    tiles = pl.BlockSpec((both, low), lambda t: (0, t))
    whole = shape_of((2 * low, low), BF)
    block_specs = weight_specs(low)
    block_shapes = [whole] * 3 + [shape_of((low, low), BF)] * 2
    z_specs = [pl.BlockSpec((2, 2, low // 2, low), lambda t: (t % 2, t // 2, 0, 0))]
    found = call(
        body,
        (4,),
        [fixed((rows, width))] * 2 + weight_specs(low, up_blocks) + weight_specs(low, down_blocks) + [tiles, tiles, fixed((both, width))],
        [pl.BlockSpec((8, low), lambda t: (0, t)), fixed((rows, width)), fixed((rows, width))]
        + (z_specs + block_specs if by_z else block_specs[:3] * 2 + [fixed((2, low, low))] * 2),
        [shape_of((8, hid), F32), shape_of((rows, width), F32), shape_of((rows, width), BF)]
        + ([shape_of((4, 4, low // 2, low), BF)] + block_shapes if by_z
           else [whole] * 6 + [shape_of((2, low, low), BF)] * 2),
        [pltpu.VMEM((both, width), BF), pltpu.VMEM((both, low), BF), pltpu.VMEM((both, width), F32)],
        8 * both * width * hid,
        8 * hid * width + 6 * both * width + 4 * both * hid + 6 * rows * width,
        (own, other, *up_blocks, *down_blocks, slope, act, hidden),
    )
    if by_z:
        return found[:3], found[3], found[4:]
    return found[:3], found[3:9], found[9:]


def fc_down(left, blocks):
    both, hid = left.shape
    rows, low = both // 2, hid // 4
    width = 2 * low

    def body(left_ref, g, gx, gy, ga, gb, own, other, acc):
        step = pl.program_id(0)

        def product(one, two, first, last):
            for i, sl in enumerate((slice(rows, both), slice(0, rows))):
                for lanes, right in ((slice(0, low), one), (slice(low, width), two)):
                    part = dot(left_ref[sl, :], matrix(right))
                    if not first:
                        part = part + acc[sl, lanes]
                    if not last:
                        acc[sl, lanes] = part
                    elif i == 0:
                        other[:, lanes] = part.astype(BF)
                    else:
                        own[:, lanes] = part

        @pl.when(step == 0)
        def _():
            product(g, gy, True, False)

        @pl.when(step == 1)
        def _():
            product(g, gy, False, False)

        @pl.when(step == 2)
        def _():
            product(gx, ga, False, False)

        @pl.when(step == 3)
        def _():
            product(gx, gb, False, True)

    return call(
        body,
        (4,),
        [pl.BlockSpec((both, low), lambda t: (0, t))] + weight_specs(low, blocks),
        [fixed((rows, width))] * 2,
        [shape_of((rows, width), F32), shape_of((rows, width), BF)],
        [pltpu.VMEM((both, width), F32)],
        2 * both * width * hid,
        2 * hid * width + 2 * both * hid + 6 * rows * width,
        (left, *blocks),
    )


def head_ones(size, head_width):
    first = lax.broadcasted_iota(jnp.int32, (size, size), 0) // head_width
    second = lax.broadcasted_iota(jnp.int32, (size, size), 1) // head_width
    return (first == second).astype(BF)


def qkv_up(own, other, blocks, vectors, ones):
    rows, width = own.shape
    low, both = width // 2, 2 * rows
    tile = low // 2

    def body(own_ref, other_ref, g, gx, gy, ga, gb, vec, ones_ref, joined, q_raw, k_raw, q_low, k_low, v_low, acc):
        step = pl.program_id(0)
        part = step % 3

        @pl.when(step == 0)
        def _():
            join_into(joined, own_ref, other_ref)

        def product(first, second):
            acc[...] = dot(joined[:, :low], first, NT) + dot(joined[:, low:], second, NT)

        @pl.when(step < 3)
        def _():
            product(g[...], gy[...])

        @pl.when(jnp.logical_and(step >= 3, part < 2))
        def _():
            product(gx[...], ga[...])

        @pl.when(step == 5)
        def _():
            product(gx[...], gb[...])

        def unit(value):
            square = dot((value * value).astype(BF), ones_ref[...])
            return value * lax.rsqrt(square + EPS_UNIT)

        @pl.when(part == 0)
        def _():
            def finish(sl):
                value = acc[sl, :] + vec[0:1, :]
                q_raw[sl, :] = value.astype(BF)
                q_low[sl, :] = (unit(value) * vec[2:3, :]).astype(BF)

            row_loop(both, both // 4, finish)

        @pl.when(part == 1)
        def _():
            def finish(sl):
                value = acc[sl, :]
                k_raw[sl, :] = value.astype(BF)
                k_low[sl, :] = unit(value).astype(BF)

            row_loop(both, both // 4, finish)

        @pl.when(part == 2)
        def _():
            v_low[...] = (acc[...] + vec[1:2, :]).astype(BF)

    half = lambda t: t // 3
    kept = pl.BlockSpec((both, tile), lambda t: (0, half(t)))
    heads = shape_of((both, low), BF)
    return call(
        body,
        (6,),
        [fixed((rows, width))] * 2
        + [
            pl.BlockSpec((tile, low), lambda t: (jnp.minimum(t, 2), 0)),
            pl.BlockSpec((tile, low), lambda t: (jnp.maximum(t - 3, 0), 0)),
            pl.BlockSpec((tile, low), lambda t: (jnp.minimum(t, 2), 0)),
            pl.BlockSpec((tile, low), lambda t: (jnp.clip(t - 3, 0, 1), 0)),
            fixed((tile, low)),
            pl.BlockSpec((8, tile), lambda t: (0, half(t))),
            fixed((tile, tile)),
        ],
        [fixed((both, width))] + [kept] * 5,
        [shape_of((both, width), BF)] + [heads] * 5,
        [pltpu.VMEM((both, tile), F32)],
        2 * both * width * 3 * low,
        2 * 3 * low * width + 6 * both * width + 10 * both * low,
        (own, other, *blocks, vectors, ones),
    )


def attn_mix(q_low, k_low, v_low, end_col, place_row, head_width):
    both, low = q_low.shape
    pair = 2 * head_width
    chunk = both // 4

    def body(q_ref, k_ref, v_ref, end_ref, place_ref, out_ref, rest_ref, log_ref):
        place = place_ref[0:1, :]
        lane = lax.broadcasted_iota(jnp.int32, (both, pair), 1)
        value = v_ref[...]
        ones = jnp.ones_like(value)
        wide = [
            jnp.concatenate((jnp.where(lane // head_width == h, value, ones), ones), axis=1) for h in range(2)
        ]
        first = lane[:chunk] < head_width
        for c in range(4):
            sl = slice(c * chunk, (c + 1) * chunk)
            queries = q_ref[sl, :]
            found = []
            for h in range(2):
                own = jnp.where(first if h == 0 else ~first, queries, jnp.zeros_like(queries))
                scores = dot(own, k_ref[...], NT)
                expo = jnp.where(place < end_ref[sl, :], jnp.exp(scores), 0.0).astype(BF)
                found.append(dot(expo, wide[h]))
            out = jnp.where(first, found[0][:, :pair] / found[0][:, pair:], found[1][:, :pair] / found[1][:, pair:])
            low_out = out.astype(BF)
            out_ref[sl, :] = low_out
            rest_ref[sl, :] = (out - low_out.astype(F32)).astype(BF)
            log_ref[sl, :] = jnp.log(jnp.where(first, found[1][:, pair:], found[0][:, pair:]))

    block = pl.BlockSpec((both, pair), lambda t: (0, t))
    return call(
        body,
        (low // pair,),
        [block] * 3 + [fixed((both, 1)), fixed((8, both))],
        [block] * 3,
        [shape_of((both, low), BF)] * 2 + [shape_of((both, low), F32)],
        [],
        4 * both * both * low,
        14 * both * low,
        (q_low, k_low, v_low, end_col, place_row),
    )


def attn_back(x, own, other, blocks, q_low, k_low, v_low, attn, rest, logs, q_raw, k_raw, hidden, scale_row,
              place_col, end_row, head_width, before=None):
    rows, width = own.shape
    both, low = q_low.shape
    pair = 2 * head_width
    chunk = both // 4
    first_call = before is None

    def body(own_ref, other_ref, *refs):
        w_refs, refs = refs[:8], refs[8:]
        (q_ref, k_ref, v_ref, attn_ref, rest_ref, log_ref, qr_ref, kr_ref, hid_ref, scale_ref, place_ref,
         end_ref), refs = refs[:12], refs[12:]
        if first_call:
            sums, total_ref, near_out, far_a, far_b = refs[:5]
            joined, weights, ds_ref, three_ref = refs[5:]
        else:
            before_ref, sums, out_own, out_other, near_out, far_out = refs[:6]
            joined, weights, ds_ref, three_ref, total_ref = refs[6:]
        step = pl.program_id(0)

        @pl.when(step == 0)
        def _():
            join_into(joined, own_ref, other_ref)

        for i in range(4):
            rows_i = slice(i * pair, (i + 1) * pair)
            weights[rows_i, :low] = w_refs[2 * i][...]
            weights[rows_i, low:] = w_refs[2 * i + 1][...]

        grad = dot(joined[...], weights[3 * pair :, :], NT).astype(BF)
        ends = end_ref[0:1, :]
        lane = lax.broadcasted_iota(jnp.int32, (both, pair), 1)
        inner = lane % head_width
        row_head = lax.broadcasted_iota(jnp.int32, (pair, pair), 0) // head_width
        lane_head = lax.broadcasted_iota(jnp.int32, (pair, pair), 1) // head_width
        same = (row_head == lane_head).astype(BF)
        swap = (row_head != lane_head).astype(BF)
        swap_twice = jnp.concatenate((swap, swap), axis=0)

        def spread(value):
            high = value.astype(BF)
            left = value - high.astype(F32)
            mid = left.astype(BF)
            small = (left - mid.astype(F32)).astype(BF)
            zero = jnp.zeros_like(high)
            return jnp.where(inner == 0, high, jnp.where(inner == 1, mid, jnp.where(inner == 2, small, zero)))

        def unit_back(raw, grad_unit):
            raw = raw.astype(F32)
            rate = lax.rsqrt(dot((raw * raw).astype(BF), same) + EPS_UNIT)
            unit = raw * rate
            cross = dot((grad_unit * unit).astype(BF), same)
            return rate * (grad_unit - unit * cross), unit

        product = grad.astype(F32) * (attn_ref[...].astype(F32) + rest_ref[...].astype(F32))
        high = product.astype(BF)
        small = (product - high.astype(F32)).astype(BF)
        delta = dot(jnp.concatenate((high, small), axis=1), swap_twice)
        log_terms, delta_terms = spread(-log_ref[...]), spread(-delta)
        queries, keys, values = q_ref[...], k_ref[...], v_ref[...]
        zero, one = jnp.zeros_like(keys), jnp.ones_like(keys)
        dk_parts, dv_parts = [None] * 4, [None] * 4
        d_qt = None
        for h in range(2):
            mine = lane // head_width == h
            q_own, g_own, k_own = [jnp.where(mine, v, zero) for v in (queries, grad, keys)]
            q_wide, g_wide = jnp.where(mine, queries, log_terms), jnp.where(mine, grad, delta_terms)
            k_wide, v_wide = jnp.where(mine, keys, one), jnp.where(mine, values, one)
            for c in range(4):
                sl = slice(c * chunk, (c + 1) * chunk)
                scores = dot(k_wide[sl], q_wide, NT)
                probs = jnp.where(place_ref[sl, :] < ends, jnp.exp(scores), 0.0)
                d_scores = (probs * dot(v_wide[sl], g_wide, NT)).astype(BF)
                ds_ref[sl, :] = d_scores
                d_v, d_k = dot(probs.astype(BF), g_own), dot(d_scores, q_own)
                dv_parts[c] = d_v if h == 0 else dv_parts[c] + d_v
                dk_parts[c] = d_k if h == 0 else dk_parts[c] + d_k
            part = dot(k_own, ds_ref[...], TN)
            d_qt = part if h == 0 else d_qt + part
        d_qn = d_qt.T
        d_q, unit_q = unit_back(qr_ref[...], d_qn * scale_ref[0:1, :])
        d_k, _ = unit_back(kr_ref[...], jnp.concatenate(dk_parts, axis=0))
        d_q, d_k, d_v = d_q.astype(BF), d_k.astype(BF), jnp.concatenate(dv_parts, axis=0).astype(BF)
        for i, value in enumerate((d_q, d_k, d_v)):
            three_ref[:, i * pair : (i + 1) * pair] = value
        for i, value in enumerate((d_q.astype(F32), d_v.astype(F32), d_qn * unit_q)):
            sums[i : i + 1, :] = jnp.sum(value, axis=0, keepdims=True)

        for lanes in (slice(0, low), slice(low, width)):
            part = dot(three_ref[...], weights[: 3 * pair, lanes])

            @pl.when(step == 0)
            def _():
                total_ref[:, lanes] = part if first_call else part + before_ref[:, lanes]

            @pl.when(step == 1)
            def _():
                total = total_ref[:, lanes] + part
                if first_call:
                    total_ref[:, lanes] = total
                else:
                    out_own[:, lanes] = total[:rows]
                    out_other[:, lanes] = total[rows:].astype(BF)

        for i, lanes in enumerate((slice(0, low), slice(low, width))):
            three = dot(three_ref[...], hid_ref[:, lanes], TN).astype(BF)
            proj = dot(attn_ref[...], joined[:, lanes], TN).astype(BF)
            grads = [three[j * pair : (j + 1) * pair] for j in range(3)] + [proj]
            for j in range(4):
                if i == 0:
                    near_out[j, 0] = grads[j]
                elif first_call:
                    (far_a if j < 2 else far_b)[j % 2, 0] = grads[j]
                else:
                    far_out[j, 0] = grads[j]

    w_specs, w_args = [], []
    for i in range(4):
        far_row = 2 * (i % 2) if x else 2 * i
        w_specs += [pl.BlockSpec((pair, low), lambda t, row=row: (row + t, 0)) for row in (2 * i, far_row)]
        w_args += [blocks[1], blocks[3 + i // 2]] if x else [blocks[0], blocks[2]]
    block = pl.BlockSpec((both, pair), lambda t: (0, 2 * x + t))
    row = pl.BlockSpec((8, pair), lambda t: (0, t))
    four = pl.BlockSpec((4, 1, pair, low), lambda t: (0, t, 0, 0))
    duo = pl.BlockSpec((2, 1, pair, low), lambda t: (0, t, 0, 0))
    whole, half = shape_of((4, 2, pair, low), BF), shape_of((2, 2, pair, low), BF)
    total = shape_of((both, width), F32)
    found = call(
        body,
        (2,),
        [fixed((rows, width))] * 2 + w_specs + [block] * 8
        + [fixed((both, width)), pl.BlockSpec((8, pair), lambda t: (0, 2 * x + t)), fixed((both, 1)), fixed((8, both))]
        + ([] if first_call else [fixed((both, width))]),
        [row] + ([fixed((both, width)), four, duo, duo] if first_call else [fixed((rows, width))] * 2 + [four] * 2),
        [shape_of((8, 2 * pair), F32)]
        + (
            [total, whole, half, half] if first_call
            else [shape_of((rows, width), F32), shape_of((rows, width), BF), whole, whole]
        ),
        [
            pltpu.VMEM((both, width), BF), pltpu.VMEM((4 * pair, width), BF), pltpu.VMEM((both, both), BF),
            pltpu.VMEM((both, 3 * pair), BF),
        ] + ([] if first_call else [pltpu.VMEM((both, width), F32)]),
        5 * both * both * low + 8 * both * width * low,
        12 * both * low + 8 * both * width,
        (own, other, *w_args, q_low, k_low, v_low, attn, rest, logs, q_raw, k_raw, hidden, scale_row,
         place_col, end_row) + (() if first_call else (before,)),
    )
    start = 2 if first_call else 3
    return found[:start], [v.reshape(-1, low) for v in found[start:]]


def attn_down(attn, blocks):
    both, low = attn.shape
    rows, width, tile = both // 2, 2 * low, low // 2

    def body(attn_ref, g, gx, gy, gb, own, other):
        for lanes, first, second in ((slice(0, low), g, gx), (slice(low, width), gy, gb)):
            value = dot(attn_ref[:, :tile], first[...]) + dot(attn_ref[:, tile:], second[...])
            own[:, lanes] = value[:rows]
            other[:, lanes] = value[rows:].astype(BF)

    last = pl.BlockSpec((tile, low), lambda t: (3, 0))
    return call(
        body,
        (1,),
        [fixed((both, low))] + [last] * 3 + [pl.BlockSpec((tile, low), lambda t: (1, 0))],
        [fixed((rows, width))] * 2,
        [shape_of((rows, width), F32), shape_of((rows, width), BF)],
        [],
        2 * both * width * low,
        2 * low * width + 2 * both * low + 6 * rows * width,
        (attn, *blocks[:3], blocks[4]),
    )


def mix(own, got, state, vectors, last):
    rows, width = own.shape
    part = rows // 2

    def body(own_ref, got_ref, state_ref, vec, branch_ref, next_ref, hid_ref):
        def one(sl):
            branch = own_ref[sl, :] + got_ref[sl, :].astype(F32) + vec[0:1, :]
            branch_ref[sl, :] = branch.astype(BF)
            value = state_ref[sl, :] + vec[1:2, :] * branch
            next_ref[sl, :] = value
            if last:
                hid_ref[sl, :] = value.astype(BF)
            else:
                mean = jnp.mean(value, axis=1, keepdims=True)
                spread = jnp.mean(value * value, axis=1, keepdims=True) - mean * mean
                normed = (value - mean) * lax.rsqrt(spread + EPS_NORM)
                hid_ref[sl, :] = (normed * vec[2:3, :] + vec[3:4, :]).astype(BF)

        row_loop(part, 16, one, unroll=11)

    block = pl.BlockSpec((part, width), lambda t: (t, 0))
    return call(
        body,
        (2,),
        [block] * 3 + [fixed((8, width))],
        [block] * 3,
        [shape_of((rows, width), BF), shape_of((rows, width), F32), shape_of((rows, width), BF)],
        [],
        20 * rows * width,
        18 * rows * width,
        (own, got, state, vectors),
    )


def mix_back(own, got, state, grad, branch, vectors):
    rows, width = own.shape
    part = rows // 2

    def body(own_ref, got_ref, state_ref, grad_ref, branch_ref, vec, next_ref, low_ref, sums):
        @pl.when(pl.program_id(0) == 0)
        def _():
            sums[...] = jnp.zeros_like(sums)

        def add(i, value):
            sums[8 * i : 8 * i + 8, :] += value[:8] + value[8:]

        def one(sl):
            d_hid = own_ref[sl, :] + got_ref[sl, :].astype(F32)
            value = state_ref[sl, :]
            mean = jnp.mean(value, axis=1, keepdims=True)
            spread = jnp.mean(value * value, axis=1, keepdims=True) - mean * mean
            rate = lax.rsqrt(spread + EPS_NORM)
            normed = (value - mean) * rate
            add(0, d_hid * normed)
            add(1, d_hid)
            d_norm = d_hid * vec[0:1, :]
            means = jnp.mean(d_norm, axis=1, keepdims=True)
            crosses = jnp.mean(d_norm * normed, axis=1, keepdims=True)
            total = grad_ref[sl, :] + rate * (d_norm - means - normed * crosses)
            next_ref[sl, :] = total
            add(2, total * branch_ref[sl, :].astype(F32))
            low = (total * vec[1:2, :]).astype(BF)
            low_ref[sl, :] = low
            add(3, low.astype(F32))

        row_loop(part, 16, one, unroll=11)

    block = pl.BlockSpec((part, width), lambda t: (t, 0))
    return call(
        body,
        (2,),
        [block] * 5 + [fixed((8, width))],
        [block] * 2 + [fixed((32, width))],
        [shape_of((rows, width), F32), shape_of((rows, width), BF), shape_of((32, width), F32)],
        [],
        30 * rows * width,
        20 * rows * width,
        (own, got, state, grad, branch, vectors),
    )


def tie(value, *others):
    return lax.optimization_barrier((value,) + others)[0]


def add_low(*values):
    return sum(v.astype(F32) for v in values).astype(BF)


def near_parts(pairs, got_a, got_b):
    half, low = got_a.shape[-2:]
    count = len(pairs)
    got_a, got_b = [v.reshape(count, half, low) for v in (got_a, got_b)]

    def body(*refs):
        ins, a_ref, b_ref, outs = refs[: 2 * count], refs[2 * count], refs[2 * count + 1], refs[2 * count + 2 :]
        for i in range(count):
            for j, got in ((2 * i, a_ref), (2 * i + 1, b_ref)):
                outs[j][...] = (ins[j][...].astype(F32) + got[i].astype(F32)).astype(BF)

    front = pl.BlockSpec((half, low), lambda t: (0, 0))
    back = pl.BlockSpec((half, low), lambda t: (1, 0))
    flat = [v for pair in pairs for v in pair]
    found = pl.pallas_call(
        body,
        grid=(1,),
        in_specs=[front, back] * count + [fixed(got_a.shape)] * 2,
        out_specs=[front, back] * count,
        out_shape=[shape_of(v.shape, BF) for v in flat],
        input_output_aliases={i: i for i in range(2 * count)},
        compiler_params=pltpu.CompilerParams(vmem_limit_bytes=VMEM_BYTES),
        cost_estimate=pl.CostEstimate(
            flops=2 * count * half * low, bytes_accessed=12 * count * half * low, transcendentals=0
        ),
    )(*flat, got_a, got_b)
    return [found[2 * i : 2 * i + 2] for i in range(count)]


def summed(keep, got_x, got_y, parts, z_size):
    total = add_low(keep, got_x, got_y)
    total = jnp.swapaxes(total.reshape(parts, z_size, -1, keep.shape[1]), 0, 1)
    return total.reshape(z_size, -1, keep.shape[1])


def over_z(total):
    return lax.psum_scatter(total, "z", scatter_dimension=0, tiled=False)


def eight_rows(*rows):
    rows = [r.reshape(1, -1) for r in rows]
    return jnp.concatenate(rows + [jnp.zeros_like(rows[0])] * (8 - len(rows)), axis=0)


def on_pair(
    hidden_in, cond, scale_sizes, w_ada, b_ada, w_qkv, b_qkv, head_scale,
    w_proj, b_proj, w_fc1, b_fc1, w_fc2, b_fc2, grad_out,
):
    y = lax.axis_index("y")
    core = lax.axis_index("core")
    z = lax.axis_index("z")
    x = lax.axis_index("x")
    layer_count = w_ada.shape[0]
    seq_row, width = cond.shape
    rows_dev = hidden_in.shape[0]
    rows_pad = -(-rows_dev // 32) * 32
    d_col = b_qkv.shape[2]
    head_width = d_col // head_scale.shape[1]
    y_size, z_size, x_size = (lax.axis_size(a) for a in ("y", "z", "x"))
    heads = z_size * x_size
    low = width // 2
    rows_d = w_qkv.shape[1]
    hid_dev = w_fc1.shape[2]
    hid_core = hid_dev // 2

    qkv_t = jnp.transpose(w_qkv, (0, 2, 3, 1)).reshape(layer_count, 3, 2, head_width, rows_d)
    qkv_t = jnp.transpose(qkv_t, (0, 2, 1, 3, 4)).reshape(layer_count, 6 * head_width, rows_d)
    fc1_t = jnp.transpose(w_fc1, (0, 2, 1))
    three, four = 3 * head_width, 4 * head_width
    halves = [
        jnp.concatenate(parts, axis=1)
        for parts in (
            (qkv_t[:, :three], w_proj[:, :head_width], fc1_t[:, :hid_core], w_fc2[:, :hid_core]),
            (qkv_t[:, three:], w_proj[:, head_width:], fc1_t[:, hid_core:], w_fc2[:, hid_core:]),
        )
    ]
    kept = jnp.where(core == 0, halves[0], halves[1])
    came = sibling(jnp.where(core == 0, halves[1], halves[0]))
    shards = jnp.concatenate(
        (jnp.where(core == 0, kept, came), jnp.where(core == 0, came, kept)), axis=2
    )
    cuts = (0, four, four + hid_core, four + 2 * hid_core)

    def z_gather(l, i):
        by_z = lax.all_gather(shards[l, cuts[i] : cuts[i + 1]], "z", axis=0, tiled=False)
        if i == 0:
            by_z = jnp.swapaxes(by_z.reshape(z_size, 4, head_width, low), 0, 1)
        return by_z.reshape(-1, low)

    def send(rows):
        return rows, across(rows, "x"), across(rows, "y")

    def send_on(state, then):
        _, by_x, by_y = state
        half = by_x.shape[0] // 2
        first, second, then = together(by_x[:half], by_y[half:], then)
        return (across(first, "y"), across(second, "x")), then

    def whole(state, halves):
        return (*state, *halves)

    def together(*values):
        return lax.optimization_barrier(values)

    late = shards[1, cuts[2] :]
    late_x, late_y = across(late, "x"), across(late, "y")
    chunks = [z_gather(l, i) for l in range(layer_count) for i in range(3)][:5]

    cond_low = jax.nn.silu(cond.astype(F32)).astype(BF)
    silu_rows = lax.all_gather(tie(cond_low, late), ("y", "core"), axis=0, tiled=True)
    late_x, late_y, silu_rows = together(late_x, late_y, silu_rows)
    late_far = across(late_x, "y")
    row = y * 2 + core
    silu_own = lax.dynamic_slice_in_dim(silu_rows, row * rows_d, rows_d, axis=1)
    seqs = silu_rows.shape[0]
    ada_size = layer_count * 6 * d_col
    part = dot(silu_own, jnp.transpose(w_ada, (1, 0, 2, 3)).reshape(rows_d, ada_size))
    part = part + jnp.where(row == 0, b_ada.astype(F32).reshape(1, ada_size), 0.0)
    smalls = (b_qkv, b_fc1, b_proj, b_fc2, head_scale)
    sizes = [v.size for v in smalls]
    offs = [sum(sizes[:i]) for i in range(6)]
    n_rows = y_size * 2
    quarter = -(-offs[5] // (n_rows * 128)) * 128
    small = jnp.concatenate([v.reshape(-1).astype(F32) for v in smalls])
    small = jnp.pad(small, (0, n_rows * quarter - offs[5])).reshape(n_rows, quarter)
    small = lax.dynamic_index_in_dim(small, row, axis=0, keepdims=True)
    part = jnp.concatenate((part, jnp.broadcast_to(small, (seqs, quarter))), axis=1)
    to_all = jnp.swapaxes(part.reshape(y_size, x_size, z_size, -1), 1, 2)
    to_all = jnp.broadcast_to(to_all[:, None], (y_size, 2) + to_all.shape[1:])
    from_all = lax.all_to_all(
        tie(to_all.reshape(n_rows * z_size * x_size, -1), chunks[0]), ("y", "core", "z", "x"),
        split_axis=0, concat_axis=0, tiled=True,
    ).reshape(n_rows, z_size, x_size, -1)
    *sent, from_all = together(*send(tie(chunks[0], late_far, late_y)), from_all)
    late_blocks = lax.all_gather(
        tie(jnp.stack((late, late_y, late_x, late_far)), *sent), "z", axis=0, tiled=False
    )
    halves, from_all = send_on(sent, from_all)
    ada = jnp.sum(from_all[..., :ada_size], axis=0).reshape(z_size * x_size, layer_count, 6, d_col)
    ada = turned(jnp.transpose(ada, (1, 2, 0, 3)).reshape(layer_count, 6, width), y, 2)
    small = jnp.transpose(from_all[..., ada_size:], (1, 2, 0, 3)).reshape(z_size, x_size, -1)
    s_qkv, s_fc1, s_proj, s_fc2, s_scale = [small[:, :, offs[i] : offs[i + 1]] for i in range(5)]

    def by_core(values, shape, axis):
        values = values.reshape((z_size, x_size) + shape)
        values = lax.dynamic_index_in_dim(values, core, axis=axis, keepdims=False)
        return turned(jnp.swapaxes(values, 0, 1), x, 0)

    def by_d(values):
        values = jnp.swapaxes(values.reshape(z_size * x_size, layer_count, d_col), 0, 1)
        return turned(values.reshape(layer_count, width), y, 1)

    bias_qkv = by_core(s_qkv, (layer_count, 2, 2, head_width), 4)
    bias_qkv = jnp.transpose(bias_qkv, (2, 3, 0, 1, 4)).reshape(layer_count, 2, low)
    scales = by_core(s_scale, (layer_count, 2), 3)
    scales = jnp.transpose(scales, (2, 0, 1)).reshape(layer_count, heads)
    scales = jnp.repeat(scales, head_width, axis=1)
    bias_fc1 = by_core(s_fc1, (layer_count, 2, hid_core), 3)
    bias_fc1 = jnp.transpose(bias_fc1, (2, 0, 1, 3)).reshape(layer_count, 1, -1)
    bias_proj, bias_fc2 = by_d(s_proj), by_d(s_fc2)

    sizes_f = scale_sizes.astype(F32)
    sizes_f = jnp.where(core == x, sizes_f, sibling(sizes_f))
    own_sizes = lax.dynamic_index_in_dim(sizes_f, z, axis=0, keepdims=False).astype(jnp.int32)
    index = jnp.arange(rows_pad, dtype=jnp.int32)
    places = jnp.concatenate((core * rows_dev + index, (1 - core) * rows_dev + index))
    starts = jnp.cumsum(own_sizes) - own_sizes
    ends = jnp.sum(jnp.where(starts[None, :] <= places[:, None], own_sizes[None, :], 0), axis=1)
    real = jnp.concatenate((index, index)) < rows_dev
    key_places = jnp.where(real, places, 1 << 20).astype(F32)
    ends = ends.astype(F32)
    place_col, end_col = key_places[:, None], ends[:, None]
    place_row, end_row = eight_rows(key_places), eight_rows(ends)
    ones = head_ones(low // 2, head_width)

    def own_tokens(values):
        return jnp.pad(turned(trade(values, core != x), y, 1), ((0, rows_pad - rows_dev), (0, 0)))

    state = own_tokens(tie(hidden_in, silu_rows)).astype(F32)
    hidden = (normalize(state)[0] * (1.0 + ada[0, 2][None]) + ada[0, 4][None]).astype(BF)
    weights = [None] * 5 + [(late_blocks,) * 5]

    def attn_start(l, hidden):
        vectors = eight_rows(bias_qkv[l, 0], bias_qkv[l, 1], scales[l])
        found = qkv_up(hidden, sibling(hidden), weights[3 * l], vectors, ones)
        return found

    def attn_end(l, attn, state):
        own, send_own = attn_down(attn, weights[3 * l])
        branch, middle, hidden = mix(
            own, sibling(send_own), state,
            eight_rows(bias_proj[l], ada[l, 0], 1.0 + ada[l, 3], ada[l, 5]), False,
        )
        return branch, middle, hidden

    def fc_start(l, hidden):
        return fc_up(hidden, sibling(hidden), weights[3 * l + 1], bias_fc1[l])

    def fc_end(l, act, middle):
        own, send_own = fc_down(act, weights[3 * l + 2])
        last = l == layer_count - 1
        after = ada[l if last else l + 1]
        return mix(
            own, sibling(send_own), middle,
            eight_rows(bias_fc2[l], ada[l, 1], 1.0 + after[2], after[4]), last,
        )

    *halves, chunks[1], hidden = together(*halves, chunks[1], hidden)
    weights[0], sent = whole(sent, halves), send(chunks[1])
    found0 = attn_start(0, hidden)
    attn0, rest0, logs0 = attn_mix(*found0[3:6], end_col, place_row, head_width)
    *sent, attn0 = together(*sent, attn0)
    halves, attn0 = send_on(sent, attn0)
    branch0, middle0, hidden2 = attn_end(0, attn0, state)
    *halves, chunks[2], hidden2 = together(*halves, chunks[2], hidden2)
    weights[1], sent = whole(sent, halves), send(chunks[2])
    joined2, act, slope = fc_start(0, hidden2)
    *sent, act = together(*sent, act)
    halves, act = send_on(sent, act)
    *halves, chunks[3], act = together(*halves, chunks[3], act)
    weights[2], sent = whole(sent, halves), send(chunks[3])
    feed, state1, hidden = fc_end(0, act, middle0)
    saved = [(*found0, logs0, attn0, rest0, branch0, middle0, joined2, act, slope, feed, state)]
    *sent, hidden = together(*sent, hidden)
    halves, hidden = send_on(sent, hidden)
    *halves, chunks[4], hidden = together(*halves, chunks[4], hidden)
    weights[3], sent = whole(sent, halves), send(chunks[4])
    found1 = attn_start(1, hidden)
    attn1, rest1, logs1 = attn_mix(*found1[3:6], end_col, place_row, head_width)
    *sent, attn1 = together(*sent, attn1)
    halves, attn1 = send_on(sent, attn1)
    branch1, middle1, hidden2 = attn_end(1, attn1, state1)
    *halves, hidden2, grad_out = together(*halves, hidden2, grad_out)
    weights[4] = whole(sent, halves)
    grad = own_tokens(grad_out).astype(F32)
    joined2, act, slope = fc_start(1, hidden2)
    feed, state2, mixed = fc_end(1, act, middle1)
    mixed, grad = together(mixed, grad)
    saved.append((*found1, logs1, attn1, rest1, branch1, middle1, joined2, act, slope, feed, state1))

    top = layer_count - 1
    d_ada = [[None] * 6 for _ in range(layer_count)]
    d_biases = [[None] * 5 for _ in range(layer_count)]
    d_weights = [None] * layer_count
    fold = lambda sums: jnp.sum(sums.reshape(-1, 8, sums.shape[1]), axis=1)
    d_low = (grad * ada[top, 1][None]).astype(BF)
    d_ada[top][1] = jnp.sum(grad * saved[1][-2].astype(F32), axis=0)
    d_biases[top][1] = jnp.sum(d_low.astype(F32), axis=0)
    def fc_turn(l, d_low):
        act, slope, joined2 = saved[l][-4], saved[l][-3], saved[l][-5]
        return fc_back(
            d_low, sibling(d_low), weights[3 * l + 2], weights[3 * l + 1], slope, act, joined2, l == 1
        )

    def fc_norm(l, sums_pre, own, got_own, grad):
        d_middle, d_low, sums = mix_back(
            own, got_own, saved[l][10], grad, saved[l][9], eight_rows(1.0 + ada[l, 3], ada[l, 0])
        )
        d_ada[l][3], d_ada[l][5], d_ada[l][0], d_biases[l][0] = fold(sums)
        d_biases[l][3] = fold(sums_pre)[0]
        return d_middle, d_low

    def attn_turn(x, l, d_low, d_other, before=None):
        joined1, q_raw, k_raw, q_low, k_low, v_low, logs, attn, rest = saved[l][:9]
        return attn_back(
            x, d_low, d_other, weights[3 * l], q_low, k_low, v_low, attn, rest, logs, q_raw, k_raw, joined1,
            eight_rows(scales[l]), place_col, end_row, head_width, before,
        )

    def attn_norm(l, sums_one, found, got_own, d_middle):
        sums_qkv, own = found
        sums_qkv = jnp.concatenate((sums_qkv, sums_one), axis=1)
        before = max(l - 1, 0)
        grad, d_low, sums = mix_back(
            own, got_own, saved[l][-1], d_middle, saved[before][-2],
            eight_rows(1.0 + ada[l, 2], ada[before, 1]),
        )
        sums = fold(sums)
        d_ada[l][2], d_ada[l][4] = sums[0], sums[1]
        if l > 0:
            d_ada[l - 1][1], d_biases[l - 1][1] = sums[2], sums[3]
        d_biases[l][2] = sums_qkv[:2]
        d_biases[l][4] = jnp.sum(sums_qkv[2].reshape(heads, head_width), axis=1)
        return grad, d_low

    def given_back(values):
        return trade(turned(values[:rows_dev], y, 1).astype(BF), core != x)

    def halves_out(parts):
        return across(parts[-2], "y"), across(parts[-1], "x")

    def near_out(pair):
        return across(pair[0], "x"), across(pair[1], "y")

    (sums_pre, own, send_own), two, one = fc_turn(1, d_low)
    z_two = over_z(two)
    got = halves_out(one)
    d_middle, d_low = fc_norm(1, sums_pre, own, sibling(send_own), grad)
    *got, d_low = together(*got, d_low)
    near = near_out(near_parts([one[1:3]], *got)[0])

    d_other = sibling(d_low)
    (sums_one, total), last_x = attn_turn(1, 1, d_low, d_other)
    near_a, near_b, total, *last_x = together(*near, total, *last_x)
    got = halves_out(last_x)
    sum_one, total = together(summed(one[0], near_a, near_b, 1, z_size), total)
    (sums_two, own, send_own), last = attn_turn(0, 1, d_low, d_other, total)
    *got, send_own = together(*got, send_own)
    pair = near_parts([(last_x[0], last[1])], *got)[0]
    *pair, send_own = together(*pair, send_own)
    near = near_out(pair)
    grad, d_low = attn_norm(1, sums_one, (sums_two, own), sibling(send_own), d_middle)
    z_two, d_low = together(z_two, d_low)
    g_one1 = over_z(sum_one)

    (sums_pre, own, send_own), blocks, far = fc_turn(0, d_low)
    near_a, near_b, send_own = together(*near, send_own)
    got = across(far[0], "y"), across(far[1], "x")
    d_middle, d_low = fc_norm(0, sums_pre, own, sibling(send_own), grad)
    sum_attn, d_low = together(summed(last[0], near_a, near_b, 4, z_size), d_low)
    g_attn1 = over_z(sum_attn)
    d_other = sibling(d_low)
    (sums_one, total), last_x = attn_turn(1, 0, d_low, d_other)
    *got, total, last_a, last_b, last_c, g_one1 = together(*got, total, *last_x, g_one1)
    last_x = (last_a, last_b, last_c)
    one, two = near_parts([blocks[4:6], blocks[1:3]], *got)
    *one, total = together(*one, total)
    near_one, near_two = near_out(one), near_out(two)
    (sums_two, own, send_own), last = attn_turn(0, 0, d_low, d_other, total)
    near_a, near_b, send_own, g_attn1 = together(*near_one, send_own, g_attn1)
    got = halves_out(last_x)
    sum_one, send_own = together(summed(blocks[3], near_a, near_b, 1, z_size), send_own)
    g_one0 = over_z(sum_one)
    grad, d_low = attn_norm(0, sums_one, (sums_two, own), sibling(send_own), d_middle)
    near_a, near_b, grad = together(*near_two, grad)
    sum_two, *got = together(summed(blocks[0], near_a, near_b, 1, z_size), *got)
    g_two0 = over_z(sum_two)
    near = near_out(near_parts([(last_x[0], last[1])], *got)[0])
    *near, z_two, mixed = together(*near, z_two, mixed)
    g_attn0 = over_z(summed(last[0], *near, 4, z_size))
    late_far, late_y = across(z_two[3], "y"), across(z_two[1], "y")
    mixed, grad_in = given_back(mixed), given_back(grad).astype(F32)
    late_x = across(add_low(z_two[2], late_far), "x")
    g_two1 = add_low(z_two[0], late_x, late_y)

    def by_col(values):
        values = turned(values, y, values.ndim - 1)
        values = values.reshape(values.shape[:-1] + (z_size, x_size, d_col))
        return jnp.moveaxis(values, (-3, -2), (0, 1)).reshape(z_size, x_size, -1)

    def by_hidden(values):
        return jnp.swapaxes(turned(values, x, 0), 0, 1).reshape(z_size, x_size, -1)

    packs = [by_col(jnp.stack([jnp.stack(v) for v in d_ada]))]
    for l in range(layer_count):
        db_proj, db_fc2, db_qkv, db_fc1, d_head = d_biases[l]
        packs.append(by_col(db_proj))
        packs.append(by_col(db_fc2))
        packs.append(by_hidden(jnp.moveaxis(db_qkv.reshape(2, x_size, z_size, head_width), 0, 2)))
        packs.append(by_hidden(db_fc1.reshape(x_size, z_size, hid_core)))
        packs.append(by_hidden(d_head.reshape(x_size, z_size, 1)))
    lens = [p.shape[2] for p in packs]
    pack = jnp.concatenate(packs, axis=2)
    pack = jnp.broadcast_to(pack[None], (n_rows,) + pack.shape)
    got = lax.all_to_all(
        pack.reshape(n_rows * z_size * x_size, -1), ("y", "core", "z", "x"),
        split_axis=0, concat_axis=0, tiled=True,
    ).reshape(y_size, 2, z_size, x_size, -1)
    pos = lens[0]
    d_ada_all = jnp.sum(got[..., :pos], axis=1)
    d_ada_all = jnp.swapaxes(d_ada_all, 1, 2).reshape(seqs, -1).astype(BF)
    out_b_ada = jnp.sum(d_ada_all.astype(F32), axis=0).reshape(layer_count, 6, d_col)
    out_w_ada = dot(silu_own, d_ada_all, TN).reshape(rows_d, layer_count, 6, d_col)
    out_w_ada = jnp.swapaxes(out_w_ada, 0, 1)
    sums = jnp.sum(got[..., pos:], axis=(0, 2, 3))
    outs = [[] for _ in range(5)]
    pos = 0
    for l in range(layer_count):
        for i in range(5):
            count = lens[1 + 5 * l + i]
            outs[i].append(sums[:, pos : pos + count])
            pos += count
    out_b_proj = jnp.stack([v[0] + v[1] for v in outs[0]])
    out_b_fc2 = jnp.stack([v[0] + v[1] for v in outs[1]])
    out_b_qkv = jnp.stack(
        [jnp.swapaxes(v.reshape(2, 2, head_width), 0, 1).reshape(2, d_col) for v in outs[2]]
    )
    out_b_fc1 = jnp.stack([v.reshape(-1) for v in outs[3]])
    out_scale = jnp.stack([v.reshape(-1) for v in outs[4]])

    def both_cores(own):
        kept = jnp.where(core == 0, own[:, :, :rows_d], own[:, :, rows_d:])
        came = sibling(jnp.where(core == 0, own[:, :, rows_d:], own[:, :, :rows_d]))
        return jnp.where(core == 0, kept, came).astype(F32), jnp.where(core == 0, came, kept).astype(F32)

    fc_first, fc_second = both_cores(
        jnp.stack((jnp.concatenate((g_one0, g_two0)), jnp.concatenate((g_one1, g_two1))))
    )
    out_w_fc1 = jnp.swapaxes(jnp.concatenate((fc_first[:, :hid_core], fc_second[:, :hid_core]), axis=1), 1, 2)
    out_w_fc2 = jnp.concatenate((fc_first[:, hid_core:], fc_second[:, hid_core:]), axis=1)
    own, out_w_fc1, out_w_fc2, out_w_ada = together(jnp.stack((g_attn0, g_attn1)), out_w_fc1, out_w_fc2, out_w_ada)
    first, second = both_cores(own)
    wq = jnp.stack((first[:, :three], second[:, :three]), axis=1)
    wq = wq.reshape(layer_count, 2, 3, head_width, rows_d)
    out_w_qkv = jnp.transpose(wq, (0, 4, 2, 1, 3)).reshape(layer_count, rows_d, 3, d_col)
    out_w_proj = jnp.concatenate((first[:, three:], second[:, three:]), axis=1)

    return (
        mixed, grad_in, out_w_ada, out_b_ada, out_w_qkv, out_b_qkv, out_scale,
        out_w_proj, out_b_proj, out_w_fc1, out_b_fc1, out_w_fc2, out_b_fc2,
    )


def solution(mesh):
    rows, cols = mesh.devices.shape
    row, col, body, used = ("row",), ("col",), on_device, mesh
    if rows == 4 and cols == 8:
        used = jax.sharding.Mesh(
            mesh.devices.reshape(rows // 2, 2, cols // 2, 2), ("y", "core", "z", "x")
        )
        row, col, body = ("y", "core"), ("z", "x"), on_pair
    tokens = P(row + col, None)
    out_weights = (
        P(None, row, None, col),
        P(None, None, col),
        P(None, row, None, col),
        P(None, None, col),
        P(None, col),
        P(None, col, row),
        P(None, col),
        P(None, row, col),
        P(None, col),
        P(None, col, row),
        P(None, col),
    )
    return jax.shard_map(
        body,
        mesh=used,
        in_specs=(tokens, P(row, None), P(row, None)) + out_weights + (tokens,),
        out_specs=(tokens, tokens) + out_weights,
        check_vma=False,
    )
```

```python
import jax
import jax.numpy as jnp
from jax import lax
from jax.experimental import pallas as pl
from jax.experimental.pallas import tpu as pltpu
from jax.sharding import PartitionSpec as P

HIGH = lax.Precision.HIGHEST
EPS_NORM = 1e-06
EPS_UNIT = 1e-06
NEG_FILL = -1e30


def block_ends(scale_sizes, seq_len):
    ends = jnp.cumsum(scale_sizes, axis=1)
    starts = ends - scale_sizes
    position = jnp.arange(seq_len, dtype=jnp.int32)
    picked = jnp.where(starts[:, None, :] <= position[None, :, None], scale_sizes[:, None, :], 0)
    return jnp.sum(picked, axis=2)


def normalize(values):
    center = jnp.mean(values, axis=-1, keepdims=True)
    spread = jnp.mean(values * values, axis=-1, keepdims=True) - center * center
    rstd = lax.rsqrt(spread + EPS_NORM)
    return ((values - center) * rstd, rstd)


def norm_back(grad_normed, normed, rstd):
    means = jnp.mean(grad_normed, axis=-1, keepdims=True)
    crosses = jnp.mean(grad_normed * normed, axis=-1, keepdims=True)
    return rstd * (grad_normed - means - normed * crosses)


def unit_pair(queries, key_rows, scale_here):
    q_norm = (
        queries
        * lax.rsqrt(jnp.sum(queries * queries, axis=-1, keepdims=True) + EPS_UNIT)
        * scale_here[:, None]
    )
    k_norm = key_rows * lax.rsqrt(jnp.sum(key_rows * key_rows, axis=-1, keepdims=True) + EPS_UNIT)
    return (q_norm, k_norm)


def project_in(hidden_low, weight):
    return (
        jnp.dot(
            lax.all_gather(hidden_low, "col", axis=0, tiled=True),
            weight,
            preferred_element_type=jnp.float32,
        ),
        hidden_low,
    )


def back_in(grad_three, kept, weight, whole_weight):
    tok_row = grad_three.shape[0]
    grad_low = grad_three.reshape(tok_row, grad_three.shape[1] * grad_three.shape[2])
    own_grads = lax.all_to_all(grad_three, "col", split_axis=0, concat_axis=2, tiled=True)
    grad_hidden = lax.dot_general(
        own_grads, whole_weight, (((1, 2), (1, 2)), ((), ())), preferred_element_type=jnp.float32
    )

    def add_piece(total, piece, start):
        return lax.dot_general(
            piece, grad_low, (((0,), (0,)), ((), ())), preferred_element_type=jnp.float32
        )

    init = jnp.zeros(weight.shape, jnp.float32)
    grad_weight = add_piece(init, lax.all_gather(kept, "col", axis=0, tiled=True), jnp.int32(0))
    return (grad_hidden, grad_weight)


def project_out(act_low, whole_weight):
    own_rows = lax.all_to_all(act_low, "col", split_axis=0, concat_axis=1, tiled=True)
    return jnp.dot(own_rows, whole_weight, preferred_element_type=jnp.float32)


def back_out(grad_low, act_low, weight):

    def add_piece(carry, piece, start):
        part = lax.dot_general(
            piece, weight, (((1,), (1,)), ((), ())), preferred_element_type=jnp.float32
        )
        grad_weight = lax.dot_general(
            act_low, piece, (((0,), (0,)), ((), ())), preferred_element_type=jnp.float32
        )
        return (part, grad_weight)

    init = (
        jnp.zeros((act_low.shape[0], weight.shape[0]), jnp.float32),
        jnp.zeros(weight.shape, jnp.float32),
    )
    return add_piece(init, lax.all_gather(grad_low, "col", axis=0, tiled=True), jnp.int32(0))


def masked_scores(q_rows, k_rows, ends):
    position = jnp.arange(k_rows.shape[0], dtype=jnp.int32)
    scores = jnp.einsum("the,she->hts", q_rows, k_rows, preferred_element_type=jnp.float32)
    visible = position[None, :] < ends[:, None]
    return jnp.where(visible[None], scores, NEG_FILL)


def attend(pieces):
    q_rows, k_rows, v_rows, ends = pieces
    scores = masked_scores(q_rows, k_rows, ends)
    top = jnp.max(scores, axis=-1, keepdims=True)
    expo = jnp.exp(scores - top)
    total = jnp.sum(expo, axis=-1, keepdims=True)
    probs = (expo / total).astype(jnp.bfloat16)
    attended = jnp.einsum("hts,she->the", probs, v_rows, preferred_element_type=jnp.float32)
    return (attended, (top + jnp.log(total))[..., 0])


def attend_back(pieces):
    q_rows, k_rows, v_rows, ends, log_total, grad_rows = pieces
    scores = masked_scores(q_rows, k_rows, ends)
    probs = jnp.exp(scores - log_total[..., None])
    grad_probs = jnp.einsum("the,she->hts", grad_rows, v_rows, preferred_element_type=jnp.float32)
    delta = jnp.sum(probs * grad_probs, axis=-1, keepdims=True)
    grad_scores = (probs * (grad_probs - delta)).astype(jnp.bfloat16)
    grad_q = jnp.einsum("hts,she->the", grad_scores, k_rows, preferred_element_type=jnp.float32)
    grad_k = jnp.einsum("hts,the->she", grad_scores, q_rows, preferred_element_type=jnp.float32)
    grad_v = jnp.einsum(
        "hts,the->she", probs.astype(jnp.bfloat16), grad_rows, preferred_element_type=jnp.float32
    )
    return (grad_q, grad_k, grad_v)


def gelu_tanh(values):
    return jax.nn.gelu(values, approximate=True)


def on_device(
    hidden_in,
    cond,
    scale_sizes,
    w_ada,
    b_ada,
    w_qkv,
    b_qkv,
    head_scale,
    w_proj,
    b_proj,
    w_fc1,
    b_fc1,
    w_fc2,
    b_fc2,
    grad_out,
):
    seq_row, width = cond.shape
    rows_dev = hidden_in.shape[0]
    tok_row = rows_dev * lax.axis_size("col")
    seq_len = tok_row // seq_row
    layer_count = w_ada.shape[0]
    d_col = b_qkv.shape[2]
    heads_dev = head_scale.shape[1]
    head_width = d_col // heads_dev
    full_ada, full_qkv, full_fc1, full_proj, full_fc2 = (
        lax.all_gather(w_ada, "row", axis=1, tiled=True),
        lax.all_gather(w_qkv, "row", axis=1, tiled=True),
        lax.all_gather(w_fc1, "row", axis=1, tiled=True),
        lax.all_gather(w_proj, "row", axis=2, tiled=True),
        lax.all_gather(w_fc2, "row", axis=2, tiled=True),
    )
    whole_proj, whole_fc2, whole_qkv, whole_fc1 = (
        lax.all_gather(full_proj, "col", axis=1, tiled=True),
        lax.all_gather(full_fc2, "col", axis=1, tiled=True),
        lax.all_gather(full_qkv, "col", axis=3, tiled=True),
        lax.all_gather(full_fc1, "col", axis=2, tiled=True),
    )
    ends = block_ends(scale_sizes, seq_len)
    silu_low = jax.nn.silu(cond.astype(jnp.float32)).astype(jnp.bfloat16)
    places = lax.axis_index("col") * rows_dev + jnp.arange(rows_dev, dtype=jnp.int32)
    member = (places[:, None] // seq_len == jnp.arange(seq_row, dtype=jnp.int32)[None, :]).astype(
        jnp.float32
    )

    def per_token(values):
        return jnp.dot(member, values, precision=HIGH)

    def per_sequence(values):
        return lax.dot_general(member, values, (((0,), (0,)), ((), ())), precision=HIGH)

    ada_parts = []
    for layer_index in range(layer_count):
        part = jnp.dot(
            silu_low,
            full_ada[layer_index].reshape(width, 6 * d_col),
            preferred_element_type=jnp.float32,
        )
        ada_parts.append(
            part.reshape(seq_row, 6, d_col) + b_ada[layer_index].astype(jnp.float32)[None]
        )
    ada_full, bias_proj_full, bias_fc2_full = (
        lax.all_gather(jnp.stack(ada_parts), "col", axis=3, tiled=True),
        lax.all_gather(b_proj.astype(jnp.float32), "col", axis=1, tiled=True),
        lax.all_gather(b_fc2.astype(jnp.float32), "col", axis=1, tiled=True),
    )
    current = hidden_in.astype(jnp.float32)
    saved = []
    for layer_index in range(layer_count):
        ada = ada_full[layer_index]
        gamma1, gamma2, scale1, scale2, shift1, shift2 = [
            per_token(ada[:, index]) for index in range(6)
        ]
        normed1, rstd1 = normalize(current)
        hidden1 = (normed1 * (1.0 + scale1) + shift1).astype(jnp.bfloat16)
        mixed_qkv, kept1 = project_in(hidden1, full_qkv[layer_index].reshape(width, 3 * d_col))
        bias_two = b_qkv[layer_index].astype(jnp.float32)
        bias_three = jnp.stack((bias_two[0], jnp.zeros_like(bias_two[0]), bias_two[1]))
        mixed_qkv = mixed_qkv + bias_three.reshape(1, 3 * d_col)
        split = mixed_qkv.reshape(seq_row, seq_len, 3, heads_dev, head_width)
        queries, key_rows, value_rows = (split[:, :, 0], split[:, :, 1], split[:, :, 2])
        scale_here = head_scale[layer_index].astype(jnp.float32)
        q_norm, k_norm = unit_pair(queries, key_rows, scale_here)
        q_low = q_norm.astype(jnp.bfloat16)
        k_low = k_norm.astype(jnp.bfloat16)
        v_low = value_rows.astype(jnp.bfloat16)
        attended, log_total = lax.map(attend, (q_low, k_low, v_low, ends))
        attn_low = attended.reshape(tok_row, d_col).astype(jnp.bfloat16)
        branch = project_out(attn_low, whole_proj[layer_index]) + bias_proj_full[layer_index][None]
        middle = current + gamma1 * branch
        normed2, rstd2 = normalize(middle)
        hidden2 = (normed2 * (1.0 + scale2) + shift2).astype(jnp.bfloat16)
        pre_act, kept2 = project_in(hidden2, full_fc1[layer_index])
        pre_act = pre_act + b_fc1[layer_index].astype(jnp.float32)[None]
        act_low = gelu_tanh(pre_act).astype(jnp.bfloat16)
        feed = project_out(act_low, whole_fc2[layer_index]) + bias_fc2_full[layer_index][None]
        saved.append(
            (
                normed1,
                rstd1,
                kept1,
                queries,
                key_rows,
                scale_here,
                q_low,
                k_low,
                v_low,
                log_total,
                attn_low,
                branch,
                normed2,
                rstd2,
                kept2,
                pre_act,
                act_low,
                feed,
            )
        )
        current = middle + gamma2 * feed
    mixed = current.astype(jnp.bfloat16)
    grad_state = grad_out.astype(jnp.float32)
    grads_ada = [None] * layer_count
    grads_w_qkv = [None] * layer_count
    grads_b_qkv = [None] * layer_count
    grads_scale = [None] * layer_count
    grads_w_proj = [None] * layer_count
    grads_b_proj = [None] * layer_count
    grads_w_fc1 = [None] * layer_count
    grads_b_fc1 = [None] * layer_count
    grads_w_fc2 = [None] * layer_count
    grads_b_fc2 = [None] * layer_count
    for layer_index in reversed(range(layer_count)):
        (
            normed1,
            rstd1,
            kept1,
            queries,
            key_rows,
            scale_here,
            q_low,
            k_low,
            v_low,
            log_total,
            attn_low,
            branch,
            normed2,
            rstd2,
            kept2,
            pre_act,
            act_low,
            feed,
        ) = saved[layer_index]
        ada = ada_full[layer_index]
        gamma1, gamma2, scale1, scale2, shift1, shift2 = [
            per_token(ada[:, index]) for index in range(6)
        ]
        d_gamma2 = per_sequence(grad_state * feed)
        grad_feed = (grad_state * gamma2).astype(jnp.bfloat16)
        grads_b_fc2[layer_index] = jnp.sum(grad_feed.astype(jnp.float32), axis=0)
        grad_act, grads_w_fc2[layer_index] = back_out(grad_feed, act_low, full_fc2[layer_index])
        gelu_pull = jax.vjp(gelu_tanh, pre_act)[1]
        grad_pre = gelu_pull(grad_act)[0].astype(jnp.bfloat16)
        grads_b_fc1[layer_index] = jnp.sum(grad_pre.astype(jnp.float32), axis=0)
        whole_one = whole_fc1[layer_index].reshape(width, 1, whole_fc1.shape[2])
        grad_hidden2, grads_w_fc1[layer_index] = back_in(
            grad_pre.reshape(tok_row, 1, grad_pre.shape[1]), kept2, full_fc1[layer_index], whole_one
        )
        d_scale2 = per_sequence(grad_hidden2 * normed2)
        d_shift2 = per_sequence(grad_hidden2)
        grad_middle = grad_state + norm_back(grad_hidden2 * (1.0 + scale2), normed2, rstd2)
        d_gamma1 = per_sequence(grad_middle * branch)
        grad_branch = (grad_middle * gamma1).astype(jnp.bfloat16)
        grads_b_proj[layer_index] = jnp.sum(grad_branch.astype(jnp.float32), axis=0)
        grad_attn, grads_w_proj[layer_index] = back_out(
            grad_branch, attn_low, full_proj[layer_index]
        )
        grad_attn_low = grad_attn.astype(jnp.bfloat16).reshape(
            seq_row, seq_len, heads_dev, head_width
        )
        grad_qn, grad_kn, grad_v = lax.map(
            attend_back, (q_low, k_low, v_low, ends, log_total, grad_attn_low)
        )
        unit_pull = jax.vjp(unit_pair, queries, key_rows, scale_here)[1]
        grad_q, grad_k, grads_scale[layer_index] = unit_pull((grad_qn, grad_kn))
        grad_qkv = (
            jnp.stack((grad_q, grad_k, grad_v), axis=2)
            .reshape(tok_row, 3, d_col)
            .astype(jnp.bfloat16)
        )
        bias_sums = jnp.sum(grad_qkv.astype(jnp.float32), axis=0)
        grads_b_qkv[layer_index] = jnp.stack((bias_sums[0], bias_sums[2]))
        grad_hidden1, weight_qkv = back_in(
            grad_qkv, kept1, full_qkv[layer_index].reshape(width, 3 * d_col), whole_qkv[layer_index]
        )
        grads_w_qkv[layer_index] = weight_qkv.reshape(width, 3, d_col)
        d_scale1 = per_sequence(grad_hidden1 * normed1)
        d_shift1 = per_sequence(grad_hidden1)
        grad_state = grad_middle + norm_back(grad_hidden1 * (1.0 + scale1), normed1, rstd1)
        grads_ada[layer_index] = jnp.stack(
            (d_gamma1, d_gamma2, d_scale1, d_scale2, d_shift1, d_shift2), axis=1
        )
    ada_sums, bias_proj_col, bias_fc2_col = (
        lax.psum_scatter(
            jnp.stack(grads_ada).astype(jnp.bfloat16), "col", scatter_dimension=3, tiled=True
        ).astype(jnp.float32),
        lax.psum_scatter(
            jnp.stack(grads_b_proj).astype(jnp.bfloat16), "col", scatter_dimension=1, tiled=True
        ).astype(jnp.float32),
        lax.psum_scatter(
            jnp.stack(grads_b_fc2).astype(jnp.bfloat16), "col", scatter_dimension=1, tiled=True
        ).astype(jnp.float32),
    )
    grad_ada = ada_sums.astype(jnp.bfloat16)
    weights_ada = []
    for layer_index in range(layer_count):
        weight_ada = lax.dot_general(
            silu_low,
            grad_ada[layer_index].reshape(seq_row, 6 * d_col),
            (((0,), (0,)), ((), ())),
            preferred_element_type=jnp.float32,
        )
        weights_ada.append(weight_ada.reshape(width, 6, d_col))
    bias_ada_local = jnp.sum(grad_ada.astype(jnp.float32), axis=1)
    sum_ada, sum_qkv, sum_fc1, sum_proj, sum_fc2 = (
        lax.psum_scatter(
            jnp.stack(weights_ada).astype(jnp.bfloat16), "row", scatter_dimension=1, tiled=True
        ).astype(jnp.float32),
        lax.psum_scatter(
            jnp.stack(grads_w_qkv).astype(jnp.bfloat16), "row", scatter_dimension=1, tiled=True
        ).astype(jnp.float32),
        lax.psum_scatter(
            jnp.stack(grads_w_fc1).astype(jnp.bfloat16), "row", scatter_dimension=1, tiled=True
        ).astype(jnp.float32),
        lax.psum_scatter(
            jnp.stack(grads_w_proj).astype(jnp.bfloat16), "row", scatter_dimension=2, tiled=True
        ).astype(jnp.float32),
        lax.psum_scatter(
            jnp.stack(grads_w_fc2).astype(jnp.bfloat16), "row", scatter_dimension=2, tiled=True
        ).astype(jnp.float32),
    )
    bias_ada, bias_qkv, scale_grad, bias_proj, bias_fc1, bias_fc2 = lax.psum(
        (
            bias_ada_local,
            jnp.stack(grads_b_qkv),
            jnp.stack(grads_scale),
            bias_proj_col,
            jnp.stack(grads_b_fc1),
            bias_fc2_col,
        ),
        "row",
    )
    return (
        mixed,
        grad_state,
        sum_ada,
        bias_ada,
        sum_qkv,
        bias_qkv,
        scale_grad,
        sum_proj,
        bias_proj,
        sum_fc1,
        bias_fc1,
        sum_fc2,
        bias_fc2,
    )


BF = jnp.bfloat16
F32 = jnp.float32
NN = (((1,), (0,)), ((), ()))
NT = (((1,), (1,)), ((), ()))
TN = (((0,), (0,)), ((), ()))
VMEM_BYTES = 60 * 1024 * 1024


def sibling(values):
    return lax.ppermute(values, "core", [(0, 1), (1, 0)])


def across(values, axis):
    return lax.ppermute(values, axis, [(0, 1), (1, 0)])


def trade(values, moves):
    return jnp.where(moves, lax.ppermute(values, ("core", "x"), [(1, 2), (2, 1)]), values)


def turned(values, flag, axis):
    half = values.shape[axis] // 2
    return jnp.where(flag == 1, jnp.roll(values, half, axis), values)


def dot(left, right, dims=NN):
    return lax.dot_general(left, right, dims, preferred_element_type=F32)


def shape_of(dims, kind):
    return jax.ShapeDtypeStruct(dims, kind)


def call(body, grid, in_specs, out_specs, out_shape, scratch, flops, moved, args):
    return pl.pallas_call(
        body,
        grid=grid,
        in_specs=in_specs,
        out_specs=out_specs,
        out_shape=out_shape,
        scratch_shapes=scratch,
        compiler_params=pltpu.CompilerParams(
            dimension_semantics=("arbitrary",) * len(grid), vmem_limit_bytes=VMEM_BYTES
        ),
        cost_estimate=pl.CostEstimate(flops=flops // 64, bytes_accessed=moved // 64, transcendentals=0),
    )(*args)


def fixed(dims):
    return pl.BlockSpec(dims, lambda *_: (0,) * len(dims))


def row_loop(total, size, body, unroll=1):
    @pl.loop(0, total // size, unroll=unroll)
    def _(step):
        body(pl.ds(pl.multiple_of(step * size, size), size))


def early(dims, row=0):
    return pl.BlockSpec(dims, lambda t: (row + jnp.minimum(t, 1), 0))


def late(dims, row=0):
    return pl.BlockSpec(dims, lambda t: (row + jnp.maximum(t - 2, 0), 0))


def weight_specs(low, blocks=None):
    if blocks is not None and blocks[0].ndim == 4:
        shape = (2, None, low // 2, low)

        def spec(block, pick):
            return pl.BlockSpec(shape, lambda t: (pick(t), block, 0, 0))

        first, second = lambda t: jnp.minimum(t, 1), lambda t: jnp.maximum(t - 2, 0)
        return [spec(0, first), spec(2, second), spec(1, first), spec(3, lambda t: 0), spec(3, lambda t: 1)]
    return [early((low, low)), late((low, low)), early((low, low)), fixed((low, low)), fixed((low, low))]


def matrix(ref):
    value = ref[...]
    return value.reshape(-1, value.shape[-1])


def with_tile(step, refs, body):
    g, gx, gy, ga, gb = refs

    @pl.when(step < 2)
    def _():
        body(g, gy)

    @pl.when(step == 2)
    def _():
        body(gx, ga)

    @pl.when(step == 3)
    def _():
        body(gx, gb)


def join_into(joined, own, other):
    rows = own.shape[0]
    joined[:rows, :] = own[...]
    joined[rows:, :] = other[...]


def fc_up(own, other, blocks, bias):
    rows, width = own.shape
    low, both = width // 2, 2 * rows
    hid = 4 * low

    def body(own_ref, other_ref, g, gx, gy, ga, gb, bias_ref, joined, act, slope):
        step = pl.program_id(0)

        @pl.when(step == 0)
        def _():
            join_into(joined, own_ref, other_ref)

        def product(first, second):
            for lanes in (slice(0, low // 2), slice(low // 2, low)):
                for sl in (slice(0, rows), slice(rows, both)):
                    pre = dot(joined[sl, :low], first[lanes, :], NT)
                    pre = pre + dot(joined[sl, low:], second[lanes, :], NT) + bias_ref[:, lanes]
                    root = 0.7978845608028654
                    square = pre * pre
                    tanh = jnp.tanh(pre * (root + (root * 0.044715) * square))
                    half = 0.5 + 0.5 * tanh
                    act[sl, lanes] = (pre * half).astype(BF)
                    inner = pre * ((0.5 * root) + (1.5 * 0.044715 * root) * square)
                    slope[sl, lanes] = (half + (1.0 - tanh * tanh) * inner).astype(BF)

        with_tile(step, (g, gx, gy, ga, gb), product)

    return call(
        body,
        (4,),
        [fixed((rows, width))] * 2 + weight_specs(low) + [pl.BlockSpec((1, low), lambda t: (0, t))],
        [fixed((both, width))] + [pl.BlockSpec((both, low), lambda t: (0, t))] * 2,
        [shape_of((both, width), BF), shape_of((both, hid), BF), shape_of((both, hid), BF)],
        [],
        2 * both * width * hid,
        2 * hid * width + 6 * both * width + 4 * both * hid,
        (own, other, *blocks, bias),
    )


def fc_forward(own, other, up_blocks, down_blocks, bias):
    rows, width = own.shape
    low, both = width // 2, 2 * rows
    hid = 4 * low

    def body(own_ref, other_ref, ug, ugx, ugy, uga, ugb, dg, dgx, dgy, dga, dgb, bias_ref,
             joined, act, slope, out_own, out_other, acc):
        step = pl.program_id(0)

        @pl.when(step == 0)
        def _():
            join_into(joined, own_ref, other_ref)

        def product(up_one, up_two, down_one, down_two, first, last):
            for i, sl in enumerate((slice(rows, both), slice(0, rows))):
                pre = dot(joined[sl, :low], up_one[...], NT) + dot(joined[sl, low:], up_two[...], NT)
                pre = pre + bias_ref[...]
                root = 0.7978845608028654
                square = pre * pre
                tanh = jnp.tanh(pre * (root + (root * 0.044715) * square))
                half = 0.5 + 0.5 * tanh
                value = (pre * half).astype(BF)
                act[sl, :] = value
                inner = pre * ((0.5 * root) + (1.5 * 0.044715 * root) * square)
                slope[sl, :] = (half + (1.0 - tanh * tanh) * inner).astype(BF)
                for lanes, down in ((slice(0, low), down_one), (slice(low, width), down_two)):
                    part = dot(value, matrix(down))
                    if not first:
                        part = part + acc[sl, lanes]
                    if not last:
                        acc[sl, lanes] = part
                    elif i == 0:
                        out_other[:, lanes] = part.astype(BF)
                    else:
                        out_own[:, lanes] = part

        @pl.when(step == 0)
        def _():
            product(ug, ugy, dg, dgy, True, False)

        @pl.when(step == 1)
        def _():
            product(ug, ugy, dg, dgy, False, False)

        @pl.when(step == 2)
        def _():
            product(ugx, uga, dgx, dga, False, False)

        @pl.when(step == 3)
        def _():
            product(ugx, ugb, dgx, dgb, False, True)

    tiles = pl.BlockSpec((both, low), lambda t: (0, t))
    return call(
        body,
        (4,),
        [fixed((rows, width))] * 2 + weight_specs(low) + weight_specs(low, down_blocks)
        + [pl.BlockSpec((1, low), lambda t: (0, t))],
        [fixed((both, width)), tiles, tiles, fixed((rows, width)), fixed((rows, width))],
        [
            shape_of((both, width), BF), shape_of((both, hid), BF), shape_of((both, hid), BF),
            shape_of((rows, width), F32), shape_of((rows, width), BF),
        ],
        [pltpu.VMEM((both, width), F32)],
        4 * both * width * hid,
        4 * hid * width + 6 * both * width + 4 * both * hid + 6 * rows * width,
        (own, other, *up_blocks, *down_blocks, bias),
    )


def fc_back(own, other, up_blocks, down_blocks, slope, act, hidden, by_z):
    rows, width = own.shape
    low, both = width // 2, 2 * rows
    hid = 4 * low

    def body(own_ref, other_ref, ug, ugx, ugy, uga, ugb, dg, dgx, dgy, dga, dgb, slope_ref, act_ref, hid_ref,
             sums, out_own, out_other, *rest):
        joined, grad, acc = rest[-3:]
        if by_z:
            two_refs, one_refs = rest[:1], rest[1:-3]
        else:
            far_a, far_b = rest[6], rest[7]
            two_refs = (*rest[:3], far_a.at[1], far_b.at[1])
            one_refs = (*rest[3:6], far_a.at[0], far_b.at[0])
        step = pl.program_id(0)

        @pl.when(step == 0)
        def _():
            join_into(joined, own_ref, other_ref)

        def product(up_one, up_two, down_one, down_two, first, last, near, far):
            for i, sl in enumerate((slice(rows, both), slice(0, rows))):
                value = dot(joined[sl, :low], matrix(up_one), NT) + dot(joined[sl, low:], matrix(up_two), NT)
                value = (value * slope_ref[sl, :].astype(F32)).astype(BF)
                grad[sl, :] = value
                total = jnp.sum(value.astype(F32).reshape(rows // 8, 8, low), axis=0)
                sums[...] = total if i == 0 else sums[...] + total
                for lanes, down in ((slice(0, low), down_one), (slice(low, width), down_two)):
                    part = dot(value, matrix(down))
                    if not first:
                        part = part + acc[sl, lanes]
                    if not last:
                        acc[sl, lanes] = part
                    elif i == 0:
                        out_other[:, lanes] = part.astype(BF)
                    else:
                        out_own[:, lanes] = part
            for refs, left, right in ((two_refs, act_ref, joined), (one_refs, grad, hid_ref)):
                for j, lanes in ((near, slice(0, low)), (far, slice(low, width))):
                    value = dot(left[...], right[:, lanes], TN).astype(BF)
                    if len(refs) == 1:
                        refs[0][:, min(j, 3) // 2] = value.reshape(2, low // 2, low)
                    else:
                        refs[j][...] = value

        @pl.when(step == 0)
        def _():
            product(ug, ugy, dg, dgy, True, False, 0, 2)

        @pl.when(step == 1)
        def _():
            product(ug, ugy, dg, dgy, False, False, 0, 2)

        @pl.when(step == 2)
        def _():
            product(ugx, uga, dgx, dga, False, False, 1, 3)

        @pl.when(step == 3)
        def _():
            product(ugx, ugb, dgx, dgb, False, True, 1, 4)

    tiles = pl.BlockSpec((both, low), lambda t: (0, t))
    whole = shape_of((2 * low, low), BF)
    block_specs = weight_specs(low)
    block_shapes = [whole] * 3 + [shape_of((low, low), BF)] * 2
    z_specs = [pl.BlockSpec((2, 2, low // 2, low), lambda t: (t % 2, t // 2, 0, 0))]
    found = call(
        body,
        (4,),
        [fixed((rows, width))] * 2 + weight_specs(low, up_blocks) + weight_specs(low, down_blocks) + [tiles, tiles, fixed((both, width))],
        [pl.BlockSpec((8, low), lambda t: (0, t)), fixed((rows, width)), fixed((rows, width))]
        + (z_specs + block_specs if by_z else block_specs[:3] * 2 + [fixed((2, low, low))] * 2),
        [shape_of((8, hid), F32), shape_of((rows, width), F32), shape_of((rows, width), BF)]
        + ([shape_of((4, 4, low // 2, low), BF)] + block_shapes if by_z
           else [whole] * 6 + [shape_of((2, low, low), BF)] * 2),
        [pltpu.VMEM((both, width), BF), pltpu.VMEM((both, low), BF), pltpu.VMEM((both, width), F32)],
        8 * both * width * hid,
        8 * hid * width + 6 * both * width + 4 * both * hid + 6 * rows * width,
        (own, other, *up_blocks, *down_blocks, slope, act, hidden),
    )
    if by_z:
        return found[:3], found[3], found[4:]
    return found[:3], found[3:9], found[9:]


def fc_down(left, blocks):
    both, hid = left.shape
    rows, low = both // 2, hid // 4
    width = 2 * low

    def body(left_ref, g, gx, gy, ga, gb, own, other, acc):
        step = pl.program_id(0)

        def product(one, two, first, last):
            for i, sl in enumerate((slice(rows, both), slice(0, rows))):
                for lanes, right in ((slice(0, low), one), (slice(low, width), two)):
                    part = dot(left_ref[sl, :], matrix(right))
                    if not first:
                        part = part + acc[sl, lanes]
                    if not last:
                        acc[sl, lanes] = part
                    elif i == 0:
                        other[:, lanes] = part.astype(BF)
                    else:
                        own[:, lanes] = part

        @pl.when(step == 0)
        def _():
            product(g, gy, True, False)

        @pl.when(step == 1)
        def _():
            product(g, gy, False, False)

        @pl.when(step == 2)
        def _():
            product(gx, ga, False, False)

        @pl.when(step == 3)
        def _():
            product(gx, gb, False, True)

    return call(
        body,
        (4,),
        [pl.BlockSpec((both, low), lambda t: (0, t))] + weight_specs(low, blocks),
        [fixed((rows, width))] * 2,
        [shape_of((rows, width), F32), shape_of((rows, width), BF)],
        [pltpu.VMEM((both, width), F32)],
        2 * both * width * hid,
        2 * hid * width + 2 * both * hid + 6 * rows * width,
        (left, *blocks),
    )


def head_ones(size, head_width):
    first = lax.broadcasted_iota(jnp.int32, (size, size), 0) // head_width
    second = lax.broadcasted_iota(jnp.int32, (size, size), 1) // head_width
    return (first == second).astype(BF)


def qkv_up(own, other, blocks, vectors, ones):
    rows, width = own.shape
    low, both = width // 2, 2 * rows
    tile = low // 2

    def body(own_ref, other_ref, g, gx, gy, ga, gb, vec, ones_ref, joined, q_raw, k_raw, q_low, k_low, v_low):
        step = pl.program_id(0)

        @pl.when(step == 0)
        def _():
            join_into(joined, own_ref, other_ref)

        def unit(value):
            square = dot((value * value).astype(BF), ones_ref[...])
            return value * lax.rsqrt(square + EPS_UNIT)

        def product(near, far):
            for part in range(3):
                near_rows = slice(part * tile, (part + 1) * tile)
                far_ref, far_rows = (far[0], near_rows) if part < 2 else far[1]
                for sl in (slice(0, rows), slice(rows, both)):
                    value = dot(joined[sl, :low], near[near_rows, :], NT)
                    value = value + dot(joined[sl, low:], far_ref[far_rows, :], NT)
                    if part == 0:
                        value = value + vec[0:1, :]
                        q_raw[sl, :] = value.astype(BF)
                        q_low[sl, :] = (unit(value) * vec[2:3, :]).astype(BF)
                    elif part == 1:
                        k_raw[sl, :] = value.astype(BF)
                        k_low[sl, :] = unit(value).astype(BF)
                    else:
                        v_low[sl, :] = (value + vec[1:2, :]).astype(BF)

        last = slice(2 * tile, 3 * tile)

        @pl.when(step == 0)
        def _():
            product(g, (gy, (gy, last)))

        @pl.when(step == 1)
        def _():
            product(gx, (ga, (gb, slice(0, tile))))

    kept = pl.BlockSpec((both, tile), lambda t: (0, t))
    heads = shape_of((both, low), BF)
    return call(
        body,
        (2,),
        [fixed((rows, width))] * 2 + [fixed((3 * tile, low))] * 3 + [fixed((low, low)), fixed((tile, low))]
        + [pl.BlockSpec((8, tile), lambda t: (0, t)), fixed((tile, tile))],
        [fixed((both, width))] + [kept] * 5,
        [shape_of((both, width), BF)] + [heads] * 5,
        [],
        2 * both * width * 3 * low,
        2 * 3 * low * width + 6 * both * width + 10 * both * low,
        (own, other, *blocks, vectors, ones),
    )


def attn_mix(q_low, k_low, v_low, end_col, place_row, blocks, head_width):
    both, low = q_low.shape
    rows, width = both // 2, 2 * low
    pair = 2 * head_width
    chunk = both // 4

    def body(q_ref, k_ref, v_ref, end_ref, place_ref, g, gx, gy, gb, out_ref, rest_ref, log_ref, own, other,
             weights, acc):
        step = pl.program_id(0)

        @pl.when(step < 2)
        def _():
            weights[:, :low] = g[...]
            weights[:, low:] = gy[...]

        @pl.when(step >= 2)
        def _():
            weights[:, :low] = gx[...]
            weights[:, low:] = gb[...]

        place = place_ref[0:1, :]
        lane = lax.broadcasted_iota(jnp.int32, (both, pair), 1)
        value = v_ref[...]
        ones = jnp.ones_like(value)
        wide = [
            jnp.concatenate((jnp.where(lane // head_width == h, value, ones), ones), axis=1) for h in range(2)
        ]
        first = lane[:chunk] < head_width
        for c in range(4):
            sl = slice(c * chunk, (c + 1) * chunk)
            queries = q_ref[sl, :]
            found = []
            for h in range(2):
                mine = jnp.where(first if h == 0 else ~first, queries, jnp.zeros_like(queries))
                scores = dot(mine, k_ref[...], NT)
                expo = jnp.where(place < end_ref[sl, :], jnp.exp(scores), 0.0).astype(BF)
                found.append(dot(expo, wide[h]))
            out = jnp.where(first, found[0][:, :pair] / found[0][:, pair:], found[1][:, :pair] / found[1][:, pair:])
            low_out = out.astype(BF)
            out_ref[sl, :] = low_out
            rest_ref[sl, :] = (out - low_out.astype(F32)).astype(BF)
            log_ref[sl, :] = jnp.log(jnp.where(first, found[1][:, pair:], found[0][:, pair:]))
        part = dot(out_ref[...], weights[...])

        @pl.when(step == 0)
        def _():
            acc[...] = part

        @pl.when(jnp.logical_and(step > 0, step < 3))
        def _():
            acc[...] += part

        @pl.when(step == 3)
        def _():
            total = acc[...] + part
            own[...] = total[:rows]
            other[...] = total[rows:].astype(BF)

    block = pl.BlockSpec((both, pair), lambda t: (0, t))
    w_specs = [early((pair, low), 6), late((pair, low), 6), early((pair, low), 6), late((pair, low), 2)]
    return call(
        body,
        (4,),
        [block] * 3 + [fixed((both, 1)), fixed((8, both))] + w_specs,
        [block] * 3 + [fixed((rows, width))] * 2,
        [shape_of((both, low), BF)] * 2 + [shape_of((both, low), F32)]
        + [shape_of((rows, width), F32), shape_of((rows, width), BF)],
        [pltpu.VMEM((pair, width), BF), pltpu.VMEM((both, width), F32)],
        4 * both * both * low + 2 * both * width * low,
        14 * both * low + 8 * both * low,
        (q_low, k_low, v_low, end_col, place_row, *blocks[:3], blocks[4]),
    )


def attn_back(x, own, other, blocks, q_low, k_low, v_low, attn, rest, logs, q_raw, k_raw, hidden, scale_row,
              place_col, end_row, head_width, before=None):
    rows, width = own.shape
    both, low = q_low.shape
    pair = 2 * head_width
    chunk = both // 4
    first_call = before is None

    def body(own_ref, other_ref, *refs):
        w_refs, refs = refs[:8], refs[8:]
        (q_ref, k_ref, v_ref, attn_ref, rest_ref, log_ref, qr_ref, kr_ref, hid_ref, scale_ref, place_ref,
         end_ref), refs = refs[:12], refs[12:]
        if first_call:
            sums, total_ref, near_out, far_a, far_b = refs[:5]
            joined, weights, ds_ref, three_ref = refs[5:]
        else:
            before_ref, sums, out_own, out_other, near_out, far_out = refs[:6]
            joined, weights, ds_ref, three_ref, total_ref = refs[6:]
        step = pl.program_id(0)

        @pl.when(step == 0)
        def _():
            join_into(joined, own_ref, other_ref)

        for i in range(4):
            rows_i = slice(i * pair, (i + 1) * pair)
            weights[rows_i, :low] = w_refs[2 * i][...]
            weights[rows_i, low:] = w_refs[2 * i + 1][...]

        grad = dot(joined[...], weights[3 * pair :, :], NT).astype(BF)
        ends = end_ref[0:1, :]
        lane = lax.broadcasted_iota(jnp.int32, (both, pair), 1)
        inner = lane % head_width
        row_head = lax.broadcasted_iota(jnp.int32, (pair, pair), 0) // head_width
        lane_head = lax.broadcasted_iota(jnp.int32, (pair, pair), 1) // head_width
        same = (row_head == lane_head).astype(BF)
        swap = (row_head != lane_head).astype(BF)
        swap_twice = jnp.concatenate((swap, swap), axis=0)

        def spread(value):
            high = value.astype(BF)
            left = value - high.astype(F32)
            mid = left.astype(BF)
            small = (left - mid.astype(F32)).astype(BF)
            zero = jnp.zeros_like(high)
            return jnp.where(inner == 0, high, jnp.where(inner == 1, mid, jnp.where(inner == 2, small, zero)))

        def unit_back(raw, grad_unit):
            raw = raw.astype(F32)
            rate = lax.rsqrt(dot((raw * raw).astype(BF), same) + EPS_UNIT)
            unit = raw * rate
            cross = dot((grad_unit * unit).astype(BF), same)
            return rate * (grad_unit - unit * cross), unit

        product = grad.astype(F32) * (attn_ref[...].astype(F32) + rest_ref[...].astype(F32))
        high = product.astype(BF)
        small = (product - high.astype(F32)).astype(BF)
        delta = dot(jnp.concatenate((high, small), axis=1), swap_twice)
        log_terms, delta_terms = spread(-log_ref[...]), spread(-delta)
        queries, keys, values = q_ref[...], k_ref[...], v_ref[...]
        zero, one = jnp.zeros_like(keys), jnp.ones_like(keys)
        dk_parts, dv_parts = [None] * 4, [None] * 4
        d_qt = None
        for h in range(2):
            mine = lane // head_width == h
            q_own, g_own, k_own = [jnp.where(mine, v, zero) for v in (queries, grad, keys)]
            q_wide, g_wide = jnp.where(mine, queries, log_terms), jnp.where(mine, grad, delta_terms)
            k_wide, v_wide = jnp.where(mine, keys, one), jnp.where(mine, values, one)
            for c in range(4):
                sl = slice(c * chunk, (c + 1) * chunk)
                scores = dot(k_wide[sl], q_wide, NT)
                probs = jnp.where(place_ref[sl, :] < ends, jnp.exp(scores), 0.0)
                d_scores = (probs * dot(v_wide[sl], g_wide, NT)).astype(BF)
                ds_ref[sl, :] = d_scores
                d_v, d_k = dot(probs.astype(BF), g_own), dot(d_scores, q_own)
                dv_parts[c] = d_v if h == 0 else dv_parts[c] + d_v
                dk_parts[c] = d_k if h == 0 else dk_parts[c] + d_k
            part = dot(k_own, ds_ref[...], TN)
            d_qt = part if h == 0 else d_qt + part
        d_qn = d_qt.T
        d_q, unit_q = unit_back(qr_ref[...], d_qn * scale_ref[0:1, :])
        d_k, _ = unit_back(kr_ref[...], jnp.concatenate(dk_parts, axis=0))
        d_q, d_k, d_v = d_q.astype(BF), d_k.astype(BF), jnp.concatenate(dv_parts, axis=0).astype(BF)
        for i, value in enumerate((d_q, d_k, d_v)):
            three_ref[:, i * pair : (i + 1) * pair] = value
        for i, value in enumerate((d_q.astype(F32), d_v.astype(F32), d_qn * unit_q)):
            sums[i : i + 1, :] = jnp.sum(value, axis=0, keepdims=True)

        for lanes in (slice(0, low), slice(low, width)):
            part = dot(three_ref[...], weights[: 3 * pair, lanes])

            @pl.when(step == 0)
            def _():
                total_ref[:, lanes] = part if first_call else part + before_ref[:, lanes]

            @pl.when(step == 1)
            def _():
                total = total_ref[:, lanes] + part
                if first_call:
                    total_ref[:, lanes] = total
                else:
                    out_own[:, lanes] = total[:rows]
                    out_other[:, lanes] = total[rows:].astype(BF)

        for i, lanes in enumerate((slice(0, low), slice(low, width))):
            three = dot(three_ref[...], hid_ref[:, lanes], TN).astype(BF)
            proj = dot(attn_ref[...], joined[:, lanes], TN).astype(BF)
            grads = [three[j * pair : (j + 1) * pair] for j in range(3)] + [proj]
            for j in range(4):
                if i == 0:
                    near_out[j, 0] = grads[j]
                elif first_call:
                    (far_a if j < 2 else far_b)[j % 2, 0] = grads[j]
                else:
                    far_out[j, 0] = grads[j]

    w_specs, w_args = [], []
    for i in range(4):
        far_row = 2 * (i % 2) if x else 2 * i
        w_specs += [pl.BlockSpec((pair, low), lambda t, row=row: (row + t, 0)) for row in (2 * i, far_row)]
        w_args += [blocks[1], blocks[3 + i // 2]] if x else [blocks[0], blocks[2]]
    block = pl.BlockSpec((both, pair), lambda t: (0, 2 * x + t))
    row = pl.BlockSpec((8, pair), lambda t: (0, t))
    four = pl.BlockSpec((4, 1, pair, low), lambda t: (0, t, 0, 0))
    duo = pl.BlockSpec((2, 1, pair, low), lambda t: (0, t, 0, 0))
    whole, half = shape_of((4, 2, pair, low), BF), shape_of((2, 2, pair, low), BF)
    total = shape_of((both, width), F32)
    found = call(
        body,
        (2,),
        [fixed((rows, width))] * 2 + w_specs + [block] * 8
        + [fixed((both, width)), pl.BlockSpec((8, pair), lambda t: (0, 2 * x + t)), fixed((both, 1)), fixed((8, both))]
        + ([] if first_call else [fixed((both, width))]),
        [row] + ([fixed((both, width)), four, duo, duo] if first_call else [fixed((rows, width))] * 2 + [four] * 2),
        [shape_of((8, 2 * pair), F32)]
        + (
            [total, whole, half, half] if first_call
            else [shape_of((rows, width), F32), shape_of((rows, width), BF), whole, whole]
        ),
        [
            pltpu.VMEM((both, width), BF), pltpu.VMEM((4 * pair, width), BF), pltpu.VMEM((both, both), BF),
            pltpu.VMEM((both, 3 * pair), BF),
        ] + ([] if first_call else [pltpu.VMEM((both, width), F32)]),
        5 * both * both * low + 8 * both * width * low,
        12 * both * low + 8 * both * width,
        (own, other, *w_args, q_low, k_low, v_low, attn, rest, logs, q_raw, k_raw, hidden, scale_row,
         place_col, end_row) + (() if first_call else (before,)),
    )
    start = 2 if first_call else 3
    return found[:start], [v.reshape(-1, low) for v in found[start:]]


def mix(own, got, state, vectors, last):
    rows, width = own.shape
    part = rows // 2

    def body(own_ref, got_ref, state_ref, vec, branch_ref, next_ref, hid_ref):
        def one(sl):
            branch = own_ref[sl, :] + got_ref[sl, :].astype(F32) + vec[0:1, :]
            branch_ref[sl, :] = branch.astype(BF)
            value = state_ref[sl, :] + vec[1:2, :] * branch
            next_ref[sl, :] = value
            if last:
                hid_ref[sl, :] = value.astype(BF)
            else:
                mean = jnp.mean(value, axis=1, keepdims=True)
                spread = jnp.mean(value * value, axis=1, keepdims=True) - mean * mean
                normed = (value - mean) * lax.rsqrt(spread + EPS_NORM)
                hid_ref[sl, :] = (normed * vec[2:3, :] + vec[3:4, :]).astype(BF)

        row_loop(part, 16, one, unroll=11)

    block = pl.BlockSpec((part, width), lambda t: (t, 0))
    return call(
        body,
        (2,),
        [block] * 3 + [fixed((8, width))],
        [block] * 3,
        [shape_of((rows, width), BF), shape_of((rows, width), F32), shape_of((rows, width), BF)],
        [],
        20 * rows * width,
        18 * rows * width,
        (own, got, state, vectors),
    )


def mix_back(own, got, state, grad, branch, vectors):
    rows, width = own.shape
    part = rows // 2

    def body(own_ref, got_ref, state_ref, grad_ref, branch_ref, vec, next_ref, low_ref, sums):
        @pl.when(pl.program_id(0) == 0)
        def _():
            sums[...] = jnp.zeros_like(sums)

        def add(i, value):
            sums[8 * i : 8 * i + 8, :] += value[:8] + value[8:]

        def one(sl):
            d_hid = own_ref[sl, :] + got_ref[sl, :].astype(F32)
            value = state_ref[sl, :]
            mean = jnp.mean(value, axis=1, keepdims=True)
            spread = jnp.mean(value * value, axis=1, keepdims=True) - mean * mean
            rate = lax.rsqrt(spread + EPS_NORM)
            normed = (value - mean) * rate
            add(0, d_hid * normed)
            add(1, d_hid)
            d_norm = d_hid * vec[0:1, :]
            means = jnp.mean(d_norm, axis=1, keepdims=True)
            crosses = jnp.mean(d_norm * normed, axis=1, keepdims=True)
            total = grad_ref[sl, :] + rate * (d_norm - means - normed * crosses)
            next_ref[sl, :] = total
            add(2, total * branch_ref[sl, :].astype(F32))
            low = (total * vec[1:2, :]).astype(BF)
            low_ref[sl, :] = low
            add(3, low.astype(F32))

        row_loop(part, 16, one, unroll=11)

    block = pl.BlockSpec((part, width), lambda t: (t, 0))
    return call(
        body,
        (2,),
        [block] * 5 + [fixed((8, width))],
        [block] * 2 + [fixed((32, width))],
        [shape_of((rows, width), F32), shape_of((rows, width), BF), shape_of((32, width), F32)],
        [],
        30 * rows * width,
        20 * rows * width,
        (own, got, state, grad, branch, vectors),
    )


def tie(value, *others):
    return lax.optimization_barrier((value,) + others)[0]


def add_low(*values):
    return sum(v.astype(F32) for v in values).astype(BF)


def near_parts(pairs, got_a, got_b):
    half, low = got_a.shape[-2:]
    count = len(pairs)
    got_a, got_b = [v.reshape(count, half, low) for v in (got_a, got_b)]

    def body(*refs):
        ins, a_ref, b_ref, outs = refs[: 2 * count], refs[2 * count], refs[2 * count + 1], refs[2 * count + 2 :]
        for i in range(count):
            for j, got in ((2 * i, a_ref), (2 * i + 1, b_ref)):
                outs[j][...] = (ins[j][...].astype(F32) + got[i].astype(F32)).astype(BF)

    front = pl.BlockSpec((half, low), lambda t: (0, 0))
    back = pl.BlockSpec((half, low), lambda t: (1, 0))
    flat = [v for pair in pairs for v in pair]
    found = pl.pallas_call(
        body,
        grid=(1,),
        in_specs=[front, back] * count + [fixed(got_a.shape)] * 2,
        out_specs=[front, back] * count,
        out_shape=[shape_of(v.shape, BF) for v in flat],
        input_output_aliases={i: i for i in range(2 * count)},
        compiler_params=pltpu.CompilerParams(vmem_limit_bytes=VMEM_BYTES),
        cost_estimate=pl.CostEstimate(
            flops=2 * count * half * low, bytes_accessed=12 * count * half * low, transcendentals=0
        ),
    )(*flat, got_a, got_b)
    return [found[2 * i : 2 * i + 2] for i in range(count)]


def summed(keep, got_x, got_y, parts, z_size):
    total = add_low(keep, got_x, got_y)
    total = jnp.swapaxes(total.reshape(parts, z_size, -1, keep.shape[1]), 0, 1)
    return total.reshape(z_size, -1, keep.shape[1])


def over_z(total):
    return lax.psum_scatter(total, "z", scatter_dimension=0, tiled=False)


def eight_rows(*rows):
    rows = [r.reshape(1, -1) for r in rows]
    return jnp.concatenate(rows + [jnp.zeros_like(rows[0])] * (8 - len(rows)), axis=0)


def on_pair(
    hidden_in, cond, scale_sizes, w_ada, b_ada, w_qkv, b_qkv, head_scale,
    w_proj, b_proj, w_fc1, b_fc1, w_fc2, b_fc2, grad_out,
):
    y = lax.axis_index("y")
    core = lax.axis_index("core")
    z = lax.axis_index("z")
    x = lax.axis_index("x")
    layer_count = w_ada.shape[0]
    seq_row, width = cond.shape
    rows_dev = hidden_in.shape[0]
    rows_pad = -(-rows_dev // 32) * 32
    d_col = b_qkv.shape[2]
    head_width = d_col // head_scale.shape[1]
    y_size, z_size, x_size = (lax.axis_size(a) for a in ("y", "z", "x"))
    heads = z_size * x_size
    low = width // 2
    rows_d = w_qkv.shape[1]
    hid_dev = w_fc1.shape[2]
    hid_core = hid_dev // 2

    qkv_t = jnp.transpose(w_qkv, (0, 2, 3, 1)).reshape(layer_count, 3, 2, head_width, rows_d)
    qkv_t = jnp.transpose(qkv_t, (0, 2, 1, 3, 4)).reshape(layer_count, 6 * head_width, rows_d)
    fc1_t = jnp.transpose(w_fc1, (0, 2, 1))
    three, four = 3 * head_width, 4 * head_width
    halves = [
        jnp.concatenate(parts, axis=1)
        for parts in (
            (qkv_t[:, :three], w_proj[:, :head_width], fc1_t[:, :hid_core], w_fc2[:, :hid_core]),
            (qkv_t[:, three:], w_proj[:, head_width:], fc1_t[:, hid_core:], w_fc2[:, hid_core:]),
        )
    ]
    kept = jnp.where(core == 0, halves[0], halves[1])
    came = sibling(jnp.where(core == 0, halves[1], halves[0]))
    shards = jnp.concatenate(
        (jnp.where(core == 0, kept, came), jnp.where(core == 0, came, kept)), axis=2
    )
    cuts = (0, four, four + hid_core, four + 2 * hid_core)

    def z_gather(l, i):
        by_z = lax.all_gather(shards[l, cuts[i] : cuts[i + 1]], "z", axis=0, tiled=False)
        if i == 0:
            by_z = jnp.swapaxes(by_z.reshape(z_size, 4, head_width, low), 0, 1)
        return by_z.reshape(-1, low)

    def send(rows):
        return rows, across(rows, "x"), across(rows, "y")

    def send_on(state):
        _, by_x, by_y = state
        half = by_x.shape[0] // 2
        return across(by_x[:half], "y"), across(by_y[half:], "x")

    def whole(state, halves):
        return (*state, *halves)

    def together(*values):
        return lax.optimization_barrier(values)

    late = shards[1, cuts[2] :]
    late_x, late_y = across(late, "x"), across(late, "y")
    chunks = [z_gather(l, i) for l in range(layer_count) for i in range(3)][:5]

    cond_low = jax.nn.silu(cond.astype(F32)).astype(BF)
    silu_rows = lax.all_gather(tie(cond_low, late), ("y", "core"), axis=0, tiled=True)
    late_x, late_y, silu_rows = together(late_x, late_y, silu_rows)
    late_far = across(late_x, "y")
    row = y * 2 + core
    silu_own = lax.dynamic_slice_in_dim(silu_rows, row * rows_d, rows_d, axis=1)
    seqs = silu_rows.shape[0]
    ada_size = layer_count * 6 * d_col
    part = dot(silu_own, jnp.transpose(w_ada, (1, 0, 2, 3)).reshape(rows_d, ada_size))
    part = part + jnp.where(row == 0, b_ada.astype(F32).reshape(1, ada_size), 0.0)
    smalls = (b_qkv, b_fc1, b_proj, b_fc2, head_scale)
    sizes = [v.size for v in smalls]
    offs = [sum(sizes[:i]) for i in range(6)]
    n_rows = y_size * 2
    quarter = -(-offs[5] // (n_rows * 128)) * 128
    small = jnp.concatenate([v.reshape(-1).astype(F32) for v in smalls])
    small = jnp.pad(small, (0, n_rows * quarter - offs[5])).reshape(n_rows, quarter)
    small = lax.dynamic_index_in_dim(small, row, axis=0, keepdims=True)
    part = jnp.concatenate((part, jnp.broadcast_to(small, (seqs, quarter))), axis=1)
    to_all = jnp.swapaxes(part.reshape(y_size, x_size, z_size, -1), 1, 2)
    to_all = jnp.broadcast_to(to_all[:, None], (y_size, 2) + to_all.shape[1:])
    from_all = lax.all_to_all(
        tie(to_all.reshape(n_rows * z_size * x_size, -1), chunks[0]), ("y", "core", "z", "x"),
        split_axis=0, concat_axis=0, tiled=True,
    ).reshape(n_rows, z_size, x_size, -1)
    sent = together(*send(tie(chunks[0], late_far, late_y)))
    late_blocks = lax.all_gather(
        tie(jnp.stack((late, late_y, late_x, late_far)), *sent), "z", axis=0, tiled=False
    )
    halves = send_on(sent)
    from_all = tie(from_all, *sent)
    ada = jnp.sum(from_all[..., :ada_size], axis=0).reshape(z_size * x_size, layer_count, 6, d_col)
    ada = turned(jnp.transpose(ada, (1, 2, 0, 3)).reshape(layer_count, 6, width), y, 2)
    small = jnp.transpose(from_all[..., ada_size:], (1, 2, 0, 3)).reshape(z_size, x_size, -1)
    s_qkv, s_fc1, s_proj, s_fc2, s_scale = [small[:, :, offs[i] : offs[i + 1]] for i in range(5)]

    def by_core(values, shape, axis):
        values = values.reshape((z_size, x_size) + shape)
        values = lax.dynamic_index_in_dim(values, core, axis=axis, keepdims=False)
        return turned(jnp.swapaxes(values, 0, 1), x, 0)

    def by_d(values):
        values = jnp.swapaxes(values.reshape(z_size * x_size, layer_count, d_col), 0, 1)
        return turned(values.reshape(layer_count, width), y, 1)

    bias_qkv = by_core(s_qkv, (layer_count, 2, 2, head_width), 4)
    bias_qkv = jnp.transpose(bias_qkv, (2, 3, 0, 1, 4)).reshape(layer_count, 2, low)
    scales = by_core(s_scale, (layer_count, 2), 3)
    scales = jnp.transpose(scales, (2, 0, 1)).reshape(layer_count, heads)
    scales = jnp.repeat(scales, head_width, axis=1)
    bias_fc1 = by_core(s_fc1, (layer_count, 2, hid_core), 3)
    bias_fc1 = jnp.transpose(bias_fc1, (2, 0, 1, 3)).reshape(layer_count, 1, -1)
    bias_proj, bias_fc2 = by_d(s_proj), by_d(s_fc2)

    sizes_f = scale_sizes.astype(F32)
    sizes_f = jnp.where(core == x, sizes_f, sibling(sizes_f))
    own_sizes = lax.dynamic_index_in_dim(sizes_f, z, axis=0, keepdims=False).astype(jnp.int32)
    index = jnp.arange(rows_pad, dtype=jnp.int32)
    places = jnp.concatenate((core * rows_dev + index, (1 - core) * rows_dev + index))
    starts = jnp.cumsum(own_sizes) - own_sizes
    ends = jnp.sum(jnp.where(starts[None, :] <= places[:, None], own_sizes[None, :], 0), axis=1)
    real = jnp.concatenate((index, index)) < rows_dev
    key_places = jnp.where(real, places, 1 << 20).astype(F32)
    ends = ends.astype(F32)
    place_col, end_col = key_places[:, None], ends[:, None]
    place_row, end_row = eight_rows(key_places), eight_rows(ends)
    ones = head_ones(low // 2, head_width)

    def own_tokens(values):
        return jnp.pad(turned(trade(values, core != x), y, 1), ((0, rows_pad - rows_dev), (0, 0)))

    state = own_tokens(tie(hidden_in, silu_rows)).astype(F32)
    hidden = (normalize(state)[0] * (1.0 + ada[0, 2][None]) + ada[0, 4][None]).astype(BF)
    weights = [None] * 5 + [(late_blocks,) * 5]

    def attn_start(l, hidden):
        vectors = eight_rows(bias_qkv[l, 0], bias_qkv[l, 1], scales[l])
        found = qkv_up(hidden, sibling(hidden), weights[3 * l], vectors, ones)
        return found

    def attn_end(l, own, send_own, state):
        branch, middle, hidden = mix(
            own, sibling(send_own), state,
            eight_rows(bias_proj[l], ada[l, 0], 1.0 + ada[l, 3], ada[l, 5]), False,
        )
        return branch, middle, hidden

    def fc_start(l, hidden):
        return fc_up(hidden, sibling(hidden), weights[3 * l + 1], bias_fc1[l])

    def fc_end(l, act, middle):
        own, send_own = fc_down(act, weights[3 * l + 2])
        last = l == layer_count - 1
        after = ada[l if last else l + 1]
        return mix(
            own, sibling(send_own), middle,
            eight_rows(bias_fc2[l], ada[l, 1], 1.0 + after[2], after[4]), last,
        )

    *halves, chunks[1], hidden = together(*halves, chunks[1], hidden)
    weights[0], sent = whole(sent, halves), send(chunks[1])
    found0 = attn_start(0, hidden)
    attn0, rest0, logs0, own, send_own = attn_mix(
        *found0[3:6], end_col, place_row, weights[0], head_width
    )
    *sent, send_own = together(*sent, send_own)
    halves = send_on(sent)
    branch0, middle0, hidden2 = attn_end(0, own, send_own, state)
    *halves, chunks[2], hidden2 = together(*halves, chunks[2], hidden2)
    weights[1], sent = whole(sent, halves), send(chunks[2])
    joined2, act, slope = fc_start(0, hidden2)
    *sent, act = together(*sent, act)
    halves = send_on(sent)
    *halves, chunks[3], act = together(*halves, chunks[3], act)
    weights[2], sent = whole(sent, halves), send(chunks[3])
    feed, state1, hidden = fc_end(0, act, middle0)
    saved = [(*found0, logs0, attn0, rest0, branch0, middle0, joined2, act, slope, feed, state)]
    *sent, hidden = together(*sent, hidden)
    halves = send_on(sent)
    *halves, chunks[4], hidden = together(*halves, chunks[4], hidden)
    weights[3], sent = whole(sent, halves), send(chunks[4])
    found1 = attn_start(1, hidden)
    attn1, rest1, logs1, own, send_own = attn_mix(
        *found1[3:6], end_col, place_row, weights[3], head_width
    )
    *sent, send_own = together(*sent, send_own)
    halves = send_on(sent)
    branch1, middle1, hidden2 = attn_end(1, own, send_own, state1)
    *halves, hidden2, grad_out = together(*halves, hidden2, grad_out)
    weights[4] = whole(sent, halves)
    grad = own_tokens(grad_out).astype(F32)
    joined2, act, slope, own, send_own = fc_forward(
        hidden2, sibling(hidden2), weights[4], weights[5], bias_fc1[1]
    )
    feed, state2, mixed = mix(
        own, sibling(send_own), middle1, eight_rows(bias_fc2[1], ada[1, 1], ada[1, 2], ada[1, 4]), True
    )
    mixed, grad = together(mixed, grad)
    saved.append((*found1, logs1, attn1, rest1, branch1, middle1, joined2, act, slope, feed, state1))

    top = layer_count - 1
    d_ada = [[None] * 6 for _ in range(layer_count)]
    d_biases = [[None] * 5 for _ in range(layer_count)]
    d_weights = [None] * layer_count
    fold = lambda sums: jnp.sum(sums.reshape(-1, 8, sums.shape[1]), axis=1)
    d_low = (grad * ada[top, 1][None]).astype(BF)
    d_ada[top][1] = jnp.sum(grad * saved[1][-2].astype(F32), axis=0)
    d_biases[top][1] = jnp.sum(d_low.astype(F32), axis=0)
    def fc_turn(l, d_low, d_other=None):
        act, slope, joined2 = saved[l][-4], saved[l][-3], saved[l][-5]
        d_other = sibling(d_low) if d_other is None else d_other
        return fc_back(
            d_low, d_other, weights[3 * l + 2], weights[3 * l + 1], slope, act, joined2, l == 1
        )

    def fc_norm(l, sums_pre, own, got_own, grad):
        d_middle, d_low, sums = mix_back(
            own, got_own, saved[l][10], grad, saved[l][9], eight_rows(1.0 + ada[l, 3], ada[l, 0])
        )
        d_ada[l][3], d_ada[l][5], d_ada[l][0], d_biases[l][0] = fold(sums)
        d_biases[l][3] = fold(sums_pre)[0]
        return d_middle, d_low

    def attn_turn(x, l, d_low, d_other, before=None):
        joined1, q_raw, k_raw, q_low, k_low, v_low, logs, attn, rest = saved[l][:9]
        return attn_back(
            x, d_low, d_other, weights[3 * l], q_low, k_low, v_low, attn, rest, logs, q_raw, k_raw, joined1,
            eight_rows(scales[l]), place_col, end_row, head_width, before,
        )

    def attn_norm(l, sums_one, found, got_own, d_middle):
        sums_qkv, own = found
        sums_qkv = jnp.concatenate((sums_qkv, sums_one), axis=1)
        before = max(l - 1, 0)
        grad, d_low, sums = mix_back(
            own, got_own, saved[l][-1], d_middle, saved[before][-2],
            eight_rows(1.0 + ada[l, 2], ada[before, 1]),
        )
        sums = fold(sums)
        d_ada[l][2], d_ada[l][4] = sums[0], sums[1]
        if l > 0:
            d_ada[l - 1][1], d_biases[l - 1][1] = sums[2], sums[3]
        d_biases[l][2] = sums_qkv[:2]
        d_biases[l][4] = jnp.sum(sums_qkv[2].reshape(heads, head_width), axis=1)
        return grad, d_low

    def given_back(values):
        return trade(turned(values[:rows_dev], y, 1).astype(BF), core != x)

    def halves_out(parts):
        return across(parts[-2], "y"), across(parts[-1], "x")

    def near_out(pair):
        return across(pair[0], "x"), across(pair[1], "y")

    (sums_pre, own, send_own), two, one = fc_turn(1, d_low)
    z_two = over_z(two)
    got_one = halves_out(one)
    d_middle, d_low = fc_norm(1, sums_pre, own, sibling(send_own), grad)
    d_other = sibling(d_low)

    (sums_one, total), last_x = attn_turn(1, 1, d_low, d_other)
    got_a, got_b, total, *last_x = together(*got_one, total, *last_x)
    got_last = halves_out(last_x)
    near_x, near_y, total = together(*near_parts([one[1:3]], got_a, got_b)[0], total)
    near_one = across(near_x, "x"), across(near_y, "y")
    (sums_two, own, send_own), last = attn_turn(0, 1, d_low, d_other, total)
    *got_last, send_own = together(*got_last, send_own)
    grad, d_low = attn_norm(1, sums_one, (sums_two, own), sibling(send_own), d_middle)
    near_a, near_b, d_low = together(*near_one, d_low)
    sum_one = summed(one[0], near_a, near_b, 1, z_size)
    got_a, got_b, sum_one, d_other = together(*got_last, sum_one, sibling(d_low))
    g_one1 = over_z(sum_one)
    near_last = near_out(near_parts([(last_x[0], last[1])], got_a, got_b)[0])
    keep_last = last[0]

    (sums_pre, own, send_own), blocks, far = fc_turn(0, d_low, d_other)
    z_two = turned(turned(z_two.reshape(x_size, y_size, hid_core, low), x, 0), y, 1)
    near_a, near_b, z_two, send_own = together(
        *near_last, z_two.reshape(x_size * y_size, hid_core, low), send_own
    )
    g_two1 = lax.psum_scatter(z_two, ("x", "y"), scatter_dimension=0, tiled=False)
    got = across(far[0], "y"), across(far[1], "x")
    d_middle, d_low = fc_norm(0, sums_pre, own, sibling(send_own), grad)
    sum_last, d_low = together(summed(keep_last, near_a, near_b, 4, z_size), d_low)
    g_attn1 = over_z(sum_last)
    d_other = sibling(d_low)

    (sums_one, total), last_x = attn_turn(1, 0, d_low, d_other)
    *got, total, g_one1, g_two1 = together(*got, total, g_one1, g_two1)
    one, two = near_parts([blocks[4:6], blocks[1:3]], *got)
    *one, total = together(*one, total)
    near_one, near_two = near_out(one), near_out(two)
    (sums_two, own, send_own), last = attn_turn(0, 0, d_low, d_other, total)
    near_a, near_b, send_own = together(*near_one, send_own)
    got_last = halves_out(last_x)
    sum_one, send_own = together(summed(blocks[3], near_a, near_b, 1, z_size), send_own)
    g_one0 = over_z(sum_one)
    grad, d_low = attn_norm(0, sums_one, (sums_two, own), sibling(send_own), d_middle)
    near_a, near_b, grad, g_attn1 = together(*near_two, grad, g_attn1)
    g_two0 = over_z(summed(blocks[0], near_a, near_b, 1, z_size))
    near_x, near_y = near_parts([(last_x[0], last[1])], *got_last)[0]
    near_x, near_y, g_one0 = together(near_x, near_y, g_one0)
    near_last = across(near_x, "x"), across(near_y, "y")

    def by_col(values):
        values = turned(values, y, values.ndim - 1)
        values = values.reshape(values.shape[:-1] + (z_size, x_size, d_col))
        return jnp.moveaxis(values, (-3, -2), (0, 1)).reshape(z_size, x_size, -1)

    def by_hidden(values):
        return jnp.swapaxes(turned(values, x, 0), 0, 1).reshape(z_size, x_size, -1)

    packs = [by_col(jnp.stack([jnp.stack(v) for v in d_ada]))]
    for l in range(layer_count):
        db_proj, db_fc2, db_qkv, db_fc1, d_head = d_biases[l]
        packs.append(by_col(db_proj))
        packs.append(by_col(db_fc2))
        packs.append(by_hidden(jnp.moveaxis(db_qkv.reshape(2, x_size, z_size, head_width), 0, 2)))
        packs.append(by_hidden(db_fc1.reshape(x_size, z_size, hid_core)))
        packs.append(by_hidden(d_head.reshape(x_size, z_size, 1)))
    lens = [p.shape[2] for p in packs]
    pack = jnp.concatenate(packs, axis=2)
    pack = jnp.broadcast_to(pack[None], (n_rows,) + pack.shape)
    got = lax.all_to_all(
        pack.reshape(n_rows * z_size * x_size, -1), ("y", "core", "z", "x"),
        split_axis=0, concat_axis=0, tiled=True,
    ).reshape(y_size, 2, z_size, x_size, -1)
    pos = lens[0]
    d_ada_all = jnp.sum(got[..., :pos], axis=1)
    d_ada_all = jnp.swapaxes(d_ada_all, 1, 2).reshape(seqs, -1).astype(BF)
    out_b_ada = jnp.sum(d_ada_all.astype(F32), axis=0).reshape(layer_count, 6, d_col)
    out_w_ada = dot(silu_own, d_ada_all, TN).reshape(rows_d, layer_count, 6, d_col)
    out_w_ada = jnp.swapaxes(out_w_ada, 0, 1)
    sums = jnp.sum(got[..., pos:], axis=(0, 2, 3))
    outs = [[] for _ in range(5)]
    pos = 0
    for l in range(layer_count):
        for i in range(5):
            count = lens[1 + 5 * l + i]
            outs[i].append(sums[:, pos : pos + count])
            pos += count
    out_b_proj = jnp.stack([v[0] + v[1] for v in outs[0]])
    out_b_fc2 = jnp.stack([v[0] + v[1] for v in outs[1]])
    out_b_qkv = jnp.stack(
        [jnp.swapaxes(v.reshape(2, 2, head_width), 0, 1).reshape(2, d_col) for v in outs[2]]
    )
    out_b_fc1 = jnp.stack([v.reshape(-1) for v in outs[3]])
    out_scale = jnp.stack([v.reshape(-1) for v in outs[4]])

    near_a, near_b, out_w_ada, grad, mixed = together(*near_last, out_w_ada, grad, mixed)
    sum_last, g_two0, grad, mixed = together(summed(last[0], near_a, near_b, 4, z_size), g_two0, grad, mixed)
    g_attn0 = over_z(sum_last)
    mixed, grad_in = given_back(mixed), given_back(grad).astype(F32)

    def both_cores(own):
        kept = jnp.where(core == 0, own[:, :, :rows_d], own[:, :, rows_d:])
        came = sibling(jnp.where(core == 0, own[:, :, rows_d:], own[:, :, :rows_d]))
        return jnp.where(core == 0, kept, came).astype(F32), jnp.where(core == 0, came, kept).astype(F32)

    fc_first, fc_second = both_cores(
        jnp.stack((jnp.concatenate((g_one0, g_two0)), jnp.concatenate((g_one1, g_two1))))
    )
    out_w_fc1 = jnp.swapaxes(jnp.concatenate((fc_first[:, :hid_core], fc_second[:, :hid_core]), axis=1), 1, 2)
    out_w_fc2 = jnp.concatenate((fc_first[:, hid_core:], fc_second[:, hid_core:]), axis=1)
    own, out_w_fc1, out_w_fc2, out_w_ada = together(jnp.stack((g_attn0, g_attn1)), out_w_fc1, out_w_fc2, out_w_ada)
    first, second = both_cores(own)
    wq = jnp.stack((first[:, :three], second[:, :three]), axis=1)
    wq = wq.reshape(layer_count, 2, 3, head_width, rows_d)
    out_w_qkv = jnp.transpose(wq, (0, 4, 2, 1, 3)).reshape(layer_count, rows_d, 3, d_col)
    out_w_proj = jnp.concatenate((first[:, three:], second[:, three:]), axis=1)

    return (
        mixed, grad_in, out_w_ada, out_b_ada, out_w_qkv, out_b_qkv, out_scale,
        out_w_proj, out_b_proj, out_w_fc1, out_b_fc1, out_w_fc2, out_b_fc2,
    )


def solution(mesh):
    rows, cols = mesh.devices.shape
    row, col, body, used = ("row",), ("col",), on_device, mesh
    if rows == 4 and cols == 8:
        used = jax.sharding.Mesh(
            mesh.devices.reshape(rows // 2, 2, cols // 2, 2), ("y", "core", "z", "x")
        )
        row, col, body = ("y", "core"), ("z", "x"), on_pair
    tokens = P(row + col, None)
    out_weights = (
        P(None, row, None, col),
        P(None, None, col),
        P(None, row, None, col),
        P(None, None, col),
        P(None, col),
        P(None, col, row),
        P(None, col),
        P(None, row, col),
        P(None, col),
        P(None, col, row),
        P(None, col),
    )
    return jax.shard_map(
        body,
        mesh=used,
        in_specs=(tokens, P(row, None), P(row, None)) + out_weights + (tokens,),
        out_specs=(tokens, tokens) + out_weights,
        check_vma=False,
    )
```
